32 devices in a mesh: row: 8 (over y, x, core), col: 4 (over z).
Axes of the slice: x: 2, y: 2, z: 4, core: 2. Of those that a mesh axis runs over, the one named last changes fastest.
Arguments:
- node_feats: bfloat16 [16384, 512], P('row', 'col'), may hold values from -6 to 6
- hidden_act: bfloat16 [16384, 512], P('row', 'col'), may hold values from 0 to 2
- grad_out: bfloat16 [16384, 512], P('row', 'col'), may hold values from -6 to 6
- relu_mask: int32 [16384, 512], P('row', 'col'), may hold values 0 or 1
- edge_tiles: bfloat16 [128, 20, 128, 128], P('row'), may hold values from -0.125 to 0.125
- block_cols: int32 [128, 20], P('row'), may hold values from 0 to 127
- weight_one: bfloat16 [512, 512], P('col'), may hold values from -0.25 to 0.25
- weight_two: bfloat16 [512, 512], P('col'), may hold values from -0.25 to 0.25
Outputs:
- input_grad: bfloat16 [16384, 512], P('row', 'col')
- first_grad: float32 [512, 512], P('col')
- second_grad: float32 [512, 512], P('col')
The draws below stay inside these ranges and needn't reach their ends.
All inputs are finite; a program needn't handle non-finite values. No bound on the sum of `relu_mask` on one device may be relied on, other than what follows from the above.
Results may differ from the reference program's by a relative error of at most 0.03.
Values may be sent and summed in bfloat16 or wider, within the bound.
No kernel may reach another device: no remote copies, remote signals or barrier semaphores. Data moves between devices by JAX's collectives and lax.ppermute only.
A program may use at most 128 MiB of HBM per device.

```python
import math
import jax
import jax.numpy as jnp
import numpy as np
from jax import lax

D = 512
BS = 128
K = 20
ROWB_DEV = 16
NB = 128
N = 16384


def plant(values, key, smallest, top_value):
    longest = values.shape.index(max(values.shape))
    spots = []
    for shift in (0, 1):
        where = [jax.random.randint(jax.random.fold_in(key, axis), (), 0, length) for axis, length in enumerate(values.shape)]
        where[longest] = (where[longest] + shift) % values.shape[longest]
        spots.append(tuple(where))
    return values.at[spots[0]].set(smallest).at[spots[1]].set(top_value)


def block_levels(stream_key, extent, split, smallest, top_value):
    factor_of = 1.0
    for axis_at, blocks in split:
        draws = jax.random.uniform(jax.random.fold_in(jax.random.fold_in(stream_key, 6), axis_at), (blocks,), jnp.float32, smallest / len(split), top_value / len(split))
        factor_of = factor_of * jnp.repeat(jnp.exp(draws), extent[axis_at] // blocks).reshape((-1,) + (1,) * (len(extent) - 1 - axis_at))
    return factor_of


def rank_table(count, slope):
    loads = [(1 << 20) // math.isqrt(rank ** slope) + 1 for rank in range(1, count + 1)]
    scale = 1 + sum(loads) // (1 << 30)
    return np.cumsum(np.array([max(1, weight // scale) for weight in loads]))


def ranked_ids(key, dims, amount, skew):
    grid = rank_table(amount, skew)
    pick = jax.random.randint(jax.random.fold_in(key, 1), dims, 0, int(grid[amount - 1]))
    standing = jnp.searchsorted(jnp.asarray(grid, jnp.int32), pick, side="right")
    return jax.random.permutation(jax.random.fold_in(key, 2), amount)[standing].astype(jnp.int32)


def scatter_about(own_key, shape, width, limit, cuts=(), held_as=jnp.bfloat16):
    drawn = jax.random.normal(own_key, shape, jnp.float32) * width
    if len(cuts) > 0:
        drawn = block_levels(own_key, shape, cuts, -0.22, 0.18) * drawn
    return jnp.clip(drawn, min=-limit, max=limit).astype(held_as)


def setup_inputs(seed: int = 0) -> dict:
    seeds = jax.random.split(jax.random.key(seed), 9)
    return {
        "node_feats": scatter_about(seeds[0], (N, D), 1.0, 6.0, ((0, 8), (1, 4))),
        "hidden_act": jnp.clip(2.0 * jax.random.uniform(seeds[1], (N, D), jnp.float32) ** block_levels(seeds[1], (N, D), ((0, 8), (1, 4)), -0.2, 0.2), 0.0, 2.0).astype(jnp.bfloat16),
        "grad_out": scatter_about(seeds[2], (N, D), 1.0, 6.0, ((0, 8), (1, 4))),
        "relu_mask": plant((jax.random.randint(seeds[3], (N, D), 0, 2) < 1).astype(jnp.int32), jax.random.fold_in(seeds[3], 1), 0, 1),
        "edge_tiles": scatter_about(seeds[4], (NB, K, BS, BS), (K * BS) ** -0.5, 0.125, ((0, 8),)),
        "block_cols": plant(ranked_ids(seeds[5], (NB, K), NB, 1), jax.random.fold_in(seeds[5], 3), 0, NB - 1).astype(jnp.int32),
        "weight_one": scatter_about(seeds[6], (D, D), D ** -0.5, 0.25, ((0, 4),)),
        "weight_two": scatter_about(seeds[7], (D, D), D ** -0.5, 0.25, ((0, 4),)),
    }


def aggregate(edge_tiles, block_cols, values):
    table = values.reshape(NB, BS, values.shape[1])

    def one_row(pair):
        tiles_row, cols_row = pair
        picked = table[cols_row.astype(jnp.int32)]
        return jnp.einsum("kij,kjd->id", tiles_row.astype(jnp.float32), picked.astype(jnp.float32))

    summed = lax.map(one_row, (edge_tiles, block_cols))
    return summed.reshape(N, values.shape[1])


def spread(edge_tiles, block_cols, values):
    feat_cols = values.shape[1]
    blocks = values.reshape(NB, BS, feat_cols)

    def one_group(group, carry):
        first_row = (group * ROWB_DEV).astype(jnp.int32)
        tiles_group = lax.dynamic_slice_in_dim(edge_tiles, first_row, ROWB_DEV, 0)
        cols_group = lax.dynamic_slice_in_dim(block_cols, first_row, ROWB_DEV, 0)
        vals_group = lax.dynamic_slice_in_dim(blocks, first_row, ROWB_DEV, 0)
        terms = jnp.einsum("rkij,rid->rkjd", tiles_group.astype(jnp.float32), vals_group.astype(jnp.float32))
        partial_sum = jax.ops.segment_sum(terms.reshape(ROWB_DEV * K, BS, feat_cols), cols_group.reshape(-1), num_segments=NB)
        rounded = lax.optimization_barrier(partial_sum.astype(jnp.bfloat16))
        return carry + rounded.astype(jnp.float32)

    start_sum = jnp.zeros((NB, BS, feat_cols), jnp.float32)
    total = lax.fori_loop(0, NB // ROWB_DEV, one_group, start_sum)
    return total.reshape(N, feat_cols)


def reference(node_feats, hidden_act, grad_out, relu_mask, edge_tiles, block_cols, weight_one, weight_two):
    agg_feats = aggregate(edge_tiles, block_cols, node_feats).astype(jnp.bfloat16)
    agg_hidden = aggregate(edge_tiles, block_cols, hidden_act).astype(jnp.bfloat16)
    second_grad = jnp.dot(agg_hidden.T, grad_out, preferred_element_type=jnp.float32)
    d_hidden_agg = jnp.dot(grad_out, weight_two.T, preferred_element_type=jnp.float32).astype(jnp.bfloat16)
    hidden_grad = spread(edge_tiles, block_cols, d_hidden_agg)
    delta = (hidden_grad * relu_mask.astype(jnp.float32)).astype(jnp.bfloat16)
    first_grad = jnp.dot(agg_feats.T, delta, preferred_element_type=jnp.float32)
    d_feats_agg = jnp.dot(delta, weight_one.T, preferred_element_type=jnp.float32).astype(jnp.bfloat16)
    input_grad = spread(edge_tiles, block_cols, d_feats_agg).astype(jnp.bfloat16)
    return (input_grad, first_grad, second_grad)
```

```python
import functools

import jax
import jax.numpy as jnp
from jax import lax
from jax.experimental import pallas as pl
from jax.experimental.pallas import tpu as pltpu
from jax.sharding import PartitionSpec as P

VMEM_LIMIT = 56 * 1024 * 1024
GROUPS = 2
F32 = jnp.float32
BF16 = jnp.bfloat16


def spread_kernel(groups, flip, cols_ref, me_ref, tiles_ref, vals_ref, *rest):
    outs, acc = rest[:-1], rest[-1]
    step = pl.program_id(0)
    per_row = tiles_ref.shape[1]
    width = tiles_ref.shape[3]

    @pl.when(step == 0)
    def _():
        acc[...] = jnp.zeros_like(acc)

    left = vals_ref[0]
    if flip:
        left = left.astype(F32).T.astype(BF16)
    for k in range(0, per_row, 2):
        pair = jnp.concatenate([tiles_ref[0, k], tiles_ref[0, k + 1]], axis=1)
        both = jnp.dot(left, pair, preferred_element_type=F32)
        for side in range(2):
            target = cols_ref[step, k + side]
            acc[target] += both[:, side * width : (side + 1) * width]

    @pl.when(step == pl.num_programs(0) - 1)
    def _():
        me = me_ref[0]
        halves = outs[0].shape[0]
        size = outs[0].shape[1]
        blocks_dev = groups * size
        for g in range(groups):
            for side in range(2):
                out = outs[2 * g + side]
                for rel in range(halves):
                    owner = jnp.bitwise_xor(me, 2 * rel + side)
                    first = owner * blocks_dev + g * size
                    out[rel] = acc[pl.ds(first, size)].astype(BF16)


def spread(edge_tiles, block_cols, vals, me, rows, flip):
    blocks, per_row, size, _ = edge_tiles.shape
    feat = vals.shape[2] if flip else vals.shape[1]
    per_group = blocks // GROUPS
    out_shape = jax.ShapeDtypeStruct((rows // 2, per_group, feat, size), BF16)
    whole = lambda step, *_: (0, 0, 0, 0)
    return pl.pallas_call(
        functools.partial(spread_kernel, GROUPS, flip),
        out_shape=[out_shape] * (2 * GROUPS),
        grid_spec=pltpu.PrefetchScalarGridSpec(
            num_scalar_prefetch=2,
            grid=(blocks,),
            in_specs=[
                pl.BlockSpec((1, per_row, size, size), lambda step, *_: (step, 0, 0, 0)),
                pl.BlockSpec((1,) + vals.shape[1:], lambda step, *_: (step, 0, 0)),
            ],
            out_specs=[pl.BlockSpec(out_shape.shape, whole)] * (2 * GROUPS),
            scratch_shapes=[pltpu.VMEM((rows * blocks, feat, size), F32)],
        ),
        compiler_params=pltpu.CompilerParams(vmem_limit_bytes=VMEM_LIMIT),
    )(block_cols, me.reshape(1), edge_tiles, vals)


def dense_kernel(cols, final, col_ref, weight_ref, *rest):
    shards, rest = rest[: 2 * cols - 1], rest[2 * cols - 1 :]
    if final:
        side_ref, out_ref, grad_ref = rest
    else:
        side_ref, mask_ref, out_ref, grad_ref = rest
    own, ups, downs = shards[0], shards[1:cols], shards[cols:]
    col = col_ref[0]
    blocks, feat, size = own.shape
    weight = weight_ref[...]
    total = None
    for b in range(blocks):
        parts = [own[b]]
        for s in range(1, cols):
            parts.append(jnp.where(col >= s, ups[s - 1][b], downs[cols - s - 1][b]))
        stacked = jnp.concatenate(parts, axis=0)
        res = jnp.dot(weight, stacked, preferred_element_type=F32)
        if final:
            out_ref[b] = res.T.astype(BF16)
        else:
            out_ref[b] = (res * mask_ref[b].astype(F32)).astype(BF16)
        term = jnp.dot(stacked, side_ref[b], preferred_element_type=F32)
        total = term if total is None else total + term
    for s in range(cols):
        place = lax.rem(col - s + cols, cols)
        grad_ref[place] = total[s * feat : (s + 1) * feat]


def dense(weight, shards, side, mask, col, cols):
    own = shards[0]
    blocks, feat, size = own.shape
    final = mask is None
    out = (blocks, size, feat) if final else (blocks, feat, size)
    grad = (cols, feat, side.shape[2])
    args = [weight, *shards, side] + ([] if final else [mask])
    vmem = pl.BlockSpec(memory_space=pltpu.VMEM)
    return pl.pallas_call(
        functools.partial(dense_kernel, cols, final),
        out_shape=[jax.ShapeDtypeStruct(out, BF16), jax.ShapeDtypeStruct(grad, F32)],
        in_specs=[pl.BlockSpec(memory_space=pltpu.SMEM)] + [vmem] * len(args),
        out_specs=[vmem, vmem],
        compiler_params=pltpu.CompilerParams(vmem_limit_bytes=VMEM_LIMIT),
    )(col.reshape(1), *args)


def swap(value, mask, rows):
    return lax.ppermute(value, "row", [(i, i ^ mask) for i in range(rows)])


def add(a, b):
    return (a.astype(F32) + b.astype(F32)).astype(BF16)


def scatter_chunk(keep, got, masks):
    rows = lax.axis_size("row")
    left = sorted(masks, reverse=True)
    for mask in masks:
        axis = left.index(mask)
        part = lambda v, i: lax.index_in_dim(v, i, axis, keepdims=False)
        sent = swap(add(part(keep, 1), part(got, 1)), mask, rows)
        keep = add(part(keep, 0), part(got, 0))
        got = sent
        left.remove(mask)
    return add(keep, got)


def scatter_group(keep, send):
    rows = lax.axis_size("row")
    got = swap(send, 1, rows)
    bits = rows.bit_length() - 1
    masks = [1 << b for b in range(1, bits)]
    lead = (2,) * len(masks)
    keep = keep.reshape(lead + keep.shape[1:])
    got = got.reshape(lead + got.shape[1:])
    axis = len(lead)
    half = keep.shape[axis] // 2
    done = []
    for i, order in enumerate((masks, masks[::-1])):
        cut = lambda v: lax.slice_in_dim(v, i * half, (i + 1) * half, axis=axis)
        done.append(scatter_chunk(cut(keep), cut(got), order))
    return jnp.concatenate(done, axis=0)


def chain_gather(own, cols):
    ups, downs = [], []
    up, down = own, own
    for s in range(1, cols):
        up = lax.ppermute(up, "col", [(i, i + 1) for i in range(s - 1, cols - 1)])
        down = lax.ppermute(down, "col", [(i, i - 1) for i in range(1, cols - s + 1)])
        ups.append(up)
        downs.append(down)
    return [own, *ups, *downs]


def row_sum(value, rows):
    mask = 1
    while mask < rows:
        value = value.astype(BF16)
        value = value.astype(F32) + swap(value, mask, rows).astype(F32)
        mask *= 2
    return value


def layer(edge_tiles, block_cols, vals, weight, side, mask, me, col, rows, cols, flip):
    pieces = spread(edge_tiles, block_cols, vals, me, rows, flip)
    outs, grads = [], []
    per_group = edge_tiles.shape[0] // GROUPS
    for g in range(GROUPS):
        shard = scatter_group(pieces[2 * g], pieces[2 * g + 1])
        shards = chain_gather(shard, cols)
        cut = slice(g * per_group, (g + 1) * per_group)
        out, grad = dense(weight, shards, side[cut], None if mask is None else mask[cut], col, cols)
        outs.append(out)
        grads.append(grad)
    grad = row_sum(sum(grads), rows)
    feat_all, own = grad.shape[0] * grad.shape[1], grad.shape[2]
    return jnp.concatenate(outs, axis=0), grad.reshape(feat_all, own).T


def ring_order(weight, col, cols):
    out_rows, total = weight.shape
    split = weight.reshape(out_rows, cols, total // cols)
    parts = [lax.dynamic_index_in_dim(split, lax.rem(col - s + cols, cols), 1, keepdims=False) for s in range(cols)]
    return jnp.concatenate(parts, axis=1)


def per_device(
    node_feats, hidden_act, grad_out, relu_mask, edge_tiles, block_cols, weight_one, weight_two
):
    rows, cols = lax.axis_size("row"), lax.axis_size("col")
    me, col = lax.axis_index("row").astype(jnp.int32), lax.axis_index("col").astype(jnp.int32)
    size = edge_tiles.shape[2]
    blocked = lambda v: v.reshape(v.shape[0] // size, size, v.shape[1])
    mask = blocked(relu_mask).astype(BF16).transpose(0, 2, 1)
    weight_two = ring_order(weight_two, col, cols)
    weight_one = ring_order(weight_one, col, cols)
    delta, second_grad = layer(
        edge_tiles, block_cols, blocked(grad_out), weight_two, blocked(hidden_act), mask, me, col, rows, cols, True
    )
    out, first_grad = layer(
        edge_tiles, block_cols, delta, weight_one, blocked(node_feats), None, me, col, rows, cols, False
    )
    return out.reshape(node_feats.shape), first_grad, second_grad


def solution(mesh):
    in_specs = (
        P("row", "col"),
        P("row", "col"),
        P("row", "col"),
        P("row", "col"),
        P("row", None, None, None),
        P("row", None),
        P("col", None),
        P("col", None),
    )
    out_specs = (P("row", "col"), P("col", None), P("col", None))
    return jax.shard_map(
        per_device, mesh=mesh, in_specs=in_specs, out_specs=out_specs, check_vma=False
    )
```

```python
import functools

import jax
import jax.numpy as jnp
from jax import lax
from jax.experimental import pallas as pl
from jax.experimental.pallas import tpu as pltpu
from jax.sharding import PartitionSpec as P

VMEM_LIMIT = 48 * 1024 * 1024
CHUNKS = 2
COPIES = 4
F32 = jnp.float32
BF16 = jnp.bfloat16
VMEM = pl.BlockSpec(memory_space=pltpu.VMEM)
SMEM = pl.BlockSpec(memory_space=pltpu.SMEM)
PARAMS = pltpu.CompilerParams(vmem_limit_bytes=VMEM_LIMIT)


def tile_copy(tiles_ref, held, sems, i):
    per = held.shape[0] // COPIES
    part = pl.ds(i * per, per)
    return pltpu.make_async_copy(tiles_ref.at[part], held.at[part], sems.at[i])


def over_rows(tiles_ref, held, sems, one_row):
    per = held.shape[0] // COPIES

    def piece(i, carry):
        tile_copy(tiles_ref, held, sems, i).wait()
        for j in range(per):
            one_row(i * per + j)
        return carry

    lax.fori_loop(0, COPIES, piece, 0)


def spread_kernel(flip, pieces, cols_ref, at_ref, tiles_ref, *rest):
    vals, rest = rest[:pieces], rest[pieces:]
    outs, (acc, held, left_ref, sems) = rest[: 2 * CHUNKS], rest[2 * CHUNKS :]
    for i in range(COPIES):
        tile_copy(tiles_ref, held, sems, i).start()
    acc[...] = jnp.zeros_like(acc)
    per_row, size = held.shape[1], held.shape[3]
    me, col = at_ref[0], at_ref[1]
    if not flip:
        count = vals[0].shape[0]
        for m in range(pieces):
            left_ref[pl.ds(jnp.bitwise_xor(col, m) * count, count)] = vals[m][...]

    def one_row(r):
        left = vals[0][r].astype(F32).T.astype(BF16) if flip else left_ref[r]
        for k in range(0, per_row, 2):
            pair = jnp.concatenate([held[r, k], held[r, k + 1]], axis=1)
            both = jnp.dot(left, pair, preferred_element_type=F32)
            for side in range(2):
                acc[cols_ref[r, k + side]] += both[:, side * size : (side + 1) * size]

    over_rows(tiles_ref, held, sems, one_row)
    halves, count = outs[0].shape[:2]
    for g in range(CHUNKS):
        for side in range(2):
            for rel in range(halves):
                owner = jnp.bitwise_xor(me, 2 * rel + side)
                first = (owner * CHUNKS + g) * count
                outs[2 * g + side][rel] = acc[pl.ds(first, count)].astype(BF16)


def spread(edge_tiles, block_cols, vals, at, rows, flip):
    blocks, _, size, _ = edge_tiles.shape
    feat = vals[0].shape[2] if flip else vals[0].shape[1]
    out = jax.ShapeDtypeStruct((rows // 2, blocks // CHUNKS, feat, size), BF16)
    return pl.pallas_call(
        functools.partial(spread_kernel, flip, len(vals)),
        out_shape=[out] * (2 * CHUNKS),
        in_specs=[SMEM, SMEM, pl.BlockSpec(memory_space=pl.ANY)] + [VMEM] * len(vals),
        out_specs=[VMEM] * (2 * CHUNKS),
        scratch_shapes=[
            pltpu.VMEM((rows * blocks, feat, size), F32),
            pltpu.VMEM(edge_tiles.shape, BF16),
            pltpu.VMEM((blocks, feat, size), BF16),
            pltpu.SemaphoreType.DMA((COPIES,)),
        ],
        compiler_params=PARAMS,
        cost_estimate=pl.CostEstimate(flops=2 * edge_tiles.size * feat, bytes_accessed=40_000_000, transcendentals=0),
        name="spread",
    )(block_cols, at, edge_tiles, *vals)


def aggregate_kernel(cols_ref, tiles_ref, table_ref, out_ref, held, sems):
    for i in range(COPIES):
        tile_copy(tiles_ref, held, sems, i).start()
    per_row = held.shape[1]

    def one_row(r):
        total = None
        for k in range(0, per_row, 2):
            pair = jnp.concatenate([held[r, k], held[r, k + 1]], axis=1)
            picked = jnp.concatenate([table_ref[cols_ref[r, k]], table_ref[cols_ref[r, k + 1]]], axis=0)
            term = jnp.dot(pair, picked, preferred_element_type=F32)
            total = term if total is None else total + term
        out_ref[r] = total.astype(BF16)

    over_rows(tiles_ref, held, sems, one_row)


def aggregate(edge_tiles, block_cols, table):
    blocks, _, size, _ = edge_tiles.shape
    feat = table.shape[2]
    return pl.pallas_call(
        aggregate_kernel,
        out_shape=jax.ShapeDtypeStruct((blocks, size, feat), BF16),
        in_specs=[SMEM, pl.BlockSpec(memory_space=pl.ANY), VMEM],
        out_specs=VMEM,
        scratch_shapes=[pltpu.VMEM(edge_tiles.shape, BF16), pltpu.SemaphoreType.DMA((COPIES,))],
        compiler_params=PARAMS,
        cost_estimate=pl.CostEstimate(flops=2 * edge_tiles.size * feat, bytes_accessed=30_000_000, transcendentals=0),
        name="aggregate",
    )(block_cols, edge_tiles, table)


def finish_kernel(pieces, at_ref, *rest):
    parts, outs = rest[: 2 * CHUNKS], rest[2 * CHUNKS : 2 * CHUNKS + max(pieces, 1)]
    total = [parts[2 * g][...].astype(F32) + parts[2 * g + 1][...].astype(F32) for g in range(CHUNKS)]
    count = parts[0].shape[0]
    if pieces == 0:
        for g in range(CHUNKS):
            for b in range(count):
                outs[0][g * count + b] = total[g][b].T.astype(BF16)
        return
    held = rest[-1]
    for g in range(CHUNKS):
        held[g * count : (g + 1) * count] = total[g].astype(BF16)
    per = outs[0].shape[0]
    for m in range(pieces):
        outs[m][...] = held[pl.ds(jnp.bitwise_xor(at_ref[1], m) * per, per)]


def finish(parts, at, pieces):
    count, feat, size = parts[0].shape
    blocks = count * CHUNKS
    if pieces == 0:
        outs, scratch = [jax.ShapeDtypeStruct((blocks, size, feat), BF16)], []
    else:
        outs = [jax.ShapeDtypeStruct((blocks // pieces, feat, size), BF16)] * pieces
        scratch = [pltpu.VMEM((blocks, feat, size), BF16)]
    return pl.pallas_call(
        functools.partial(finish_kernel, pieces),
        out_shape=outs,
        in_specs=[SMEM] + [VMEM] * len(parts),
        out_specs=[VMEM] * len(outs),
        scratch_shapes=scratch,
        compiler_params=PARAMS,
        name="finish",
    )(at, *parts)


def dense_kernel(cols, at_ref, weights_ref, *rest):
    sums, rest = rest[:cols], rest[cols:]
    sides, rest = rest[:cols], rest[cols:]
    outs, rest = rest[:cols], rest[cols:]
    delta_ref, rest = rest[0], rest[1:]
    grads, (held, mask) = rest[:cols], rest[cols:]
    col = at_ref[1]
    count, feat, size = sums[0].shape
    width = cols * feat
    for m in range(cols):
        place = jnp.bitwise_xor(col, m)
        for b in range(count):
            held[place, b] = sums[m][b]
            mask[place, b] = sides[m][b, size:].astype(F32).T
    outer = [weights_ref[q, 0] for q in range(cols)]
    inner = [weights_ref[q, 1] for q in range(cols)]
    for b in range(count):
        stacked = jnp.concatenate([held[q, b] for q in range(cols)], axis=0)
        for q in range(cols):
            grad = jnp.dot(outer[q], stacked, preferred_element_type=F32)
            delta_ref[q, b] = (grad * mask[q, b]).astype(BF16)
        delta = jnp.concatenate([delta_ref[q, b] for q in range(cols)], axis=0)
        for q in range(cols):
            held[q, b] = jnp.dot(inner[q], delta, preferred_element_type=F32).astype(BF16)
        for m in range(cols):
            term = jnp.dot(stacked, sides[m][b, :size], preferred_element_type=F32)
            if b == 0:
                grads[m][...] = term
            else:
                grads[m][...] += term
    for m in range(cols):
        outs[m][...] = held[jnp.bitwise_xor(col, m)]


def dense(weights, sums, sides, at):
    cols = len(sums)
    count, feat, size = sums[0].shape
    out = jax.ShapeDtypeStruct((count, feat, size), BF16)
    delta = jax.ShapeDtypeStruct((cols, count, feat, size), BF16)
    grad = jax.ShapeDtypeStruct((cols * feat, feat), F32)
    res = pl.pallas_call(
        functools.partial(dense_kernel, cols),
        out_shape=[out] * cols + [delta] + [grad] * cols,
        in_specs=[SMEM] + [VMEM] * (1 + 2 * cols),
        out_specs=[VMEM] * (2 * cols + 1),
        scratch_shapes=[pltpu.VMEM((cols, count, feat, size), BF16), pltpu.VMEM((cols, count, feat, size), F32)],
        compiler_params=PARAMS,
        name="dense",
    )(at, weights, *sums, *sides)
    return res[:cols], res[cols], res[cols + 1 :]


def weight_terms_kernel(cols, delta_ref, *rest):
    sides, grads = rest[:cols], rest[cols:]
    count = delta_ref.shape[1]
    for b in range(count):
        delta = jnp.concatenate([delta_ref[q, b] for q in range(cols)], axis=0)
        for m in range(cols):
            term = jnp.dot(delta, sides[m][b], preferred_element_type=F32)
            if b == 0:
                grads[m][...] = term
            else:
                grads[m][...] += term


def weight_terms(delta, sides):
    cols, _, feat, _ = delta.shape
    return pl.pallas_call(
        functools.partial(weight_terms_kernel, cols),
        out_shape=[jax.ShapeDtypeStruct((cols * feat, feat), F32)] * cols,
        in_specs=[VMEM] * (1 + cols),
        out_specs=[VMEM] * cols,
        compiler_params=PARAMS,
        name="weight_terms",
    )(delta, *sides)


def swap(value, mask, axis):
    return lax.ppermute(value, axis, [(i, i ^ mask) for i in range(lax.axis_size(axis))])


def swap_all(pieces, axis):
    return [pieces[0]] + [swap(pieces[m], m, axis) for m in range(1, len(pieces))]


def add(a, b):
    return (a.astype(F32) + b.astype(F32)).astype(BF16)


def scatter_chunk(keep, got, masks):
    left = sorted(masks, reverse=True)
    for mask in masks:
        axis = left.index(mask)
        part = lambda v, i: lax.index_in_dim(v, i, axis, keepdims=False)
        sent = swap(add(part(keep, 1), part(got, 1)), mask, "row")
        keep = add(part(keep, 0), part(got, 0))
        got = sent
        left.remove(mask)
    return [keep, got]


def scatter(pieces, rows):
    masks = [1 << b for b in range(1, rows.bit_length() - 1)]
    lead = (2,) * len(masks)
    done = []
    for g in range(CHUNKS):
        keep, got = pieces[2 * g], swap(pieces[2 * g + 1], 1, "row")
        order = masks if g % 2 == 0 else masks[::-1]
        done += scatter_chunk(keep.reshape(lead + keep.shape[1:]), got.reshape(lead + got.shape[1:]), order)
    return done


def reduced(terms):
    got = swap_all([terms[0]] + [t.astype(BF16) for t in terms[1:]], "col")
    value = sum(g.astype(F32) for g in got)
    mask = 1
    while mask < lax.axis_size("row"):
        value = value.astype(BF16)
        value = value.astype(F32) + swap(value, mask, "row").astype(F32)
        mask *= 2
    return value.T


def per_device(
    node_feats, hidden_act, grad_out, relu_mask, edge_tiles, block_cols, weight_one, weight_two
):
    rows, cols = lax.axis_size("row"), lax.axis_size("col")
    col = lax.axis_index("col").astype(jnp.int32)
    at = jnp.stack([lax.axis_index("row").astype(jnp.int32), col])
    blocks, _, size, _ = edge_tiles.shape
    blocked = lambda v: v.reshape(v.shape[0] // size, size, v.shape[1])

    def by_distance(v):
        per = blocks // cols
        return [lax.dynamic_slice_in_dim(v, (col ^ m) * per, per, 0) for m in range(cols)]

    weights = lax.all_gather(jnp.stack([weight_two, weight_one]), "col", axis=0)
    table = blocked(lax.all_gather(node_feats, "row", axis=0, tiled=True))

    pieces = spread(edge_tiles, block_cols, [blocked(grad_out)], at, rows, True)
    both = jnp.concatenate([blocked(hidden_act), blocked(relu_mask).astype(BF16)], axis=1)
    pieces, both = lax.optimization_barrier((pieces, both))
    sides = swap_all(by_distance(both), "col")
    sums = finish(scatter(pieces, rows), at, cols)
    sums = swap_all(sums, "col")
    spread_in, delta, second_terms = dense(weights, sums, sides, at)
    back = swap_all(spread_in, "col")
    agg_feats = by_distance(aggregate(edge_tiles, block_cols, table))
    first_terms = weight_terms(delta, swap_all(agg_feats, "col"))
    pieces = spread(edge_tiles, block_cols, back, at, rows, False)
    (out,) = finish(scatter(pieces, rows), at, 0)
    return out.reshape(node_feats.shape), reduced(first_terms), reduced(second_terms)


def solution(mesh):
    in_specs = (
        P("row", "col"),
        P("row", "col"),
        P("row", "col"),
        P("row", "col"),
        P("row", None, None, None),
        P("row", None),
        P("col", None),
        P("col", None),
    )
    out_specs = (P("row", "col"), P("col", None), P("col", None))
    return jax.shard_map(
        per_device, mesh=mesh, in_specs=in_specs, out_specs=out_specs, check_vma=False
    )
```

```python
import functools

import jax
import jax.numpy as jnp
from jax import lax
from jax.experimental import pallas as pl
from jax.experimental.pallas import tpu as pltpu
from jax.sharding import PartitionSpec as P

VMEM_LIMIT = 48 * 1024 * 1024
CHUNKS = 2
COPIES = 4
F32 = jnp.float32
BF16 = jnp.bfloat16
VMEM = pl.BlockSpec(memory_space=pltpu.VMEM)
SMEM = pl.BlockSpec(memory_space=pltpu.SMEM)
PARAMS = pltpu.CompilerParams(vmem_limit_bytes=VMEM_LIMIT)


def tile_copy(tiles_ref, held, sems, i):
    per = held.shape[0] // COPIES
    part = pl.ds(i * per, per)
    return pltpu.make_async_copy(tiles_ref.at[part], held.at[part], sems.at[i])


def over_rows(tiles_ref, held, sems, one_row):
    per = held.shape[0] // COPIES

    def piece(i, carry):
        tile_copy(tiles_ref, held, sems, i).wait()
        for j in range(per):
            one_row(i * per + j)
        return carry

    lax.fori_loop(0, COPIES, piece, 0)


def spread_kernel(flip, pieces, cols_ref, at_ref, tiles_ref, *rest):
    vals, rest = rest[:pieces], rest[pieces:]
    if flip:
        (hidden_ref, mask_ref, outer_ref, inner_ref), rest = rest[:4], rest[4:]
    outs, rest = rest[: 2 * CHUNKS], rest[2 * CHUNKS :]
    if flip:
        weights_ref, sides, rest = rest[0], rest[1:-4], rest[-4:]
    acc, held, left_ref, sems = rest
    for i in range(COPIES):
        tile_copy(tiles_ref, held, sems, i).start()
    acc[...] = jnp.zeros_like(acc)
    per_row, size = held.shape[1], held.shape[3]
    me, col = at_ref[0], at_ref[1]
    if flip:
        weights_ref[0] = outer_ref[...]
        weights_ref[1] = inner_ref[...]
        for m in range(len(sides)):
            count = sides[m].shape[0]
            part = pl.ds(jnp.bitwise_xor(col, m) * count, count)
            sides[m][:, :size] = hidden_ref[part]
            sides[m][:, size:] = mask_ref[part].astype(F32).astype(BF16)
    else:
        count = vals[0].shape[0]
        for m in range(pieces):
            left_ref[pl.ds(jnp.bitwise_xor(col, m) * count, count)] = vals[m][...]

    def one_row(r):
        left = vals[0][r].astype(F32).T.astype(BF16) if flip else left_ref[r]
        for k in range(0, per_row, 2):
            pair = jnp.concatenate([held[r, k], held[r, k + 1]], axis=1)
            both = jnp.dot(left, pair, preferred_element_type=F32)
            for side in range(2):
                acc[cols_ref[r, k + side]] += both[:, side * size : (side + 1) * size]

    over_rows(tiles_ref, held, sems, one_row)
    halves, count = outs[0].shape[:2]
    for g in range(CHUNKS):
        for side in range(2):
            for rel in range(halves):
                owner = jnp.bitwise_xor(me, 2 * rel + side)
                first = (owner * CHUNKS + g) * count
                outs[2 * g + side][rel] = acc[pl.ds(first, count)].astype(BF16)


def spread(edge_tiles, block_cols, vals, at, rows, cols, prepare=()):
    blocks, _, size, _ = edge_tiles.shape
    flip = len(prepare) > 0
    feat = vals[0].shape[2] if flip else vals[0].shape[1]
    out = jax.ShapeDtypeStruct((rows // 2, blocks // CHUNKS, feat, size), BF16)
    outs = [out] * (2 * CHUNKS)
    if flip:
        outs.append(jax.ShapeDtypeStruct((2,) + prepare[2].shape, BF16))
        outs += [jax.ShapeDtypeStruct((blocks // cols, 2 * size, feat), BF16)] * cols
    return pl.pallas_call(
        functools.partial(spread_kernel, flip, len(vals)),
        out_shape=outs,
        in_specs=[SMEM, SMEM, pl.BlockSpec(memory_space=pl.ANY)] + [VMEM] * (len(vals) + len(prepare)),
        out_specs=[VMEM] * len(outs),
        scratch_shapes=[
            pltpu.VMEM((rows * blocks, feat, size), F32),
            pltpu.VMEM(edge_tiles.shape, BF16),
            pltpu.VMEM((blocks, feat, size), BF16),
            pltpu.SemaphoreType.DMA((COPIES,)),
        ],
        compiler_params=PARAMS,
        cost_estimate=pl.CostEstimate(flops=2 * edge_tiles.size * feat, bytes_accessed=40_000_000, transcendentals=0),
        name="spread",
    )(block_cols, at, edge_tiles, *vals, *prepare)


def aggregate_kernel(cols_ref, tiles_ref, table_ref, out_ref, held, sems):
    for i in range(COPIES):
        tile_copy(tiles_ref, held, sems, i).start()
    per_row = held.shape[1]

    def one_row(r):
        total = None
        for k in range(0, per_row, 2):
            pair = jnp.concatenate([held[r, k], held[r, k + 1]], axis=1)
            picked = jnp.concatenate([table_ref[cols_ref[r, k]], table_ref[cols_ref[r, k + 1]]], axis=0)
            term = jnp.dot(pair, picked, preferred_element_type=F32)
            total = term if total is None else total + term
        out_ref[r] = total.astype(BF16)

    over_rows(tiles_ref, held, sems, one_row)


def aggregate(edge_tiles, block_cols, table):
    blocks, _, size, _ = edge_tiles.shape
    feat = table.shape[2]
    return pl.pallas_call(
        aggregate_kernel,
        out_shape=jax.ShapeDtypeStruct((blocks, size, feat), BF16),
        in_specs=[SMEM, pl.BlockSpec(memory_space=pl.ANY), VMEM],
        out_specs=VMEM,
        scratch_shapes=[pltpu.VMEM(edge_tiles.shape, BF16), pltpu.SemaphoreType.DMA((COPIES,))],
        compiler_params=PARAMS,
        cost_estimate=pl.CostEstimate(flops=2 * edge_tiles.size * feat, bytes_accessed=30_000_000, transcendentals=0),
        name="aggregate",
    )(block_cols, edge_tiles, table)


def finish_kernel(pieces, at_ref, *rest):
    parts, outs = rest[: 2 * CHUNKS], rest[2 * CHUNKS : 2 * CHUNKS + max(pieces, 1)]
    total = [parts[2 * g][...].astype(F32) + parts[2 * g + 1][...].astype(F32) for g in range(CHUNKS)]
    count = parts[0].shape[0]
    if pieces == 0:
        for g in range(CHUNKS):
            for b in range(count):
                outs[0][g * count + b] = total[g][b].T.astype(BF16)
        return
    held = rest[-1]
    for g in range(CHUNKS):
        held[g * count : (g + 1) * count] = total[g].astype(BF16)
    per = outs[0].shape[0]
    for m in range(pieces):
        outs[m][...] = held[pl.ds(jnp.bitwise_xor(at_ref[1], m) * per, per)]


def finish(parts, at, pieces):
    count, feat, size = parts[0].shape
    blocks = count * CHUNKS
    if pieces == 0:
        outs, scratch = [jax.ShapeDtypeStruct((blocks, size, feat), BF16)], []
    else:
        outs = [jax.ShapeDtypeStruct((blocks // pieces, feat, size), BF16)] * pieces
        scratch = [pltpu.VMEM((blocks, feat, size), BF16)]
    return pl.pallas_call(
        functools.partial(finish_kernel, pieces),
        out_shape=outs,
        in_specs=[SMEM] + [VMEM] * len(parts),
        out_specs=[VMEM] * len(outs),
        scratch_shapes=scratch,
        compiler_params=PARAMS,
        name="finish",
    )(at, *parts)


def dense_kernel(cols, at_ref, weights_ref, *rest):
    sums, rest = rest[:cols], rest[cols:]
    sides, rest = rest[:cols], rest[cols:]
    outs, (sum_ref, delta_ref, held, mask) = rest[:cols], rest[cols:]
    col = at_ref[1]
    count, feat, size = sums[0].shape
    for m in range(cols):
        place = jnp.bitwise_xor(col, m)
        for b in range(count):
            sum_ref[place, :, b * size : (b + 1) * size] = sums[m][b]
            mask[place, :, b * size : (b + 1) * size] = sides[m][b, size:].astype(F32).T
    stacked = jnp.concatenate([sum_ref[q] for q in range(cols)], axis=0)
    for q in range(cols):
        grad = jnp.dot(weights_ref[q, 0], stacked, preferred_element_type=F32)
        delta_ref[q] = (grad * mask[q]).astype(BF16)
    delta = jnp.concatenate([delta_ref[q] for q in range(cols)], axis=0)
    for q in range(cols):
        res = jnp.dot(weights_ref[q, 1], delta, preferred_element_type=F32).astype(BF16)
        for b in range(count):
            held[q, b] = res[:, b * size : (b + 1) * size]
    for m in range(cols):
        outs[m][...] = held[jnp.bitwise_xor(col, m)]


def dense(weights, sums, sides, at):
    cols = len(sums)
    count, feat, size = sums[0].shape
    out = jax.ShapeDtypeStruct((count, feat, size), BF16)
    flat = jax.ShapeDtypeStruct((cols, feat, count * size), BF16)
    res = pl.pallas_call(
        functools.partial(dense_kernel, cols),
        out_shape=[out] * cols + [flat] * 2,
        in_specs=[SMEM] + [VMEM] * (1 + 2 * cols),
        out_specs=[VMEM] * (cols + 2),
        scratch_shapes=[pltpu.VMEM((cols, count, feat, size), BF16), pltpu.VMEM((cols, feat, count * size), F32)],
        compiler_params=PARAMS,
        name="dense",
    )(at, weights, *sums, *sides)
    return res[:cols], res[cols], res[cols + 1]


def weight_terms_kernel(cols, at_ref, sum_ref, delta_ref, *rest):
    sides, rest = rest[:cols], rest[cols:]
    aggs, (keep_ref, send_ref) = rest[:cols], rest[cols:]
    even = jnp.bitwise_and(at_ref[0], 1) == 0
    count, size, feat = aggs[0].shape
    sums = jnp.concatenate([sum_ref[q] for q in range(cols)], axis=0)
    delta = jnp.concatenate([delta_ref[q] for q in range(cols)], axis=0)
    for m in range(cols):
        hidden = jnp.concatenate([sides[m][b, :size] for b in range(count)], axis=0)
        agg = jnp.concatenate([aggs[m][b] for b in range(count)], axis=0)
        second = jnp.dot(sums, hidden, preferred_element_type=F32)
        first = jnp.dot(delta, agg, preferred_element_type=F32)
        keep_ref[m] = jnp.where(even, second, first).T
        send_ref[m] = jnp.where(even, first, second).T.astype(BF16)


def weight_terms(sums, delta, sides, aggs, at):
    cols, feat, _ = delta.shape
    shape = (cols, feat, cols * feat)
    return pl.pallas_call(
        functools.partial(weight_terms_kernel, cols),
        out_shape=[jax.ShapeDtypeStruct(shape, F32), jax.ShapeDtypeStruct(shape, BF16)],
        in_specs=[SMEM] + [VMEM] * (2 + 2 * cols),
        out_specs=[VMEM] * 2,
        compiler_params=PARAMS,
        name="weight_terms",
    )(at, sums, delta, *sides, *aggs)


def swap(value, mask, axis):
    return lax.ppermute(value, axis, [(i, i ^ mask) for i in range(lax.axis_size(axis))])


def swap_all(pieces, axis):
    return [pieces[0]] + [swap(pieces[m], m, axis) for m in range(1, len(pieces))]


def add(a, b):
    return (a.astype(F32) + b.astype(F32)).astype(BF16)


def scatter_chunk(keep, got, masks):
    left = sorted(masks, reverse=True)
    for mask in masks:
        axis = left.index(mask)
        part = lambda v, i: lax.index_in_dim(v, i, axis, keepdims=False)
        sent = swap(add(part(keep, 1), part(got, 1)), mask, "row")
        keep = add(part(keep, 0), part(got, 0))
        got = sent
        left.remove(mask)
    return [keep, got]


def scatter(pieces, rows):
    masks = [1 << b for b in range(1, rows.bit_length() - 1)]
    lead = (2,) * len(masks)
    done = []
    for g in range(CHUNKS):
        keep, got = pieces[2 * g], swap(pieces[2 * g + 1], 1, "row")
        order = masks if g % 2 == 0 else masks[::-1]
        done += scatter_chunk(keep.reshape(lead + keep.shape[1:]), got.reshape(lead + got.shape[1:]), order)
    return done


def reduced(keep, send, me):
    terms = keep + swap(send, 1, "row").astype(F32)
    cols = terms.shape[0]
    got = swap_all([terms[0]] + [terms[m].astype(BF16) for m in range(1, cols)], "col")
    value = sum(g.astype(F32) for g in got)
    mask = 2
    while mask < lax.axis_size("row"):
        value = value.astype(BF16)
        value = value.astype(F32) + swap(value, mask, "row").astype(F32)
        mask *= 2
    other = swap(value, 1, "row")
    even = me % 2 == 0
    return jnp.where(even, other, value), jnp.where(even, value, other)


def per_device(
    node_feats, hidden_act, grad_out, relu_mask, edge_tiles, block_cols, weight_one, weight_two
):
    rows, cols = lax.axis_size("row"), lax.axis_size("col")
    me, col = lax.axis_index("row").astype(jnp.int32), lax.axis_index("col").astype(jnp.int32)
    at = jnp.stack([me, col])
    blocks, _, size, _ = edge_tiles.shape
    blocked = lambda v: v.reshape(v.shape[0] // size, size, v.shape[1])

    def by_distance(v):
        per = blocks // cols
        return [lax.dynamic_slice_in_dim(v, (col ^ m) * per, per, 0) for m in range(cols)]

    table = blocked(lax.all_gather(node_feats, "row", axis=0, tiled=True))
    prepare = [blocked(hidden_act), blocked(relu_mask), weight_two, weight_one]
    pieces = spread(edge_tiles, block_cols, [blocked(grad_out)], at, rows, cols, prepare)
    pieces, weights, sides = pieces[: 2 * CHUNKS], pieces[2 * CHUNKS], pieces[2 * CHUNKS + 1 :]
    weights = lax.all_gather(weights, "col", axis=0)
    sides = swap_all(sides, "col")
    sums = finish(scatter(pieces, rows), at, cols)
    sums, sides = lax.optimization_barrier((sums, sides))
    sums = swap_all(sums, "col")
    agg_feats = aggregate(edge_tiles, block_cols, table)
    sums, agg_feats = lax.optimization_barrier((sums, agg_feats))
    spread_in, sums, delta = dense(weights, sums, sides, at)
    agg_feats = swap_all(by_distance(agg_feats), "col")
    spread_in, agg_feats = lax.optimization_barrier((spread_in, agg_feats))
    back = swap_all(spread_in, "col")
    terms = weight_terms(sums, delta, sides, agg_feats, at)
    back, terms = lax.optimization_barrier((back, terms))
    pieces = spread(edge_tiles, block_cols, back, at, rows, cols)
    (out,) = finish(scatter(pieces, rows), at, 0)
    first_grad, second_grad = reduced(*terms, me)
    return out.reshape(node_feats.shape), first_grad, second_grad


def solution(mesh):
    in_specs = (
        P("row", "col"),
        P("row", "col"),
        P("row", "col"),
        P("row", "col"),
        P("row", None, None, None),
        P("row", None),
        P("col", None),
        P("col", None),
    )
    out_specs = (P("row", "col"), P("col", None), P("col", None))
    return jax.shard_map(
        per_device, mesh=mesh, in_specs=in_specs, out_specs=out_specs, check_vma=False
    )
```

```python
import functools

import jax
import jax.numpy as jnp
from jax import lax
from jax.experimental import pallas as pl
from jax.experimental.pallas import tpu as pltpu
from jax.sharding import PartitionSpec as P

VMEM_LIMIT = 48 * 1024 * 1024
CHUNKS = 2
COPIES = 4
F32 = jnp.float32
BF16 = jnp.bfloat16
VMEM = pl.BlockSpec(memory_space=pltpu.VMEM)
SMEM = pl.BlockSpec(memory_space=pltpu.SMEM)
PARAMS = pltpu.CompilerParams(vmem_limit_bytes=VMEM_LIMIT)


def tile_copy(tiles_ref, held, sems, i):
    per = held.shape[0] // COPIES
    part = pl.ds(i * per, per)
    return pltpu.make_async_copy(tiles_ref.at[part], held.at[part], sems.at[i])


def over_rows(tiles_ref, held, sems, one_row):
    per = held.shape[0] // COPIES

    def piece(i, carry):
        tile_copy(tiles_ref, held, sems, i).wait()
        for j in range(per):
            one_row(i * per + j)
        return carry

    lax.fori_loop(0, COPIES, piece, 0)


def spread_kernel(first, pieces, cols_ref, at_ref, tiles_ref, *rest):
    vals, rest = rest[:pieces], rest[pieces:]
    if first:
        (hidden_ref, mask_ref), rest = rest[:2], rest[2:]
    outs, rest = rest[: 2 * CHUNKS], rest[2 * CHUNKS :]
    if first:
        mask_out, sides, rest = rest[0], rest[1:-6], rest[-6:]
        acc, held, sems, left_ref, mask_held, sides_held = rest
        loads = [(vals[0], left_ref), (hidden_ref, sides_held), (mask_ref, mask_held)]
        loads = [pltpu.make_async_copy(src, dst, sems.at[COPIES + i]) for i, (src, dst) in enumerate(loads)]
        loads[0].start()
    else:
        acc, held, sems, left_ref = rest
    for i in range(COPIES):
        tile_copy(tiles_ref, held, sems, i).start()
    if first:
        loads[1].start()
        loads[2].start()
    acc[...] = jnp.zeros_like(acc)
    per_row, size = held.shape[1], held.shape[3]
    me, col = at_ref[0], at_ref[1]
    if first:
        loads[0].wait()
    else:
        for m in range(pieces):
            count = vals[m].shape[0]
            left_ref[pl.ds(jnp.bitwise_xor(col, m) * count, count)] = vals[m][...]

    def one_row(r):
        left = left_ref[r].astype(F32).T.astype(BF16) if first else left_ref[r]
        for k in range(0, per_row, 2):
            pair = jnp.concatenate([held[r, k], held[r, k + 1]], axis=1)
            both = jnp.dot(left, pair, preferred_element_type=F32)
            for side in range(2):
                acc[cols_ref[r, k + side]] += both[:, side * size : (side + 1) * size]

    over_rows(tiles_ref, held, sems, one_row)
    halves, count = outs[0].shape[:2]
    for g in range(CHUNKS):
        for side in range(2):
            for rel in range(halves):
                owner = jnp.bitwise_xor(me, 2 * rel + side)
                start = (owner * CHUNKS + g) * count
                outs[2 * g + side][rel] = acc[pl.ds(start, count)].astype(BF16)
    if first:
        loads[1].wait()
        for m in range(len(sides)):
            per = sides[m].shape[0]
            sides[m][...] = sides_held[pl.ds(jnp.bitwise_xor(col, m) * per, per)]
        loads[2].wait()
        for b in range(mask_held.shape[0]):
            mask_out[b] = mask_held[b].astype(F32).T.astype(BF16)


def spread(edge_tiles, block_cols, vals, at, rows, cols, prepare=()):
    blocks, _, size, _ = edge_tiles.shape
    first = len(prepare) > 0
    feat = vals[0].shape[2] if first else vals[0].shape[1]
    out = jax.ShapeDtypeStruct((rows // 2, blocks // CHUNKS, feat, size), BF16)
    outs = [out] * (2 * CHUNKS)
    scratch = [
        pltpu.VMEM((rows * blocks, feat, size), F32),
        pltpu.VMEM(edge_tiles.shape, BF16),
        pltpu.SemaphoreType.DMA((COPIES + 3,)),
    ]
    if first:
        outs.append(jax.ShapeDtypeStruct((blocks, feat, size), BF16))
        outs += [jax.ShapeDtypeStruct((blocks // cols, size, feat), BF16)] * cols
        scratch += [pltpu.VMEM(v.shape, v.dtype) for v in (vals[0], prepare[1], prepare[0])]
    else:
        scratch.append(pltpu.VMEM((blocks, feat, size), BF16))
    place = pl.BlockSpec(memory_space=pl.ANY) if first else VMEM
    return pl.pallas_call(
        functools.partial(spread_kernel, first, len(vals)),
        out_shape=outs,
        in_specs=[SMEM, SMEM, pl.BlockSpec(memory_space=pl.ANY)] + [place] * (len(vals) + len(prepare)),
        out_specs=[VMEM] * len(outs),
        scratch_shapes=scratch,
        compiler_params=PARAMS,
        cost_estimate=pl.CostEstimate(flops=2 * edge_tiles.size * feat, bytes_accessed=40_000_000, transcendentals=0),
        name="spread",
    )(block_cols, at, edge_tiles, *vals, *prepare)


def aggregate_kernel(cols_ref, at_ref, tiles_ref, *rest):
    parts, (out_ref, held, table, sems) = rest[:-4], rest[-4:]
    blocks, per_row = held.shape[:2]
    loads = []
    for rel, part in enumerate(parts):
        place = table.at[pl.ds(jnp.bitwise_xor(at_ref[0], rel) * blocks, blocks)]
        loads.append(pltpu.make_async_copy(part, place, sems.at[COPIES + rel]))
    for load in loads:
        load.start()
    for i in range(COPIES):
        tile_copy(tiles_ref, held, sems, i).start()
    for load in loads:
        load.wait()

    def one_row(r):
        total = None
        for k in range(0, per_row, 2):
            pair = jnp.concatenate([held[r, k], held[r, k + 1]], axis=1)
            picked = jnp.concatenate([table[cols_ref[r, k]], table[cols_ref[r, k + 1]]], axis=0)
            term = jnp.dot(pair, picked, preferred_element_type=F32)
            total = term if total is None else total + term
        out_ref[r] = total.astype(BF16)

    over_rows(tiles_ref, held, sems, one_row)


def aggregate(edge_tiles, block_cols, parts, at):
    blocks, _, size, _ = edge_tiles.shape
    feat = parts[0].shape[2]
    anywhere = pl.BlockSpec(memory_space=pl.ANY)
    return pl.pallas_call(
        aggregate_kernel,
        out_shape=jax.ShapeDtypeStruct((blocks, size, feat), BF16),
        in_specs=[SMEM, SMEM, anywhere] + [anywhere] * len(parts),
        out_specs=VMEM,
        scratch_shapes=[
            pltpu.VMEM(edge_tiles.shape, BF16),
            pltpu.VMEM((len(parts) * blocks, size, feat), BF16),
            pltpu.SemaphoreType.DMA((COPIES + len(parts),)),
        ],
        compiler_params=PARAMS,
        cost_estimate=pl.CostEstimate(flops=2 * edge_tiles.size * feat, bytes_accessed=30_000_000, transcendentals=0),
        name="aggregate",
    )(block_cols, at, edge_tiles, *parts)


def finish_kernel(pieces, at_ref, *rest):
    parts, rest = rest[: 2 * CHUNKS], rest[2 * CHUNKS :]
    total = [parts[2 * g][...].astype(F32) + parts[2 * g + 1][...].astype(F32) for g in range(CHUNKS)]
    count = parts[0].shape[0]
    if pieces == 0:
        for g in range(CHUNKS):
            for b in range(count):
                rest[0][g * count + b] = total[g][b].T.astype(BF16)
        return
    mask_ref, outs, held = rest[0], rest[1:-1], rest[-1]
    for g in range(CHUNKS):
        held[g * count : (g + 1) * count] = total[g].astype(BF16)
    per, feat = outs[0].shape[0], held.shape[1]
    for m in range(pieces):
        part = pl.ds(jnp.bitwise_xor(at_ref[1], m) * per, per)
        outs[m][:, :feat] = held[part]
        outs[m][:, feat:] = mask_ref[part]


def finish(parts, at, pieces, mask=()):
    count, feat, size = parts[0].shape
    blocks = count * CHUNKS
    if pieces == 0:
        outs, scratch = [jax.ShapeDtypeStruct((blocks, size, feat), BF16)], []
    else:
        outs = [jax.ShapeDtypeStruct((blocks // pieces, 2 * feat, size), BF16)] * pieces
        scratch = [pltpu.VMEM((blocks, feat, size), BF16)]
    return pl.pallas_call(
        functools.partial(finish_kernel, pieces),
        out_shape=outs,
        in_specs=[SMEM] + [VMEM] * (len(parts) + len(mask)),
        out_specs=[VMEM] * len(outs),
        scratch_shapes=scratch,
        compiler_params=PARAMS,
        name="finish",
    )(at, *parts, *mask)


def dense_kernel(cols, at_ref, weights_ref, *rest):
    sums, rest = rest[:cols], rest[cols:]
    outs, (sum_ref, delta_ref, held, mask) = rest[:cols], rest[cols:]
    col = at_ref[1]
    count, feat, size = outs[0].shape
    for m in range(cols):
        place = jnp.bitwise_xor(col, m)
        for b in range(count):
            sum_ref[place, :, b * size : (b + 1) * size] = sums[m][b, :feat]
            mask[place, :, b * size : (b + 1) * size] = sums[m][b, feat:].astype(F32)
    stacked = jnp.concatenate([sum_ref[q] for q in range(cols)], axis=0)
    for q in range(cols):
        grad = jnp.dot(weights_ref[q, 0], stacked, preferred_element_type=F32)
        delta_ref[q] = (grad * mask[q]).astype(BF16)
    delta = jnp.concatenate([delta_ref[q] for q in range(cols)], axis=0)
    for q in range(cols):
        res = jnp.dot(weights_ref[q, 1], delta, preferred_element_type=F32).astype(BF16)
        for b in range(count):
            held[q, b] = res[:, b * size : (b + 1) * size]
    for m in range(cols):
        outs[m][...] = held[jnp.bitwise_xor(col, m)]


def dense(weights, sums, at):
    cols = len(sums)
    count, feat, size = sums[0].shape
    feat = feat // 2
    out = jax.ShapeDtypeStruct((count, feat, size), BF16)
    flat = jax.ShapeDtypeStruct((cols, feat, count * size), BF16)
    res = pl.pallas_call(
        functools.partial(dense_kernel, cols),
        out_shape=[out] * cols + [flat] * 2,
        in_specs=[SMEM] + [VMEM] * (1 + cols),
        out_specs=[VMEM] * (cols + 2),
        scratch_shapes=[pltpu.VMEM((cols, count, feat, size), BF16), pltpu.VMEM((cols, feat, count * size), F32)],
        compiler_params=PARAMS,
        name="dense",
    )(at, weights, *sums)
    return res[:cols], res[cols], res[cols + 1]


def weight_terms_kernel(cols, at_ref, sum_ref, delta_ref, *rest):
    sides, rest = rest[:cols], rest[cols:]
    aggs, (keep_ref, send_ref) = rest[:cols], rest[cols:]
    even = jnp.bitwise_and(at_ref[0], 1) == 0
    count = aggs[0].shape[0]
    sums = jnp.concatenate([sum_ref[q] for q in range(cols)], axis=0)
    delta = jnp.concatenate([delta_ref[q] for q in range(cols)], axis=0)
    for m in range(cols):
        hidden = jnp.concatenate([sides[m][b] for b in range(count)], axis=0)
        agg = jnp.concatenate([aggs[m][b] for b in range(count)], axis=0)
        second = jnp.dot(sums, hidden, preferred_element_type=F32)
        first = jnp.dot(delta, agg, preferred_element_type=F32)
        keep_ref[m] = jnp.where(even, second, first).T
        send_ref[m] = jnp.where(even, first, second).T.astype(BF16)


def weight_terms(sums, delta, sides, aggs, at):
    cols, feat, _ = delta.shape
    shape = (cols, feat, cols * feat)
    return pl.pallas_call(
        functools.partial(weight_terms_kernel, cols),
        out_shape=[jax.ShapeDtypeStruct(shape, F32), jax.ShapeDtypeStruct(shape, BF16)],
        in_specs=[SMEM] + [VMEM] * (2 + 2 * cols),
        out_specs=[VMEM] * 2,
        compiler_params=PARAMS,
        name="weight_terms",
    )(at, sums, delta, *sides, *aggs)


def swap(value, mask, axis):
    return lax.ppermute(value, axis, [(i, i ^ mask) for i in range(lax.axis_size(axis))])


def swap_all(pieces, axis):
    return [pieces[0]] + [swap(pieces[m], m, axis) for m in range(1, len(pieces))]


def add(a, b):
    return (a.astype(F32) + b.astype(F32)).astype(BF16)


def scatter_chunk(keep, got, masks, beside):
    left = sorted(masks, reverse=True)
    for mask in masks:
        axis = left.index(mask)
        part = lambda v, i: lax.index_in_dim(v, i, axis, keepdims=False)
        sent = swap(add(part(keep, 1), part(got, 1)), mask, "row")
        keep = add(part(keep, 0), part(got, 0))
        got = sent
        left.remove(mask)
        if mask == masks[0]:
            got, beside = lax.optimization_barrier((got, beside))
    return [keep, got], beside


def scatter(pieces, rows, beside):
    masks = [1 << b for b in range(1, rows.bit_length() - 1)]
    lead = (2,) * len(masks)
    done = []
    for g in range(CHUNKS):
        keep, got = pieces[2 * g], swap(pieces[2 * g + 1], 1, "row")
        order = masks if g % 2 == 0 else masks[::-1]
        terms, beside = scatter_chunk(keep.reshape(lead + keep.shape[1:]), got.reshape(lead + got.shape[1:]), order, beside)
        done += terms
    return done, beside


def column_terms(keep, send):
    terms = keep + swap(send, 1, "row").astype(F32)
    return swap_all([terms[0]] + [terms[m].astype(BF16) for m in range(1, terms.shape[0])], "col")


def reduced(terms, me):
    value = sum(t.astype(F32) for t in terms)
    mask = 2
    while mask < lax.axis_size("row"):
        value = value.astype(BF16)
        value = value.astype(F32) + swap(value, mask, "row").astype(F32)
        mask *= 2
    other = swap(value, 1, "row")
    even = me % 2 == 0
    return jnp.where(even, other, value), jnp.where(even, value, other)


def gather_weights(weights, me, rows):
    kinds, out_rows, width = weights.shape
    part = lax.dynamic_slice_in_dim(weights, me * (out_rows // rows), out_rows // rows, 1)
    whole = lax.all_gather(part, ("row", "col"), axis=0)
    whole = whole.reshape(rows, -1, kinds, out_rows // rows, width)
    return whole.transpose(1, 2, 0, 3, 4).reshape(-1, kinds, out_rows, width)


def per_device(
    node_feats, hidden_act, grad_out, relu_mask, edge_tiles, block_cols, weight_one, weight_two
):
    rows, cols = lax.axis_size("row"), lax.axis_size("col")
    me, col = lax.axis_index("row").astype(jnp.int32), lax.axis_index("col").astype(jnp.int32)
    at = jnp.stack([me, col])
    blocks, _, size, _ = edge_tiles.shape
    blocked = lambda v: v.reshape(v.shape[0] // size, size, v.shape[1])
    after = lax.optimization_barrier

    def by_distance(v):
        per = blocks // cols
        return [lax.dynamic_slice_in_dim(v, (col ^ m) * per, per, 0) for m in range(cols)]

    weights = gather_weights(jnp.stack([weight_two, weight_one]), me, rows)
    node_feats = blocked(node_feats)
    near = {0: node_feats}
    for rel in [1 << b for b in range(rows.bit_length() - 1)]:
        near[rel] = swap(node_feats, rel, "row")
    pieces = spread(
        edge_tiles, block_cols, [blocked(grad_out)], at, rows, cols, [blocked(hidden_act), blocked(relu_mask)]
    )
    pieces, mask, sides = pieces[: 2 * CHUNKS], pieces[2 * CHUNKS], pieces[2 * CHUNKS + 1 :]
    pieces, near = after((pieces, near))
    terms, (sides, near) = scatter(pieces, rows, (swap_all(sides, "col"), near))
    for rel in range(2, rows):
        low, top = rel & 1, 1 << (rel.bit_length() - 1)
        if rel not in near:
            near[rel] = swap(near[rel - 1], 1, "row") if low else swap(near[rel - top], top, "row")
    last = near.pop(rows - 1)
    terms, near = after((terms, near))
    near[rows - 1] = last
    sums = swap_all(finish(terms, at, cols, [mask]), "col")
    parts = [near[rel] for rel in range(rows)]
    sums[1], weights = after((sums[1], weights))
    agg_feats = aggregate(edge_tiles, block_cols, parts, at)
    sums, agg_feats = after((sums, agg_feats))
    spread_in, sums, delta = dense(weights, sums, at)
    back = swap_all(spread_in, "col")
    agg_feats = swap_all(by_distance(agg_feats), "col")
    back, agg_feats = after((back, agg_feats))
    pieces = spread(edge_tiles, block_cols, back, at, rows, cols)
    grads = column_terms(*weight_terms(sums, delta, sides, agg_feats, at))
    terms, grads = scatter(pieces, rows, grads)
    (out,) = finish(terms, at, 0)
    first_grad, second_grad = reduced(grads, me)
    return out.reshape(-1, out.shape[2]), first_grad, second_grad


def solution(mesh):
    in_specs = (
        P("row", "col"),
        P("row", "col"),
        P("row", "col"),
        P("row", "col"),
        P("row", None, None, None),
        P("row", None),
        P("col", None),
        P("col", None),
    )
    out_specs = (P("row", "col"), P("col", None), P("col", None))
    return jax.shard_map(
        per_device, mesh=mesh, in_specs=in_specs, out_specs=out_specs, check_vma=False
    )
```

```python
import functools

import jax
import jax.numpy as jnp
from jax import lax
from jax.experimental import pallas as pl
from jax.experimental.pallas import tpu as pltpu
from jax.sharding import PartitionSpec as P

VMEM_LIMIT = 48 * 1024 * 1024
GROUPS = 2
COPIES = 4
F32 = jnp.float32
BF16 = jnp.bfloat16
VMEM = pl.BlockSpec(memory_space=pltpu.VMEM)
SMEM = pl.BlockSpec(memory_space=pltpu.SMEM)
PARAMS = pltpu.CompilerParams(vmem_limit_bytes=VMEM_LIMIT)


def tile_copy(tiles_ref, held, sems, i):
    per = held.shape[0] // COPIES
    part = pl.ds(i * per, per)
    return pltpu.make_async_copy(tiles_ref.at[part], held.at[part], sems.at[i])


def over_rows(tiles_ref, held, sems, one_row):
    per = held.shape[0] // COPIES

    def piece(i, carry):
        tile_copy(tiles_ref, held, sems, i).wait()
        for j in range(per):
            one_row(i * per + j)
        return carry

    lax.fori_loop(0, COPIES, piece, 0)


def spread_kernel(first, cols_ref, me_ref, tiles_ref, *rest):
    if first:
        vals_ref, mask_ref, *rest = rest
        outs, (mask_out, acc, held, sems, left_ref, mask_held) = rest[: 2 * GROUPS], rest[2 * GROUPS :]
        loads = [
            pltpu.make_async_copy(vals_ref, left_ref, sems.at[COPIES]),
            pltpu.make_async_copy(mask_ref, mask_held, sems.at[COPIES + 1]),
        ]
        loads[0].start()
    else:
        vals, rest = rest[:GROUPS], rest[GROUPS:]
        outs, (acc, held, sems, left_ref) = rest[: 2 * GROUPS], rest[2 * GROUPS :]
    for i in range(COPIES):
        tile_copy(tiles_ref, held, sems, i).start()
    if first:
        loads[1].start()
    acc[...] = jnp.zeros_like(acc)
    per_row, size = held.shape[1], held.shape[3]
    me = me_ref[0]
    if first:
        loads[0].wait()
    else:
        for g in range(GROUPS):
            count = vals[g].shape[0]
            left_ref[g * count : (g + 1) * count] = vals[g][...]

    def one_row(r):
        left = left_ref[r].astype(F32).T.astype(BF16) if first else left_ref[r]
        for k in range(0, per_row, 2):
            pair = jnp.concatenate([held[r, k], held[r, k + 1]], axis=1)
            both = jnp.dot(left, pair, preferred_element_type=F32)
            for side in range(2):
                acc[cols_ref[r, k + side]] += both[:, side * size : (side + 1) * size]

    over_rows(tiles_ref, held, sems, one_row)
    halves, count = outs[0].shape[:2]
    for g in range(GROUPS):
        for side in range(2):
            for rel in range(halves):
                owner = jnp.bitwise_xor(me, 2 * rel + side)
                start = (owner * GROUPS + g) * count
                outs[2 * g + side][rel] = acc[pl.ds(start, count)].astype(BF16)
    if first:
        loads[1].wait()
        for b in range(mask_held.shape[0]):
            mask_out[b] = mask_held[b].astype(F32).T.astype(BF16)


def spread(edge_tiles, block_cols, vals, me, rows, mask=None):
    blocks, _, size, _ = edge_tiles.shape
    first = mask is not None
    feat = vals[0].shape[2] if first else vals[0].shape[1]
    out = jax.ShapeDtypeStruct((rows // 2, blocks // GROUPS, feat, size), BF16)
    outs = [out] * (2 * GROUPS)
    scratch = [
        pltpu.VMEM((rows * blocks, feat, size), F32),
        pltpu.VMEM(edge_tiles.shape, BF16),
        pltpu.SemaphoreType.DMA((COPIES + 2,)),
    ]
    anywhere = pl.BlockSpec(memory_space=pl.ANY)
    if first:
        outs.append(jax.ShapeDtypeStruct((blocks, feat, size), BF16))
        scratch += [pltpu.VMEM(v.shape, v.dtype) for v in (vals[0], mask)]
        args, place = [vals[0], mask], anywhere
    else:
        scratch.append(pltpu.VMEM((blocks, feat, size), BF16))
        args, place = vals, VMEM
    return pl.pallas_call(
        functools.partial(spread_kernel, first),
        out_shape=outs,
        in_specs=[SMEM, SMEM, anywhere] + [place] * len(args),
        out_specs=[VMEM] * len(outs),
        scratch_shapes=scratch,
        compiler_params=PARAMS,
        cost_estimate=pl.CostEstimate(flops=2 * edge_tiles.size * feat, bytes_accessed=30_000_000, transcendentals=0),
        name="spread",
    )(block_cols, me, edge_tiles, *args)


def aggregate_kernel(cols_ref, tiles_ref, values_ref, out_ref, held, table, sems):
    load = pltpu.make_async_copy(values_ref, table, sems.at[COPIES])
    load.start()
    for i in range(COPIES):
        tile_copy(tiles_ref, held, sems, i).start()
    load.wait()
    per_row = held.shape[1]

    def one_row(r):
        total = None
        for k in range(0, per_row, 2):
            pair = jnp.concatenate([held[r, k], held[r, k + 1]], axis=1)
            picked = jnp.concatenate([table[cols_ref[r, k]], table[cols_ref[r, k + 1]]], axis=0)
            term = jnp.dot(pair, picked, preferred_element_type=F32)
            total = term if total is None else total + term
        out_ref[r] = total.astype(BF16)

    over_rows(tiles_ref, held, sems, one_row)


def aggregate(edge_tiles, block_cols, values):
    blocks, _, size, _ = edge_tiles.shape
    feat = values.shape[2]
    anywhere = pl.BlockSpec(memory_space=pl.ANY)
    return pl.pallas_call(
        aggregate_kernel,
        out_shape=jax.ShapeDtypeStruct((blocks, size, feat), BF16),
        in_specs=[SMEM, anywhere, anywhere],
        out_specs=VMEM,
        scratch_shapes=[
            pltpu.VMEM(edge_tiles.shape, BF16),
            pltpu.VMEM(values.shape, BF16),
            pltpu.SemaphoreType.DMA((COPIES + 1,)),
        ],
        compiler_params=PARAMS,
        cost_estimate=pl.CostEstimate(flops=2 * edge_tiles.size * feat, bytes_accessed=20_000_000, transcendentals=0),
        name="aggregate",
    )(block_cols, edge_tiles, values)


def sum_kernel(keep_ref, got_ref, out_ref):
    out_ref[...] = (keep_ref[...].astype(F32) + got_ref[...].astype(F32)).astype(BF16)


def last_sum(keep, got):
    return pl.pallas_call(
        sum_kernel,
        out_shape=jax.ShapeDtypeStruct(keep.shape, BF16),
        in_specs=[VMEM] * 2,
        out_specs=VMEM,
        compiler_params=PARAMS,
        name="last_sum",
    )(keep, got)


def finish_kernel(*refs):
    parts, out_ref = refs[:-1], refs[-1]
    count = parts[0].shape[0]
    for g in range(GROUPS):
        for b in range(count):
            total = parts[2 * g][b].astype(F32) + parts[2 * g + 1][b].astype(F32)
            out_ref[g * count + b] = total.T.astype(BF16)


def finish(parts):
    count, feat, size = parts[0].shape
    return pl.pallas_call(
        finish_kernel,
        out_shape=jax.ShapeDtypeStruct((count * GROUPS, size, feat), BF16),
        in_specs=[VMEM] * len(parts),
        out_specs=VMEM,
        compiler_params=PARAMS,
        name="finish",
    )(*parts)


def dense_kernel(cols, masked, col_ref, weight_ref, *rest):
    shards, rest = rest[: 2 * cols - 1], rest[2 * cols - 1 :]
    side_ref, rest = rest[0], rest[1:]
    if masked:
        mask_ref, rest = rest[0], rest[1:]
    out_ref, grad_ref, whole_ref = rest
    own, ups, downs = shards[0], shards[1:cols], shards[cols:]
    col = col_ref[0]
    blocks, feat, size = own.shape
    for s in range(cols):
        place = lax.rem(col - s + cols, cols)
        for b in range(blocks):
            part = own[b] if s == 0 else jnp.where(col >= s, ups[s - 1][b], downs[cols - s - 1][b])
            whole_ref[place, :, b * size : (b + 1) * size] = part
    whole = jnp.concatenate([whole_ref[q] for q in range(cols)], axis=0)
    res = jnp.dot(weight_ref[...], whole, preferred_element_type=F32)
    for b in range(blocks):
        part = res[:, b * size : (b + 1) * size]
        out_ref[b] = (part * mask_ref[b].astype(F32) if masked else part).astype(BF16)
    side = jnp.concatenate([side_ref[b] for b in range(blocks)], axis=0)
    grad_ref[...] = jnp.dot(whole, side, preferred_element_type=F32)


def dense(weight, shards, side, mask, col, cols):
    blocks, feat, size = shards[0].shape
    args = [weight, *shards, side] + ([] if mask is None else [mask])
    return pl.pallas_call(
        functools.partial(dense_kernel, cols, mask is not None),
        out_shape=[
            jax.ShapeDtypeStruct((blocks, feat, size), BF16),
            jax.ShapeDtypeStruct((cols * feat, side.shape[2]), F32),
        ],
        in_specs=[SMEM] + [VMEM] * len(args),
        out_specs=[VMEM, VMEM],
        scratch_shapes=[pltpu.VMEM((cols, feat, blocks * size), BF16)],
        compiler_params=PARAMS,
        name="dense",
    )(col, *args)


def weight_terms_kernel(me_ref, *refs):
    firsts, seconds = refs[:GROUPS], refs[GROUPS : 2 * GROUPS]
    keep_ref, send_ref = refs[2 * GROUPS :]
    first, second = sum(r[...] for r in firsts).T, sum(r[...] for r in seconds).T
    even = jnp.bitwise_and(me_ref[0], 1) == 0
    keep_ref[...] = jnp.where(even, second, first)
    send_ref[...] = jnp.where(even, first, second).astype(BF16)


def weight_terms(firsts, seconds, me):
    shape = firsts[0].shape[::-1]
    return pl.pallas_call(
        weight_terms_kernel,
        out_shape=[jax.ShapeDtypeStruct(shape, F32), jax.ShapeDtypeStruct(shape, BF16)],
        in_specs=[SMEM] + [VMEM] * (2 * GROUPS),
        out_specs=[VMEM] * 2,
        compiler_params=PARAMS,
        name="weight_terms",
    )(me, *firsts, *seconds)


def swap(value, mask, axis):
    return lax.ppermute(value, axis, [(i, i ^ mask) for i in range(lax.axis_size(axis))])


def add(a, b):
    return (a.astype(F32) + b.astype(F32)).astype(BF16)


def scatter_group(keep, got, masks, beside):
    left = sorted(masks, reverse=True)
    for mask in masks:
        axis = left.index(mask)
        part = lambda v, i: lax.index_in_dim(v, i, axis, keepdims=False)
        sent = swap(add(part(keep, 1), part(got, 1)), mask, "row")
        keep = add(part(keep, 0), part(got, 0))
        got = sent
        left.remove(mask)
        if beside is not None and mask == masks[0]:
            got, beside = lax.optimization_barrier((got, beside))
    return [keep, got], beside


def scatter(pieces, rows, beside=None):
    masks = [1 << b for b in range(1, rows.bit_length() - 1)]
    lead = (2,) * len(masks)
    done = []
    for g in range(GROUPS):
        keep, got = pieces[2 * g], swap(pieces[2 * g + 1], 1, "row")
        order = masks if g % 2 == 0 else masks[::-1]
        terms, beside = scatter_group(keep.reshape(lead + keep.shape[1:]), got.reshape(lead + got.shape[1:]), order, beside)
        done.append(terms)
    return done, beside


def chain_gather(own, cols):
    ups, downs = [], []
    up, down = own, own
    for s in range(1, cols):
        up = lax.ppermute(up, "col", [(i, i + 1) for i in range(s - 1, cols - 1)])
        down = lax.ppermute(down, "col", [(i, i - 1) for i in range(1, cols - s + 1)])
        ups.append(up)
        downs.append(down)
    return [own, *ups, *downs]


def reduced(value, me):
    mask = 2
    while mask < lax.axis_size("row"):
        value = value.astype(BF16)
        value = value.astype(F32) + swap(value, mask, "row").astype(F32)
        mask *= 2
    other = swap(value, 1, "row")
    even = me % 2 == 0
    return jnp.where(even, other, value), jnp.where(even, value, other)


def per_device(
    node_feats, hidden_act, grad_out, relu_mask, edge_tiles, block_cols, weight_one, weight_two
):
    rows, cols = lax.axis_size("row"), lax.axis_size("col")
    me, col = lax.axis_index("row").astype(jnp.int32), lax.axis_index("col").astype(jnp.int32)
    me_at, col_at = me.reshape(1), col.reshape(1)
    size = edge_tiles.shape[2]
    per = edge_tiles.shape[0] // GROUPS
    blocked = lambda v: v.reshape(v.shape[0] // size, size, v.shape[1])
    cut = lambda v, g: v[g * per : (g + 1) * per]

    *pieces, mask = spread(edge_tiles, block_cols, [blocked(grad_out)], me_at, rows, blocked(relu_mask))
    terms, _ = scatter(pieces, rows)
    terms, node_feats = lax.optimization_barrier((terms, node_feats))
    table = blocked(lax.all_gather(node_feats, "row", axis=0, tiled=True))
    deltas, seconds, inputs, firsts = [], [], [], []
    hidden = blocked(hidden_act)
    for g in range(GROUPS):
        shards = chain_gather(last_sum(*terms[g]), cols)
        delta, grad = dense(weight_two, shards, cut(hidden, g), cut(mask, g), col_at, cols)
        deltas.append(delta)
        seconds.append(grad)
    agg_feats = aggregate(edge_tiles, block_cols, table)
    for g in range(GROUPS):
        shards = chain_gather(deltas[g], cols)
        out, grad = dense(weight_one, shards, cut(agg_feats, g), None, col_at, cols)
        inputs.append(out)
        firsts.append(grad)
    pieces = spread(edge_tiles, block_cols, inputs, me_at, rows)
    keep, send = weight_terms(firsts, seconds, me_at)
    terms, value = scatter(pieces, rows, keep + swap(send, 1, "row").astype(F32))
    out = finish([t for pair in terms for t in pair])
    first_grad, second_grad = reduced(value, me)
    return out.reshape(-1, out.shape[2]), first_grad, second_grad


def solution(mesh):
    in_specs = (
        P("row", "col"),
        P("row", "col"),
        P("row", "col"),
        P("row", "col"),
        P("row", None, None, None),
        P("row", None),
        P("col", None),
        P("col", None),
    )
    out_specs = (P("row", "col"), P("col", None), P("col", None))
    return jax.shard_map(
        per_device, mesh=mesh, in_specs=in_specs, out_specs=out_specs, check_vma=False
    )
```

```python
import functools

import jax
import jax.numpy as jnp
from jax import lax
from jax.experimental import pallas as pl
from jax.experimental.pallas import tpu as pltpu
from jax.sharding import PartitionSpec as P

VMEM_LIMIT = 48 * 1024 * 1024
GROUPS = 2
COPIES = 4
F32 = jnp.float32
BF16 = jnp.bfloat16
VMEM = pl.BlockSpec(memory_space=pltpu.VMEM)
SMEM = pl.BlockSpec(memory_space=pltpu.SMEM)
PARAMS = pltpu.CompilerParams(vmem_limit_bytes=VMEM_LIMIT)


def tile_copy(tiles_ref, held, sems, i):
    per = held.shape[0] // COPIES
    part = pl.ds(i * per, per)
    return pltpu.make_async_copy(tiles_ref.at[part], held.at[part], sems.at[i])


def over_rows(tiles_ref, held, sems, one_row):
    per = held.shape[0] // COPIES

    def piece(i, carry):
        tile_copy(tiles_ref, held, sems, i).wait()
        for j in range(per):
            one_row(i * per + j)
        return carry

    lax.fori_loop(0, COPIES, piece, 0)


def spread_kernel(first, cols_ref, me_ref, tiles_ref, *rest):
    if first:
        vals_ref, mask_ref, *rest = rest
        outs, (mask_out, acc, held, sems, left_ref, mask_held) = rest[: 2 * GROUPS], rest[2 * GROUPS :]
        loads = [
            pltpu.make_async_copy(vals_ref, left_ref, sems.at[COPIES]),
            pltpu.make_async_copy(mask_ref, mask_held, sems.at[COPIES + 1]),
        ]
        loads[0].start()
    else:
        vals, rest = rest[:GROUPS], rest[GROUPS:]
        outs, (acc, held, sems, left_ref) = rest[: 2 * GROUPS], rest[2 * GROUPS :]
    for i in range(COPIES):
        tile_copy(tiles_ref, held, sems, i).start()
    if first:
        loads[1].start()
    acc[...] = jnp.zeros_like(acc)
    per_row, size = held.shape[1], held.shape[3]
    me = me_ref[0]
    if first:
        loads[0].wait()
    else:
        for g in range(GROUPS):
            count = vals[g].shape[0]
            left_ref[g * count : (g + 1) * count] = vals[g][...]

    def one_row(r):
        left = left_ref[r].astype(F32).T.astype(BF16) if first else left_ref[r]
        for k in range(0, per_row, 2):
            pair = jnp.concatenate([held[r, k], held[r, k + 1]], axis=1)
            both = jnp.dot(left, pair, preferred_element_type=F32)
            for side in range(2):
                acc[cols_ref[r, k + side]] += both[:, side * size : (side + 1) * size]

    over_rows(tiles_ref, held, sems, one_row)
    halves, count = outs[0].shape[:2]
    for g in range(GROUPS):
        for side in range(2):
            for rel in range(halves):
                owner = jnp.bitwise_xor(me, 2 * rel + side)
                start = (owner * GROUPS + g) * count
                outs[2 * g + side][rel] = acc[pl.ds(start, count)].astype(BF16)
    if first:
        loads[1].wait()
        for b in range(mask_held.shape[0]):
            mask_out[b] = mask_held[b].astype(F32).T.astype(BF16)


def spread(edge_tiles, block_cols, vals, me, rows, mask=None):
    blocks, _, size, _ = edge_tiles.shape
    first = mask is not None
    feat = vals[0].shape[2] if first else vals[0].shape[1]
    out = jax.ShapeDtypeStruct((rows // 2, blocks // GROUPS, feat, size), BF16)
    outs = [out] * (2 * GROUPS)
    scratch = [
        pltpu.VMEM((rows * blocks, feat, size), F32),
        pltpu.VMEM(edge_tiles.shape, BF16),
        pltpu.SemaphoreType.DMA((COPIES + 2,)),
    ]
    anywhere = pl.BlockSpec(memory_space=pl.ANY)
    if first:
        outs.append(jax.ShapeDtypeStruct((blocks, feat, size), BF16))
        scratch += [pltpu.VMEM(v.shape, v.dtype) for v in (vals[0], mask)]
        args, place = [vals[0], mask], anywhere
    else:
        scratch.append(pltpu.VMEM((blocks, feat, size), BF16))
        args, place = vals, VMEM
    return pl.pallas_call(
        functools.partial(spread_kernel, first),
        out_shape=outs,
        in_specs=[SMEM, SMEM, anywhere] + [place] * len(args),
        out_specs=[VMEM] * len(outs),
        scratch_shapes=scratch,
        compiler_params=PARAMS,
        cost_estimate=pl.CostEstimate(flops=2 * edge_tiles.size * feat, bytes_accessed=30_000_000, transcendentals=0),
        name="spread",
    )(block_cols, me, edge_tiles, *args)


def aggregate_kernel(start, cols_ref, tiles_ref, table_ref, out_ref, held, sems):
    rows = tiles_ref.at[pl.ds(start, held.shape[0])]
    for i in range(COPIES):
        tile_copy(rows, held, sems, i).start()
    per_row = held.shape[1]

    def one_row(r):
        total = None
        for k in range(0, per_row, 2):
            pair = jnp.concatenate([held[r, k], held[r, k + 1]], axis=1)
            left, right = cols_ref[start + r, k], cols_ref[start + r, k + 1]
            picked = jnp.concatenate([table_ref[left], table_ref[right]], axis=0)
            term = jnp.dot(pair, picked, preferred_element_type=F32)
            total = term if total is None else total + term
        out_ref[r] = total.astype(BF16)

    over_rows(rows, held, sems, one_row)


def aggregate(edge_tiles, block_cols, table, start, count):
    _, per_row, size, _ = edge_tiles.shape
    feat = table.shape[2]
    return pl.pallas_call(
        functools.partial(aggregate_kernel, start),
        out_shape=jax.ShapeDtypeStruct((count, size, feat), BF16),
        in_specs=[SMEM, pl.BlockSpec(memory_space=pl.ANY), VMEM],
        out_specs=VMEM,
        scratch_shapes=[
            pltpu.VMEM((count, per_row, size, size), BF16),
            pltpu.SemaphoreType.DMA((COPIES,)),
        ],
        compiler_params=PARAMS,
        cost_estimate=pl.CostEstimate(flops=2 * edge_tiles.size * feat, bytes_accessed=10_000_000, transcendentals=0),
        name="aggregate",
    )(block_cols, edge_tiles, table)


def chip_sum_kernel(groups, *refs):
    ins, outs = refs[: 2 * groups], refs[2 * groups :]
    count = ins[0].shape[1]
    for g in range(groups):
        keep_ref, got_ref = ins[2 * g : 2 * g + 2]
        for rel, out in enumerate(outs):
            out[g * count : (g + 1) * count] = (keep_ref[rel].astype(F32) + got_ref[rel].astype(F32)).astype(BF16)


def chip_sum(*pairs):
    chips, count, feat, size = pairs[0].shape
    groups = len(pairs) // 2
    return pl.pallas_call(
        functools.partial(chip_sum_kernel, groups),
        out_shape=[jax.ShapeDtypeStruct((groups * count, feat, size), BF16)] * chips,
        in_specs=[VMEM] * len(pairs),
        out_specs=[VMEM] * chips,
        compiler_params=PARAMS,
        name="chip_sum",
    )(*pairs)


def last_sum_kernel(*refs):
    refs[-1][...] = sum(ref[...].astype(F32) for ref in refs[:-1]).astype(BF16)


def last_sum(terms):
    return pl.pallas_call(
        last_sum_kernel,
        out_shape=jax.ShapeDtypeStruct(terms[0].shape, BF16),
        in_specs=[VMEM] * len(terms),
        out_specs=VMEM,
        compiler_params=PARAMS,
        name="last_sum",
    )(*terms)


def finish_kernel(*refs):
    parts, out_ref = refs[:-1], refs[-1]
    for b in range(parts[0].shape[0]):
        out_ref[b] = sum(part[b].astype(F32) for part in parts).T.astype(BF16)


def finish(parts):
    count, feat, size = parts[0].shape
    return pl.pallas_call(
        finish_kernel,
        out_shape=jax.ShapeDtypeStruct((count, size, feat), BF16),
        in_specs=[VMEM] * len(parts),
        out_specs=VMEM,
        compiler_params=PARAMS,
        cost_estimate=pl.CostEstimate(flops=0, bytes_accessed=1_000_000_000, transcendentals=0),
        name="finish",
    )(*parts)


def arrivals(shards, col, cols):
    if cols == 4:
        inner, low = (col == 1) | (col == 2), col < 2
        return [
            (col, None, shards[0], None),
            (jnp.bitwise_xor(col, 1), None, shards[1], None),
            (jnp.where(low, 2, 1), inner, shards[2], shards[3]),
            (jnp.where(low, 3, 0), inner, shards[4], shards[5]),
        ]
    ups, downs = shards[1:cols], shards[cols:]
    return [(col, None, shards[0], None)] + [
        (lax.rem(col - s + cols, cols), col >= s, ups[s - 1], downs[cols - s - 1]) for s in range(1, cols)
    ]


def dense_kernel(cols, masked, col_ref, weight_ref, *rest):
    count = 6 if cols == 4 else 2 * cols - 1
    shards, rest = rest[:count], rest[count:]
    side_ref, rest = rest[0], rest[1:]
    if masked:
        mask_ref, rest = rest[0], rest[1:]
    out_ref, grad_ref, whole_ref = rest
    col = col_ref[0]
    blocks, feat, size = shards[0].shape
    for place, use, one, other in arrivals(shards, col, cols):
        for b in range(blocks):
            part = one[b] if other is None else jnp.where(use, one[b], other[b])
            whole_ref[place, :, b * size : (b + 1) * size] = part
    whole = jnp.concatenate([whole_ref[q] for q in range(cols)], axis=0)
    res = jnp.dot(weight_ref[...], whole, preferred_element_type=F32)
    for b in range(blocks):
        part = res[:, b * size : (b + 1) * size]
        out_ref[b] = (part * mask_ref[b].astype(F32) if masked else part).astype(BF16)
    side = jnp.concatenate([side_ref[b] for b in range(blocks)], axis=0)
    grad_ref[...] = jnp.dot(whole, side, preferred_element_type=F32)


def dense(weight, shards, side, mask, col, cols):
    blocks, feat, size = shards[0].shape
    args = [weight, *shards, side] + ([] if mask is None else [mask])
    return pl.pallas_call(
        functools.partial(dense_kernel, cols, mask is not None),
        out_shape=[
            jax.ShapeDtypeStruct((blocks, feat, size), BF16),
            jax.ShapeDtypeStruct((cols * feat, side.shape[2]), F32),
        ],
        in_specs=[SMEM] + [VMEM] * len(args),
        out_specs=[VMEM, VMEM],
        scratch_shapes=[pltpu.VMEM((cols, feat, blocks * size), BF16)],
        compiler_params=PARAMS,
        name="dense",
    )(col, *args)


def weight_terms_kernel(me_ref, *refs):
    firsts, seconds = refs[:GROUPS], refs[GROUPS : 2 * GROUPS]
    keep_ref, send_ref = refs[2 * GROUPS :]
    first, second = sum(r[...] for r in firsts).T, sum(r[...] for r in seconds).T
    even = jnp.bitwise_and(me_ref[0], 1) == 0
    keep_ref[...] = jnp.where(even, second, first)
    send_ref[...] = jnp.where(even, first, second).astype(BF16)


def weight_terms(firsts, seconds, me):
    shape = firsts[0].shape[::-1]
    return pl.pallas_call(
        weight_terms_kernel,
        out_shape=[jax.ShapeDtypeStruct(shape, F32), jax.ShapeDtypeStruct(shape, BF16)],
        in_specs=[SMEM] + [VMEM] * (2 * GROUPS),
        out_specs=[VMEM] * 2,
        compiler_params=PARAMS,
        name="weight_terms",
    )(me, *firsts, *seconds)


def swap(value, mask, axis):
    return lax.ppermute(value, axis, [(i, i ^ mask) for i in range(lax.axis_size(axis))])


def from_chips(parts):
    return [parts[0]] + [swap(part, 2 * i, "row") for i, part in enumerate(parts) if i > 0]


def other_core(pieces):
    return [v for g in range(GROUPS) for v in (pieces[2 * g], swap(pieces[2 * g + 1], 1, "row"))]


def gather_columns(own, cols, beside):
    if cols == 4:
        middle, outward = [(1, 2), (2, 1)], [(1, 0), (2, 3)]
        near = swap(own, 1, "col")
        across = lax.ppermute(own, "col", middle)
        near, across, beside = lax.optimization_barrier((near, across, beside))
        far = lax.ppermute(near, "col", middle)
        return [own, near, across, lax.ppermute(across, "col", outward), far, lax.ppermute(far, "col", outward)], beside
    ups, downs = [], []
    up, down = own, own
    for s in range(1, cols):
        up = lax.ppermute(up, "col", [(i, i + 1) for i in range(s - 1, cols - 1)])
        down = lax.ppermute(down, "col", [(i, i - 1) for i in range(1, cols - s + 1)])
        ups.append(up)
        downs.append(down)
    return [own, *ups, *downs], beside


def over_chips(value, rows):
    mask = 2
    while mask < rows:
        value = value.astype(BF16)
        value = value.astype(F32) + swap(value, mask, "row").astype(F32)
        mask *= 2
    return value


def per_device(
    node_feats, hidden_act, grad_out, relu_mask, edge_tiles, block_cols, weight_one, weight_two
):
    rows, cols = lax.axis_size("row"), lax.axis_size("col")
    me, col = lax.axis_index("row").astype(jnp.int32), lax.axis_index("col").astype(jnp.int32)
    me_at, col_at = me.reshape(1), col.reshape(1)
    size = edge_tiles.shape[2]
    per = edge_tiles.shape[0] // GROUPS
    blocked = lambda v: v.reshape(v.shape[0] // size, size, v.shape[1])
    cut = lambda v, g: v[g * per : (g + 1) * per]

    *pieces, mask = spread(edge_tiles, block_cols, [blocked(grad_out)], me_at, rows, blocked(relu_mask))
    pieces = other_core(pieces)
    deltas, seconds, inputs, firsts = [], [], [], []
    hidden = blocked(hidden_act)
    for g in range(GROUPS):
        own = last_sum(from_chips(chip_sum(*pieces[2 * g : 2 * g + 2])))
        shards, node_feats = gather_columns(own, cols, node_feats)
        delta, grad = dense(weight_two, shards, cut(hidden, g), cut(mask, g), col_at, cols)
        deltas.append(delta)
        seconds.append(grad)
    table = blocked(lax.all_gather(node_feats, "row", axis=0, tiled=True))
    for g in range(GROUPS):
        agg_feats = aggregate(edge_tiles, block_cols, table, g * per, per)
        shards, agg_feats = gather_columns(deltas[g], cols, agg_feats)
        out, grad = dense(weight_one, shards, agg_feats, None, col_at, cols)
        inputs.append(out)
        firsts.append(grad)
    pieces = spread(edge_tiles, block_cols, inputs, me_at, rows)
    terms = from_chips(chip_sum(*other_core(pieces)))
    keep, send = weight_terms(firsts, seconds, me_at)
    value = over_chips(keep + swap(send, 1, "row").astype(F32), rows)
    terms, value = lax.optimization_barrier((terms, value))
    out = finish(terms)
    other = swap(value, 1, "row")
    even = me % 2 == 0
    first_grad, second_grad = jnp.where(even, other, value), jnp.where(even, value, other)
    return out.reshape(-1, out.shape[2]), first_grad, second_grad


def solution(mesh):
    in_specs = (
        P("row", "col"),
        P("row", "col"),
        P("row", "col"),
        P("row", "col"),
        P("row", None, None, None),
        P("row", None),
        P("col", None),
        P("col", None),
    )
    out_specs = (P("row", "col"), P("col", None), P("col", None))
    return jax.shard_map(
        per_device, mesh=mesh, in_specs=in_specs, out_specs=out_specs, check_vma=False
    )
```

```python
import functools

import jax
import jax.numpy as jnp
from jax import lax
from jax.experimental import pallas as pl
from jax.experimental.pallas import tpu as pltpu
from jax.sharding import PartitionSpec as P

VMEM_LIMIT = 48 * 1024 * 1024
GROUPS = 2
COPIES = 4
F32 = jnp.float32
BF16 = jnp.bfloat16
VMEM = pl.BlockSpec(memory_space=pltpu.VMEM)
SMEM = pl.BlockSpec(memory_space=pltpu.SMEM)
PARAMS = pltpu.CompilerParams(vmem_limit_bytes=VMEM_LIMIT)


def tile_copy(tiles_ref, held, sems, i):
    per = held.shape[0] // COPIES
    part = pl.ds(i * per, per)
    return pltpu.make_async_copy(tiles_ref.at[part], held.at[part], sems.at[i])


def over_rows(tiles_ref, held, sems, one_row):
    per = held.shape[0] // COPIES

    def piece(i, carry):
        tile_copy(tiles_ref, held, sems, i).wait()
        for j in range(per):
            one_row(i * per + j)
        return carry

    lax.fori_loop(0, COPIES, piece, 0)


def spread_kernel(first, cols_ref, me_ref, tiles_ref, vals_ref, *rest):
    if first:
        mask_ref, *rest = rest
        outs, (mask_out, acc, held, sems, left_ref, mask_held) = rest[: 2 * GROUPS], rest[2 * GROUPS :]
        loads = [
            pltpu.make_async_copy(vals_ref, left_ref, sems.at[COPIES]),
            pltpu.make_async_copy(mask_ref, mask_held, sems.at[COPIES + 1]),
        ]
        loads[0].start()
    else:
        outs, (acc, held, sems) = rest[: 2 * GROUPS], rest[2 * GROUPS :]
    for i in range(COPIES):
        tile_copy(tiles_ref, held, sems, i).start()
    if first:
        loads[1].start()
    acc[...] = jnp.zeros_like(acc)
    per_row, size = held.shape[1], held.shape[3]
    me = me_ref[0]
    if first:
        loads[0].wait()

    def one_row(r):
        left = left_ref[r].astype(F32).T.astype(BF16) if first else vals_ref[r]
        for k in range(0, per_row, 2):
            pair = jnp.concatenate([held[r, k], held[r, k + 1]], axis=1)
            both = jnp.dot(left, pair, preferred_element_type=F32)
            for side in range(2):
                acc[cols_ref[r, k + side]] += both[:, side * size : (side + 1) * size]

    over_rows(tiles_ref, held, sems, one_row)
    halves, count = outs[0].shape[:2]
    for g in range(GROUPS):
        for side in range(2):
            for rel in range(halves):
                owner = jnp.bitwise_xor(me, 2 * rel + side)
                start = (owner * GROUPS + g) * count
                outs[2 * g + side][rel] = acc[pl.ds(start, count)].astype(BF16)
    if first:
        loads[1].wait()
        for b in range(mask_held.shape[0]):
            mask_out[b] = mask_held[b].astype(F32).T.astype(BF16)


def spread(edge_tiles, block_cols, vals, me, rows, mask=None):
    blocks, _, size, _ = edge_tiles.shape
    first = mask is not None
    feat = vals.shape[2] if first else vals.shape[1]
    out = jax.ShapeDtypeStruct((rows // 2, blocks // GROUPS, feat, size), BF16)
    outs = [out] * (2 * GROUPS)
    scratch = [
        pltpu.VMEM((rows * blocks, feat, size), F32),
        pltpu.VMEM(edge_tiles.shape, BF16),
        pltpu.SemaphoreType.DMA((COPIES + 2,)),
    ]
    anywhere = pl.BlockSpec(memory_space=pl.ANY)
    if first:
        outs.append(jax.ShapeDtypeStruct((blocks, feat, size), BF16))
        scratch += [pltpu.VMEM(v.shape, v.dtype) for v in (vals, mask)]
        args, place = [vals, mask], anywhere
    else:
        args, place = [vals], VMEM
    return pl.pallas_call(
        functools.partial(spread_kernel, first),
        out_shape=outs,
        in_specs=[SMEM, SMEM, anywhere] + [place] * len(args),
        out_specs=[VMEM] * len(outs),
        scratch_shapes=scratch,
        compiler_params=PARAMS,
        cost_estimate=pl.CostEstimate(flops=2 * edge_tiles.size * feat, bytes_accessed=30_000_000, transcendentals=0),
        name="spread",
    )(block_cols, me, edge_tiles, *args)


def aggregate_kernel(cols_ref, me_ref, tiles_ref, *rest):
    parts, (out_ref, held, table, sems) = rest[:-4], rest[-4:]
    blocks, per_row = held.shape[:2]
    loads = []
    for rel, part in enumerate(parts):
        place = table.at[pl.ds(jnp.bitwise_xor(me_ref[0], rel) * blocks, blocks)]
        loads.append(pltpu.make_async_copy(part, place, sems.at[COPIES + rel]))
    for load in loads:
        load.start()
    for i in range(COPIES):
        tile_copy(tiles_ref, held, sems, i).start()
    for load in loads:
        load.wait()

    def one_row(r):
        total = None
        for k in range(0, per_row, 2):
            pair = jnp.concatenate([held[r, k], held[r, k + 1]], axis=1)
            picked = jnp.concatenate([table[cols_ref[r, k]], table[cols_ref[r, k + 1]]], axis=0)
            term = jnp.dot(pair, picked, preferred_element_type=F32)
            total = term if total is None else total + term
        out_ref[r] = total.astype(BF16)

    over_rows(tiles_ref, held, sems, one_row)


def aggregate(edge_tiles, block_cols, parts, me):
    blocks, _, size, _ = edge_tiles.shape
    feat = parts[0].shape[2]
    anywhere = pl.BlockSpec(memory_space=pl.ANY)
    return pl.pallas_call(
        aggregate_kernel,
        out_shape=jax.ShapeDtypeStruct((blocks, size, feat), BF16),
        in_specs=[SMEM, SMEM, anywhere] + [anywhere] * len(parts),
        out_specs=VMEM,
        scratch_shapes=[
            pltpu.VMEM(edge_tiles.shape, BF16),
            pltpu.VMEM((len(parts) * blocks, size, feat), BF16),
            pltpu.SemaphoreType.DMA((COPIES + len(parts),)),
        ],
        compiler_params=PARAMS,
        cost_estimate=pl.CostEstimate(flops=2 * edge_tiles.size * feat, bytes_accessed=30_000_000, transcendentals=0),
        name="aggregate",
    )(block_cols, me, edge_tiles, *parts)


def finish_kernel(last, *refs):
    parts, out_ref = refs[:-1], refs[-1]
    count = parts[0].shape[0]
    for g in range(GROUPS):
        for b in range(count):
            total = parts[2 * g][b].astype(F32) + parts[2 * g + 1][b].astype(F32)
            out_ref[g * count + b] = (total.T if last else total).astype(BF16)


def finish(parts, last):
    count, feat, size = parts[0].shape
    return pl.pallas_call(
        functools.partial(finish_kernel, last),
        out_shape=jax.ShapeDtypeStruct((count * GROUPS,) + ((size, feat) if last else (feat, size)), BF16),
        in_specs=[VMEM] * len(parts),
        out_specs=VMEM,
        compiler_params=PARAMS,
        cost_estimate=pl.CostEstimate(flops=0, bytes_accessed=1_000_000_000 if last else 1, transcendentals=0),
        name="finish",
    )(*parts)


def dense_kernel(cols, masked, col_ref, weight_ref, *rest):
    shards, rest = rest[:cols], rest[cols:]
    side_ref, rest = rest[0], rest[1:]
    if masked:
        mask_ref, rest = rest[0], rest[1:]
    out_ref, grad_ref, whole_ref = rest
    blocks, feat, size = shards[0].shape
    for m in range(cols):
        place = jnp.bitwise_xor(col_ref[0], m)
        for b in range(blocks):
            whole_ref[place, :, b * size : (b + 1) * size] = shards[m][b]
    half = blocks * size // 2
    total = None
    for h in range(2):
        whole = jnp.concatenate([whole_ref[q, :, h * half : (h + 1) * half] for q in range(cols)], axis=0)
        res = jnp.dot(weight_ref[...], whole, preferred_element_type=F32)
        for i in range(blocks // 2):
            b = h * (blocks // 2) + i
            part = res[:, i * size : (i + 1) * size]
            out_ref[b] = (part * mask_ref[b].astype(F32) if masked else part).astype(BF16)
        side = jnp.concatenate([side_ref[h * (blocks // 2) + i] for i in range(blocks // 2)], axis=0)
        term = jnp.dot(whole, side, preferred_element_type=F32)
        total = term if total is None else total + term
    grad_ref[...] = total


def dense(weight, shards, side, mask, col):
    blocks, feat, size = shards[0].shape
    cols = len(shards)
    args = [weight, *shards, side] + ([] if mask is None else [mask])
    return pl.pallas_call(
        functools.partial(dense_kernel, cols, mask is not None),
        out_shape=[
            jax.ShapeDtypeStruct((blocks, feat, size), BF16),
            jax.ShapeDtypeStruct((cols * feat, side.shape[2]), F32),
        ],
        in_specs=[SMEM] + [VMEM] * len(args),
        out_specs=[VMEM, VMEM],
        scratch_shapes=[pltpu.VMEM((cols, feat, blocks * size), BF16)],
        compiler_params=PARAMS,
        name="dense",
    )(col, *args)


def weight_terms_kernel(me_ref, first_ref, second_ref, keep_ref, send_ref):
    first, second = first_ref[...].T, second_ref[...].T
    even = jnp.bitwise_and(me_ref[0], 1) == 0
    keep_ref[...] = jnp.where(even, second, first)
    send_ref[...] = jnp.where(even, first, second).astype(BF16)


def weight_terms(first, second, me):
    shape = first.shape[::-1]
    return pl.pallas_call(
        weight_terms_kernel,
        out_shape=[jax.ShapeDtypeStruct(shape, F32), jax.ShapeDtypeStruct(shape, BF16)],
        in_specs=[SMEM] + [VMEM] * 2,
        out_specs=[VMEM] * 2,
        compiler_params=PARAMS,
        name="weight_terms",
    )(me, first, second)


def swap(value, mask, axis):
    return lax.ppermute(value, axis, [(i, i ^ mask) for i in range(lax.axis_size(axis))])


def add(a, b):
    return (a.astype(F32) + b.astype(F32)).astype(BF16)


def scatter_group(keep, got, masks, beside):
    left = sorted(masks, reverse=True)
    for mask in masks:
        axis = left.index(mask)
        part = lambda v, i: lax.index_in_dim(v, i, axis, keepdims=False)
        sent = swap(add(part(keep, 1), part(got, 1)), mask, "row")
        keep = add(part(keep, 0), part(got, 0))
        got = sent
        left.remove(mask)
        if beside is not None and mask == masks[0]:
            got, beside = lax.optimization_barrier((got, beside))
    return [keep, got], beside


def scatter(pieces, rows, beside=None):
    masks = [1 << b for b in range(1, rows.bit_length() - 1)]
    lead = (2,) * len(masks)
    done = []
    for g in range(GROUPS):
        keep, got = pieces[2 * g], swap(pieces[2 * g + 1], 1, "row")
        order = masks if g % 2 == 0 else masks[::-1]
        terms, beside = scatter_group(keep.reshape(lead + keep.shape[1:]), got.reshape(lead + got.shape[1:]), order, beside)
        done += terms
    return done, beside


def gather_columns(own, cols):
    if cols == 4:
        far = swap(own, 3, "col")
        return [own, swap(own, 1, "col"), swap(far, 1, "col"), far]
    return [own] + [swap(own, m, "col") for m in range(1, cols)]


def over_chips(value, rows):
    mask = 2
    while mask < rows:
        value = value.astype(BF16)
        value = value.astype(F32) + swap(value, mask, "row").astype(F32)
        mask *= 2
    return value


def per_device(
    node_feats, hidden_act, grad_out, relu_mask, edge_tiles, block_cols, weight_one, weight_two
):
    rows, cols = lax.axis_size("row"), lax.axis_size("col")
    me, col = lax.axis_index("row").astype(jnp.int32), lax.axis_index("col").astype(jnp.int32)
    me_at, col_at = me.reshape(1), col.reshape(1)
    size = edge_tiles.shape[2]
    blocked = lambda v: v.reshape(v.shape[0] // size, size, v.shape[1])
    after = lax.optimization_barrier

    *pieces, mask = spread(edge_tiles, block_cols, blocked(grad_out), me_at, rows, blocked(relu_mask))
    terms, _ = scatter(pieces, rows)
    own, node_feats = after((finish(terms, False), blocked(node_feats)))
    shards = gather_columns(own, cols)
    parts = [node_feats] + [swap(node_feats, rel, "row") for rel in range(2, rows, 2)]
    shards, parts = after((shards, parts))
    delta, second = dense(weight_two, shards, blocked(hidden_act), mask, col_at)
    delta, parts = after((delta, parts))
    shards = gather_columns(delta, cols)
    parts = [v for part in parts for v in (part, swap(part, 1, "row"))]
    agg_feats = aggregate(edge_tiles, block_cols, parts, me_at)
    spread_in, first = dense(weight_one, shards, agg_feats, None, col_at)
    pieces = spread(edge_tiles, block_cols, spread_in, me_at, rows)
    keep, send = weight_terms(first, second, me_at)
    terms, value = scatter(pieces, rows, keep + swap(send, 1, "row").astype(F32))
    out = finish(terms, True)
    value = over_chips(value, rows)
    other = swap(value, 1, "row")
    even = me % 2 == 0
    first_grad, second_grad = jnp.where(even, other, value), jnp.where(even, value, other)
    return out.reshape(-1, out.shape[2]), first_grad, second_grad


def solution(mesh):
    in_specs = (
        P("row", "col"),
        P("row", "col"),
        P("row", "col"),
        P("row", "col"),
        P("row", None, None, None),
        P("row", None),
        P("col", None),
        P("col", None),
    )
    out_specs = (P("row", "col"), P("col", None), P("col", None))
    return jax.shard_map(
        per_device, mesh=mesh, in_specs=in_specs, out_specs=out_specs, check_vma=False
    )
```

```python
import functools

import jax
import jax.numpy as jnp
from jax import lax
from jax.experimental import pallas as pl
from jax.experimental.pallas import tpu as pltpu
from jax.sharding import PartitionSpec as P

VMEM_LIMIT = 48 * 1024 * 1024
GROUPS = 2
COPIES = 4
F32 = jnp.float32
BF16 = jnp.bfloat16
VMEM = pl.BlockSpec(memory_space=pltpu.VMEM)
SMEM = pl.BlockSpec(memory_space=pltpu.SMEM)
PARAMS = pltpu.CompilerParams(vmem_limit_bytes=VMEM_LIMIT)


def tile_copy(tiles_ref, held, sems, i):
    per = held.shape[0] // COPIES
    part = pl.ds(i * per, per)
    return pltpu.make_async_copy(tiles_ref.at[part], held.at[part], sems.at[i])


def over_rows(tiles_ref, held, sems, one_row):
    per = held.shape[0] // COPIES

    def piece(i, carry):
        tile_copy(tiles_ref, held, sems, i).wait()
        for j in range(per):
            one_row(i * per + j)
        return carry

    lax.fori_loop(0, COPIES, piece, 0)


def spread_kernel(first, pieces, cols_ref, me_ref, tiles_ref, *rest):
    vals, rest = rest[:pieces], rest[pieces:]
    if first:
        mask_ref, *rest = rest
        outs, (mask_out, acc, held, sems, left_ref, mask_held) = rest[: 2 * GROUPS], rest[2 * GROUPS :]
        loads = [
            pltpu.make_async_copy(vals[0], left_ref, sems.at[COPIES]),
            pltpu.make_async_copy(mask_ref, mask_held, sems.at[COPIES + 1]),
        ]
        loads[0].start()
    else:
        outs, (acc, held, sems, left_ref) = rest[: 2 * GROUPS], rest[2 * GROUPS :]
    for i in range(COPIES):
        tile_copy(tiles_ref, held, sems, i).start()
    if first:
        loads[1].start()
    acc[...] = jnp.zeros_like(acc)
    per_row, size = held.shape[1], held.shape[3]
    me = me_ref[0]
    if first:
        loads[0].wait()
    else:
        for g in range(pieces):
            count = vals[g].shape[0]
            left_ref[g * count : (g + 1) * count] = vals[g][...]

    def one_row(r):
        left = left_ref[r].astype(F32).T.astype(BF16) if first else left_ref[r]
        for k in range(0, per_row, 2):
            pair = jnp.concatenate([held[r, k], held[r, k + 1]], axis=1)
            both = jnp.dot(left, pair, preferred_element_type=F32)
            for side in range(2):
                acc[cols_ref[r, k + side]] += both[:, side * size : (side + 1) * size]

    over_rows(tiles_ref, held, sems, one_row)
    halves, count = outs[0].shape[:2]
    for g in range(GROUPS):
        for side in range(2):
            for rel in range(halves):
                owner = jnp.bitwise_xor(me, 2 * rel + side)
                start = (owner * GROUPS + g) * count
                outs[2 * g + side][rel] = acc[pl.ds(start, count)].astype(BF16)
    if first:
        loads[1].wait()
        for b in range(mask_held.shape[0]):
            mask_out[b] = mask_held[b].astype(F32).T.astype(BF16)


def spread(edge_tiles, block_cols, vals, me, rows, mask=None):
    blocks, _, size, _ = edge_tiles.shape
    first = mask is not None
    feat = vals[0].shape[2] if first else vals[0].shape[1]
    out = jax.ShapeDtypeStruct((rows // 2, blocks // GROUPS, feat, size), BF16)
    outs = [out] * (2 * GROUPS)
    scratch = [
        pltpu.VMEM((rows * blocks, feat, size), F32),
        pltpu.VMEM(edge_tiles.shape, BF16),
        pltpu.SemaphoreType.DMA((COPIES + 2,)),
    ]
    anywhere = pl.BlockSpec(memory_space=pl.ANY)
    if first:
        outs.append(jax.ShapeDtypeStruct((blocks, feat, size), BF16))
        scratch += [pltpu.VMEM(v.shape, v.dtype) for v in (vals[0], mask)]
        args, place = [vals[0], mask], anywhere
    else:
        scratch.append(pltpu.VMEM((blocks, feat, size), BF16))
        args, place = vals, VMEM
    return pl.pallas_call(
        functools.partial(spread_kernel, first, len(vals)),
        out_shape=outs,
        in_specs=[SMEM, SMEM, anywhere] + [place] * len(args),
        out_specs=[VMEM] * len(outs),
        scratch_shapes=scratch,
        compiler_params=PARAMS,
        cost_estimate=pl.CostEstimate(flops=2 * edge_tiles.size * feat, bytes_accessed=30_000_000, transcendentals=0),
        name="spread",
    )(block_cols, me, edge_tiles, *args)


def aggregate_kernel(cols_ref, me_ref, tiles_ref, *rest):
    parts, (out_ref, held, table, sems) = rest[:-4], rest[-4:]
    blocks, per_row = held.shape[:2]
    loads = []
    for rel, part in enumerate(parts):
        place = table.at[pl.ds(jnp.bitwise_xor(me_ref[0], rel) * blocks, blocks)]
        loads.append(pltpu.make_async_copy(part, place, sems.at[COPIES + rel]))
    for load in loads:
        load.start()
    for i in range(COPIES):
        tile_copy(tiles_ref, held, sems, i).start()
    for load in loads:
        load.wait()

    def one_row(r):
        total = None
        for k in range(0, per_row, 2):
            pair = jnp.concatenate([held[r, k], held[r, k + 1]], axis=1)
            picked = jnp.concatenate([table[cols_ref[r, k]], table[cols_ref[r, k + 1]]], axis=0)
            term = jnp.dot(pair, picked, preferred_element_type=F32)
            total = term if total is None else total + term
        out_ref[r] = total.astype(BF16)

    over_rows(tiles_ref, held, sems, one_row)


def aggregate(edge_tiles, block_cols, parts, me):
    blocks, _, size, _ = edge_tiles.shape
    feat = parts[0].shape[2]
    anywhere = pl.BlockSpec(memory_space=pl.ANY)
    return pl.pallas_call(
        aggregate_kernel,
        out_shape=jax.ShapeDtypeStruct((blocks, size, feat), BF16),
        in_specs=[SMEM, SMEM, anywhere] + [anywhere] * len(parts),
        out_specs=VMEM,
        scratch_shapes=[
            pltpu.VMEM(edge_tiles.shape, BF16),
            pltpu.VMEM((len(parts) * blocks, size, feat), BF16),
            pltpu.SemaphoreType.DMA((COPIES + len(parts),)),
        ],
        compiler_params=PARAMS,
        cost_estimate=pl.CostEstimate(flops=2 * edge_tiles.size * feat, bytes_accessed=30_000_000, transcendentals=0),
        name="aggregate",
    )(block_cols, me, edge_tiles, *parts)


def finish_kernel(last, *refs):
    parts, out_ref = refs[:-1], refs[-1]
    count = parts[0].shape[0]
    for g in range(len(parts) // 2):
        for b in range(count):
            total = parts[2 * g][b].astype(F32) + parts[2 * g + 1][b].astype(F32)
            out_ref[g * count + b] = (total.T if last else total).astype(BF16)


def finish(parts, last):
    count, feat, size = parts[0].shape
    return pl.pallas_call(
        functools.partial(finish_kernel, last),
        out_shape=jax.ShapeDtypeStruct((count * len(parts) // 2,) + ((size, feat) if last else (feat, size)), BF16),
        in_specs=[VMEM] * len(parts),
        out_specs=VMEM,
        compiler_params=PARAMS,
        cost_estimate=pl.CostEstimate(flops=0, bytes_accessed=1_000_000_000 if last else 1, transcendentals=0),
        name="finish",
    )(*parts)


def dense_kernel(cols, masked, col_ref, weight_ref, *rest):
    shards, rest = rest[:cols], rest[cols:]
    side_ref, rest = rest[0], rest[1:]
    if masked:
        mask_ref, rest = rest[0], rest[1:]
    out_ref, grad_ref, whole_ref = rest
    blocks, feat, size = shards[0].shape
    for m in range(cols):
        place = jnp.bitwise_xor(col_ref[0], m)
        for b in range(blocks):
            whole_ref[place, :, b * size : (b + 1) * size] = shards[m][b]
    whole = jnp.concatenate([whole_ref[q] for q in range(cols)], axis=0)
    res = jnp.dot(weight_ref[...], whole, preferred_element_type=F32)
    for b in range(blocks):
        part = res[:, b * size : (b + 1) * size]
        out_ref[b] = (part * mask_ref[b].astype(F32) if masked else part).astype(BF16)
    side = jnp.concatenate([side_ref[b] for b in range(blocks)], axis=0)
    grad_ref[...] = jnp.dot(whole, side, preferred_element_type=F32)


def dense(weight, shards, side, mask, col):
    blocks, feat, size = shards[0].shape
    cols = len(shards)
    args = [weight, *shards, side] + ([] if mask is None else [mask])
    return pl.pallas_call(
        functools.partial(dense_kernel, cols, mask is not None),
        out_shape=[
            jax.ShapeDtypeStruct((blocks, feat, size), BF16),
            jax.ShapeDtypeStruct((cols * feat, side.shape[2]), F32),
        ],
        in_specs=[SMEM] + [VMEM] * len(args),
        out_specs=[VMEM, VMEM],
        scratch_shapes=[pltpu.VMEM((cols, feat, blocks * size), BF16)],
        compiler_params=PARAMS,
        name="dense",
    )(col, *args)


def weight_terms_kernel(me_ref, *refs):
    firsts, seconds, (keep_ref, send_ref) = refs[:GROUPS], refs[GROUPS : 2 * GROUPS], refs[2 * GROUPS :]
    first, second = sum(r[...] for r in firsts).T, sum(r[...] for r in seconds).T
    even = jnp.bitwise_and(me_ref[0], 1) == 0
    keep_ref[...] = jnp.where(even, second, first)
    send_ref[...] = jnp.where(even, first, second).astype(BF16)


def weight_terms(firsts, seconds, me):
    shape = firsts[0].shape[::-1]
    return pl.pallas_call(
        weight_terms_kernel,
        out_shape=[jax.ShapeDtypeStruct(shape, F32), jax.ShapeDtypeStruct(shape, BF16)],
        in_specs=[SMEM] + [VMEM] * (2 * GROUPS),
        out_specs=[VMEM] * 2,
        compiler_params=PARAMS,
        name="weight_terms",
    )(me, *firsts, *seconds)


def swap(value, mask, axis):
    return lax.ppermute(value, axis, [(i, i ^ mask) for i in range(lax.axis_size(axis))])


def add(a, b):
    return (a.astype(F32) + b.astype(F32)).astype(BF16)


def scatter_group(keep, got, masks, beside):
    left = sorted(masks, reverse=True)
    for mask in masks:
        axis = left.index(mask)
        part = lambda v, i: lax.index_in_dim(v, i, axis, keepdims=False)
        sent = swap(add(part(keep, 1), part(got, 1)), mask, "row")
        keep = add(part(keep, 0), part(got, 0))
        got = sent
        left.remove(mask)
        if beside is not None and mask == masks[0]:
            got, beside = lax.optimization_barrier((got, beside))
    return [keep, got], beside


def scatter(pieces, rows, beside=None):
    masks = [1 << b for b in range(1, rows.bit_length() - 1)]
    lead = (2,) * len(masks)
    done = []
    for g in range(GROUPS):
        keep, got = pieces[2 * g], swap(pieces[2 * g + 1], 1, "row")
        order = masks if g % 2 == 0 else masks[::-1]
        terms, beside = scatter_group(keep.reshape(lead + keep.shape[1:]), got.reshape(lead + got.shape[1:]), order, beside)
        done.append(terms)
    return done, beside


def gather_columns(own, cols):
    if cols == 4:
        near, far = lax.optimization_barrier((swap(own, 1, "col"), swap(own, 3, "col")))
        return [own, near, swap(far, 1, "col"), far]
    return [own] + [swap(own, m, "col") for m in range(1, cols)]


def over_chips(value, masks):
    for mask in masks:
        value = value.astype(BF16)
        value = value.astype(F32) + swap(value, mask, "row").astype(F32)
    return value


def per_device(
    node_feats, hidden_act, grad_out, relu_mask, edge_tiles, block_cols, weight_one, weight_two
):
    rows, cols = lax.axis_size("row"), lax.axis_size("col")
    me, col = lax.axis_index("row").astype(jnp.int32), lax.axis_index("col").astype(jnp.int32)
    me_at, col_at = me.reshape(1), col.reshape(1)
    size = edge_tiles.shape[2]
    per = edge_tiles.shape[0] // GROUPS
    chips = [1 << b for b in range(1, rows.bit_length() - 1)]
    cut = lambda v, g: v[g * per : (g + 1) * per]
    blocked = lambda v: v.reshape(v.shape[0] // size, size, v.shape[1])
    after = lax.optimization_barrier

    parts = {0: blocked(node_feats)}
    for rel in chips:
        parts[rel] = swap(parts[0], rel, "row")
    *pieces, mask = spread(edge_tiles, block_cols, [blocked(grad_out)], me_at, rows, blocked(relu_mask))
    pieces, parts = after((pieces, parts))
    terms, parts = scatter(pieces, rows, parts)
    for rel in [0] + chips:
        parts[rel + 1] = swap(parts[rel], 1, "row")
    hidden = blocked(hidden_act)
    owns = [finish(terms[g], False) for g in range(GROUPS)]
    owns, parts = after((owns, parts))
    for rel in range(2, rows, 2):
        top = 1 << (rel.bit_length() - 1)
        if rel not in parts:
            parts[rel] = swap(parts[rel - top], top, "row")
    deltas, seconds, inputs, firsts = [], [], [], []
    for g in range(GROUPS):
        delta, grad = dense(weight_two, gather_columns(owns[g], cols), cut(hidden, g), cut(mask, g), col_at)
        deltas.append(delta)
        seconds.append(grad)
    deltas[-1], parts = after((deltas[-1], parts))
    for rel in range(1, rows, 2):
        if rel not in parts:
            parts[rel] = swap(parts[rel - 1], 1, "row")
    agg_feats = aggregate(edge_tiles, block_cols, [parts[rel] for rel in range(rows)], me_at)
    for g in range(GROUPS):
        out, grad = dense(weight_one, gather_columns(deltas[g], cols), cut(agg_feats, g), None, col_at)
        inputs.append(out)
        firsts.append(grad)
    pieces = spread(edge_tiles, block_cols, inputs, me_at, rows)
    keep, send = weight_terms(firsts, seconds, me_at)
    value = over_chips(keep + swap(send, 1, "row").astype(F32), chips[:1])
    terms, value = scatter(pieces, rows, value)
    terms, value = after((terms, over_chips(value, chips[1:])))
    out = finish([t for pair in terms for t in pair], True)
    other = swap(value, 1, "row")
    even = me % 2 == 0
    first_grad, second_grad = jnp.where(even, other, value), jnp.where(even, value, other)
    return out.reshape(-1, out.shape[2]), first_grad, second_grad


def solution(mesh):
    in_specs = (
        P("row", "col"),
        P("row", "col"),
        P("row", "col"),
        P("row", "col"),
        P("row", None, None, None),
        P("row", None),
        P("col", None),
        P("col", None),
    )
    out_specs = (P("row", "col"), P("col", None), P("col", None))
    return jax.shard_map(
        per_device, mesh=mesh, in_specs=in_specs, out_specs=out_specs, check_vma=False
    )
```

```python
import functools

import jax
import jax.numpy as jnp
from jax import lax
from jax.experimental import pallas as pl
from jax.experimental.pallas import tpu as pltpu
from jax.sharding import PartitionSpec as P

VMEM_LIMIT = 48 * 1024 * 1024
GROUPS = 2
COPIES = 4
F32 = jnp.float32
BF16 = jnp.bfloat16
VMEM = pl.BlockSpec(memory_space=pltpu.VMEM)
SMEM = pl.BlockSpec(memory_space=pltpu.SMEM)
PARAMS = pltpu.CompilerParams(vmem_limit_bytes=VMEM_LIMIT)


def tile_copy(tiles_ref, held, sems, i):
    per = held.shape[0] // COPIES
    part = pl.ds(i * per, per)
    return pltpu.make_async_copy(tiles_ref.at[part], held.at[part], sems.at[i])


def over_rows(tiles_ref, held, sems, one_row):
    per = held.shape[0] // COPIES

    def piece(i, carry):
        tile_copy(tiles_ref, held, sems, i).wait()
        for j in range(per):
            one_row(i * per + j)
        return carry

    lax.fori_loop(0, COPIES, piece, 0)


def spread_kernel(first, pieces, cols_ref, me_ref, tiles_ref, *rest):
    vals, rest = rest[:pieces], rest[pieces:]
    if first:
        mask_ref, *rest = rest
        outs, (mask_out, acc, held, sems, left_ref, mask_held) = rest[: 2 * GROUPS], rest[2 * GROUPS :]
        loads = [
            pltpu.make_async_copy(vals[0], left_ref, sems.at[COPIES]),
            pltpu.make_async_copy(mask_ref, mask_held, sems.at[COPIES + 1]),
        ]
        loads[0].start()
    else:
        outs, (acc, held, sems, left_ref) = rest[: 2 * GROUPS], rest[2 * GROUPS :]
    for i in range(COPIES):
        tile_copy(tiles_ref, held, sems, i).start()
    if first:
        loads[1].start()
    acc[...] = jnp.zeros_like(acc)
    per_row, size = held.shape[1], held.shape[3]
    me = me_ref[0]
    if first:
        loads[0].wait()
    else:
        for g in range(pieces):
            count = vals[g].shape[0]
            left_ref[g * count : (g + 1) * count] = vals[g][...]

    def one_row(r):
        left = left_ref[r].astype(F32).T.astype(BF16) if first else left_ref[r]
        for k in range(0, per_row, 2):
            pair = jnp.concatenate([held[r, k], held[r, k + 1]], axis=1)
            both = jnp.dot(left, pair, preferred_element_type=F32)
            for side in range(2):
                acc[cols_ref[r, k + side]] += both[:, side * size : (side + 1) * size]

    over_rows(tiles_ref, held, sems, one_row)
    halves, count = outs[0].shape[:2]
    for g in range(GROUPS):
        for side in range(2):
            for rel in range(halves):
                owner = jnp.bitwise_xor(me, 2 * rel + side)
                start = (owner * GROUPS + g) * count
                outs[2 * g + side][rel] = acc[pl.ds(start, count)].astype(BF16)
    if first:
        loads[1].wait()
        for b in range(mask_held.shape[0]):
            mask_out[b] = mask_held[b].astype(F32).T.astype(BF16)


def spread(edge_tiles, block_cols, vals, me, rows, mask=None):
    blocks, _, size, _ = edge_tiles.shape
    first = mask is not None
    feat = vals[0].shape[2] if first else vals[0].shape[1]
    out = jax.ShapeDtypeStruct((rows // 2, blocks // GROUPS, feat, size), BF16)
    outs = [out] * (2 * GROUPS)
    scratch = [
        pltpu.VMEM((rows * blocks, feat, size), F32),
        pltpu.VMEM(edge_tiles.shape, BF16),
        pltpu.SemaphoreType.DMA((COPIES + 2,)),
    ]
    anywhere = pl.BlockSpec(memory_space=pl.ANY)
    if first:
        outs.append(jax.ShapeDtypeStruct((blocks, feat, size), BF16))
        scratch += [pltpu.VMEM(v.shape, v.dtype) for v in (vals[0], mask)]
        args, place = [vals[0], mask], anywhere
    else:
        scratch.append(pltpu.VMEM((blocks, feat, size), BF16))
        args, place = vals, VMEM
    return pl.pallas_call(
        functools.partial(spread_kernel, first, len(vals)),
        out_shape=outs,
        in_specs=[SMEM, SMEM, anywhere] + [place] * len(args),
        out_specs=[VMEM] * len(outs),
        scratch_shapes=scratch,
        compiler_params=PARAMS,
        cost_estimate=pl.CostEstimate(flops=2 * edge_tiles.size * feat, bytes_accessed=30_000_000, transcendentals=0),
        name="spread",
    )(block_cols, me, edge_tiles, *args)


def aggregate_kernel(cols_ref, me_ref, tiles_ref, *rest):
    parts, (out_ref, held, table, sems) = rest[:-4], rest[-4:]
    blocks, per_row = held.shape[:2]
    loads = []
    for rel, part in enumerate(parts):
        place = table.at[pl.ds(jnp.bitwise_xor(me_ref[0], rel) * blocks, blocks)]
        loads.append(pltpu.make_async_copy(part, place, sems.at[COPIES + rel]))
    for load in loads:
        load.start()
    for i in range(COPIES):
        tile_copy(tiles_ref, held, sems, i).start()
    for load in loads:
        load.wait()

    def one_row(r):
        total = None
        for k in range(0, per_row, 2):
            pair = jnp.concatenate([held[r, k], held[r, k + 1]], axis=1)
            picked = jnp.concatenate([table[cols_ref[r, k]], table[cols_ref[r, k + 1]]], axis=0)
            term = jnp.dot(pair, picked, preferred_element_type=F32)
            total = term if total is None else total + term
        out_ref[r] = total.astype(BF16)

    over_rows(tiles_ref, held, sems, one_row)


def aggregate(edge_tiles, block_cols, parts, me):
    blocks, _, size, _ = edge_tiles.shape
    feat = parts[0].shape[2]
    anywhere = pl.BlockSpec(memory_space=pl.ANY)
    return pl.pallas_call(
        aggregate_kernel,
        out_shape=jax.ShapeDtypeStruct((blocks, size, feat), BF16),
        in_specs=[SMEM, SMEM, anywhere] + [anywhere] * len(parts),
        out_specs=VMEM,
        scratch_shapes=[
            pltpu.VMEM(edge_tiles.shape, BF16),
            pltpu.VMEM((len(parts) * blocks, size, feat), BF16),
            pltpu.SemaphoreType.DMA((COPIES + len(parts),)),
        ],
        compiler_params=PARAMS,
        cost_estimate=pl.CostEstimate(flops=2 * edge_tiles.size * feat, bytes_accessed=30_000_000, transcendentals=0),
        name="aggregate",
    )(block_cols, me, edge_tiles, *parts)


def finish_kernel(last, *refs):
    parts, out_ref = refs[:-1], refs[-1]
    count = parts[0].shape[0]
    for g in range(len(parts) // 2):
        for b in range(count):
            total = parts[2 * g][b].astype(F32) + parts[2 * g + 1][b].astype(F32)
            out_ref[g * count + b] = (total.T if last else total).astype(BF16)


def finish(parts, last):
    count, feat, size = parts[0].shape
    return pl.pallas_call(
        functools.partial(finish_kernel, last),
        out_shape=jax.ShapeDtypeStruct((count * len(parts) // 2,) + ((size, feat) if last else (feat, size)), BF16),
        in_specs=[VMEM] * len(parts),
        out_specs=VMEM,
        compiler_params=PARAMS,
        cost_estimate=pl.CostEstimate(flops=0, bytes_accessed=1_000_000_000 if last else 1, transcendentals=0),
        name="finish",
    )(*parts)


def dense_kernel(cols, masked, pieces, col_ref, weight_ref, *rest):
    shards, rest = rest[:cols], rest[cols:]
    side_ref, rest = rest[0], rest[1:]
    if masked:
        mask_ref, rest = rest[0], rest[1:]
    outs, (grad_ref, whole_ref) = rest[:pieces], rest[pieces:]
    blocks, feat, size = shards[0].shape
    for m in range(cols):
        place = jnp.bitwise_xor(col_ref[0], m)
        for b in range(blocks):
            whole_ref[place, :, b * size : (b + 1) * size] = shards[m][b]
    per = blocks // pieces
    total = None
    for i, out in enumerate(outs):
        part = slice(i * per * size, (i + 1) * per * size)
        whole = jnp.concatenate([whole_ref[q, :, part] for q in range(cols)], axis=0)
        res = jnp.dot(weight_ref[...], whole, preferred_element_type=F32)
        for b in range(per):
            block = res[:, b * size : (b + 1) * size]
            out[b] = (block * mask_ref[i * per + b].astype(F32) if masked else block).astype(BF16)
        side = jnp.concatenate([side_ref[i * per + b] for b in range(per)], axis=0)
        term = jnp.dot(whole, side, preferred_element_type=F32)
        total = term if total is None else total + term
    grad_ref[...] = total


def dense(weight, shards, side, mask, col, pieces):
    blocks, feat, size = shards[0].shape
    cols = len(shards)
    args = [weight, *shards, side] + ([] if mask is None else [mask])
    return pl.pallas_call(
        functools.partial(dense_kernel, cols, mask is not None, pieces),
        out_shape=[jax.ShapeDtypeStruct((blocks // pieces, feat, size), BF16)] * pieces
        + [jax.ShapeDtypeStruct((cols * feat, side.shape[2]), F32)],
        in_specs=[SMEM] + [VMEM] * len(args),
        out_specs=[VMEM] * (pieces + 1),
        scratch_shapes=[pltpu.VMEM((cols, feat, blocks * size), BF16)],
        compiler_params=PARAMS,
        name="dense",
    )(col, *args)


def weight_terms_kernel(me_ref, second_ref, *refs):
    firsts, (keep_ref, send_ref) = refs[:-2], refs[-2:]
    first, second = sum(r[...] for r in firsts).T, second_ref[...].T
    even = jnp.bitwise_and(me_ref[0], 1) == 0
    keep_ref[...] = jnp.where(even, second, first)
    send_ref[...] = jnp.where(even, first, second).astype(BF16)


def weight_terms(firsts, second, me):
    shape = second.shape[::-1]
    return pl.pallas_call(
        weight_terms_kernel,
        out_shape=[jax.ShapeDtypeStruct(shape, F32), jax.ShapeDtypeStruct(shape, BF16)],
        in_specs=[SMEM] + [VMEM] * (1 + len(firsts)),
        out_specs=[VMEM] * 2,
        compiler_params=PARAMS,
        name="weight_terms",
    )(me, second, *firsts)


def swap(value, mask, axis):
    return lax.ppermute(value, axis, [(i, i ^ mask) for i in range(lax.axis_size(axis))])


def add(a, b):
    return (a.astype(F32) + b.astype(F32)).astype(BF16)


def scatter_group(keep, got, masks, beside):
    left = sorted(masks, reverse=True)
    for mask in masks:
        axis = left.index(mask)
        part = lambda v, i: lax.index_in_dim(v, i, axis, keepdims=False)
        sent = swap(add(part(keep, 1), part(got, 1)), mask, "row")
        keep = add(part(keep, 0), part(got, 0))
        got = sent
        left.remove(mask)
        if beside is not None and mask == masks[0]:
            got, beside = lax.optimization_barrier((got, beside))
    return [keep, got], beside


def scatter(pieces, rows, beside=None):
    masks = [1 << b for b in range(1, rows.bit_length() - 1)]
    lead = (2,) * len(masks)
    done = []
    for g in range(GROUPS):
        keep, got = pieces[2 * g], swap(pieces[2 * g + 1], 1, "row")
        order = masks if g % 2 == 0 else masks[::-1]
        terms, beside = scatter_group(keep.reshape(lead + keep.shape[1:]), got.reshape(lead + got.shape[1:]), order, beside)
        done.append(terms)
    return done, beside


def gather_columns(own, cols, beside=()):
    if cols == 4:
        near, far, beside = lax.optimization_barrier((swap(own, 1, "col"), swap(own, 3, "col"), beside))
        return [own, near, swap(far, 1, "col"), far], beside
    return [own] + [swap(own, m, "col") for m in range(1, cols)], beside


def over_chips(value, masks):
    for mask in masks:
        value = value.astype(BF16)
        value = value.astype(F32) + swap(value, mask, "row").astype(F32)
    return value


def per_device(
    node_feats, hidden_act, grad_out, relu_mask, edge_tiles, block_cols, weight_one, weight_two
):
    rows, cols = lax.axis_size("row"), lax.axis_size("col")
    me, col = lax.axis_index("row").astype(jnp.int32), lax.axis_index("col").astype(jnp.int32)
    me_at, col_at = me.reshape(1), col.reshape(1)
    size = edge_tiles.shape[2]
    per = edge_tiles.shape[0] // GROUPS
    chips = [1 << b for b in range(1, rows.bit_length() - 1)]
    cut = lambda v, g: v[g * per : (g + 1) * per]
    blocked = lambda v: v.reshape(v.shape[0] // size, size, v.shape[1])
    after = lax.optimization_barrier

    *pieces, mask = spread(edge_tiles, block_cols, [blocked(grad_out)], me_at, rows, blocked(relu_mask))
    terms, _ = scatter(pieces, rows)
    own, node_feats = after((finish([t for pair in terms for t in pair], False), blocked(node_feats)))
    shards, _ = gather_columns(own, cols)
    parts = [node_feats] + [swap(node_feats, rel, "row") for rel in range(2, rows, 2)]
    parts = [v for part in parts for v in (part, swap(part, 1, "row"))]
    shards, parts = after((shards, parts))
    *deltas, second = dense(weight_two, shards, blocked(hidden_act), mask, col_at, GROUPS)
    deltas[0], parts = after((deltas[0], parts))
    agg_feats = aggregate(edge_tiles, block_cols, parts, me_at)
    inputs, firsts = [], []
    for g in range(GROUPS):
        shards, beside = gather_columns(deltas[g], cols, agg_feats if g == 0 else ())
        agg_feats = beside if g == 0 else agg_feats
        out, grad = dense(weight_one, shards, cut(agg_feats, g), None, col_at, 1)
        inputs.append(out)
        firsts.append(grad)
    pieces = spread(edge_tiles, block_cols, inputs, me_at, rows)
    keep, send = weight_terms(firsts, second, me_at)
    value = over_chips(keep + swap(send, 1, "row").astype(F32), chips[-1:])
    terms, value = scatter(pieces, rows, value)
    terms, value = after((terms, over_chips(value, chips[:-1])))
    out = finish([t for pair in terms for t in pair], True)
    other = swap(value, 1, "row")
    even = me % 2 == 0
    first_grad, second_grad = jnp.where(even, other, value), jnp.where(even, value, other)
    return out.reshape(-1, out.shape[2]), first_grad, second_grad


def solution(mesh):
    in_specs = (
        P("row", "col"),
        P("row", "col"),
        P("row", "col"),
        P("row", "col"),
        P("row", None, None, None),
        P("row", None),
        P("col", None),
        P("col", None),
    )
    out_specs = (P("row", "col"), P("col", None), P("col", None))
    return jax.shard_map(
        per_device, mesh=mesh, in_specs=in_specs, out_specs=out_specs, check_vma=False
    )
```

```python
import functools

import jax
import jax.numpy as jnp
from jax import lax
from jax.experimental import pallas as pl
from jax.experimental.pallas import tpu as pltpu
from jax.sharding import PartitionSpec as P

VMEM_LIMIT = 48 * 1024 * 1024
GROUPS = 2
COPIES = 4
F32 = jnp.float32
BF16 = jnp.bfloat16
VMEM = pl.BlockSpec(memory_space=pltpu.VMEM)
SMEM = pl.BlockSpec(memory_space=pltpu.SMEM)
PARAMS = pltpu.CompilerParams(vmem_limit_bytes=VMEM_LIMIT)


def tile_copy(tiles_ref, held, sems, i):
    per = held.shape[0] // COPIES
    part = pl.ds(i * per, per)
    return pltpu.make_async_copy(tiles_ref.at[part], held.at[part], sems.at[i])


def over_rows(tiles_ref, held, sems, one_row):
    per = held.shape[0] // COPIES

    def piece(i, carry):
        tile_copy(tiles_ref, held, sems, i).wait()
        for j in range(per):
            one_row(i * per + j)
        return carry

    lax.fori_loop(0, COPIES, piece, 0)


def spread_kernel(first, pieces, cols_ref, me_ref, tiles_ref, *rest):
    vals, rest = rest[:pieces], rest[pieces:]
    if first:
        mask_ref, *rest = rest
        outs, (mask_out, acc, held, sems, left_ref, mask_held) = rest[: 2 * GROUPS], rest[2 * GROUPS :]
        loads = [
            pltpu.make_async_copy(vals[0], left_ref, sems.at[COPIES]),
            pltpu.make_async_copy(mask_ref, mask_held, sems.at[COPIES + 1]),
        ]
        loads[0].start()
    else:
        outs, (acc, held, sems, left_ref) = rest[: 2 * GROUPS], rest[2 * GROUPS :]
    for i in range(COPIES):
        tile_copy(tiles_ref, held, sems, i).start()
    if first:
        loads[1].start()
    acc[...] = jnp.zeros_like(acc)
    per_row, size = held.shape[1], held.shape[3]
    me = me_ref[0]
    if first:
        loads[0].wait()
    else:
        for g in range(pieces):
            count = vals[g].shape[0]
            left_ref[g * count : (g + 1) * count] = vals[g][...]

    def one_row(r):
        left = left_ref[r].astype(F32).T.astype(BF16) if first else left_ref[r]
        for k in range(0, per_row, 2):
            pair = jnp.concatenate([held[r, k], held[r, k + 1]], axis=1)
            both = jnp.dot(left, pair, preferred_element_type=F32)
            for side in range(2):
                acc[cols_ref[r, k + side]] += both[:, side * size : (side + 1) * size]

    over_rows(tiles_ref, held, sems, one_row)
    halves, count = outs[0].shape[:2]
    for g in range(GROUPS):
        for side in range(2):
            for rel in range(halves):
                owner = jnp.bitwise_xor(me, 2 * rel + side)
                start = (owner * GROUPS + g) * count
                outs[2 * g + side][rel] = acc[pl.ds(start, count)].astype(BF16)
    if first:
        loads[1].wait()
        for b in range(mask_held.shape[0]):
            mask_out[b] = mask_held[b].astype(F32).T.astype(BF16)


def spread(edge_tiles, block_cols, vals, me, rows, mask=None):
    blocks, _, size, _ = edge_tiles.shape
    first = mask is not None
    feat = vals[0].shape[2] if first else vals[0].shape[1]
    out = jax.ShapeDtypeStruct((rows // 2, blocks // GROUPS, feat, size), BF16)
    outs = [out] * (2 * GROUPS)
    scratch = [
        pltpu.VMEM((rows * blocks, feat, size), F32),
        pltpu.VMEM(edge_tiles.shape, BF16),
        pltpu.SemaphoreType.DMA((COPIES + 2,)),
    ]
    anywhere = pl.BlockSpec(memory_space=pl.ANY)
    if first:
        outs.append(jax.ShapeDtypeStruct((blocks, feat, size), BF16))
        scratch += [pltpu.VMEM(v.shape, v.dtype) for v in (vals[0], mask)]
        args, place = [vals[0], mask], anywhere
    else:
        scratch.append(pltpu.VMEM((blocks, feat, size), BF16))
        args, place = vals, VMEM
    return pl.pallas_call(
        functools.partial(spread_kernel, first, len(vals)),
        out_shape=outs,
        in_specs=[SMEM, SMEM, anywhere] + [place] * len(args),
        out_specs=[VMEM] * len(outs),
        scratch_shapes=scratch,
        compiler_params=PARAMS,
        cost_estimate=pl.CostEstimate(flops=2 * edge_tiles.size * feat, bytes_accessed=30_000_000, transcendentals=0),
        name="spread",
    )(block_cols, me, edge_tiles, *args)


def aggregate_kernel(cols_ref, me_ref, tiles_ref, *rest):
    parts, (out_ref, held, table, sems) = rest[:-5], rest[-4:]
    blocks, per_row = held.shape[:2]
    loads = []
    for rel, part in enumerate(parts):
        place = table.at[pl.ds(jnp.bitwise_xor(me_ref[0], rel) * blocks, blocks)]
        loads.append(pltpu.make_async_copy(part, place, sems.at[COPIES + rel]))
    for load in loads:
        load.start()
    for i in range(COPIES):
        tile_copy(tiles_ref, held, sems, i).start()
    for load in loads:
        load.wait()

    def one_row(r):
        total = None
        for k in range(0, per_row, 2):
            pair = jnp.concatenate([held[r, k], held[r, k + 1]], axis=1)
            picked = jnp.concatenate([table[cols_ref[r, k]], table[cols_ref[r, k + 1]]], axis=0)
            term = jnp.dot(pair, picked, preferred_element_type=F32)
            total = term if total is None else total + term
        out_ref[r] = total.astype(BF16)

    over_rows(tiles_ref, held, sems, one_row)


def aggregate(edge_tiles, block_cols, parts, me, order):
    blocks, _, size, _ = edge_tiles.shape
    feat = parts[0].shape[2]
    anywhere = pl.BlockSpec(memory_space=pl.ANY)
    return pl.pallas_call(
        aggregate_kernel,
        out_shape=jax.ShapeDtypeStruct((blocks, size, feat), BF16),
        in_specs=[SMEM, SMEM, anywhere] + [anywhere] * (len(parts) + 1),
        out_specs=VMEM,
        scratch_shapes=[
            pltpu.VMEM(edge_tiles.shape, BF16),
            pltpu.VMEM((len(parts) * blocks, size, feat), BF16),
            pltpu.SemaphoreType.DMA((COPIES + len(parts),)),
        ],
        compiler_params=PARAMS,
        cost_estimate=pl.CostEstimate(flops=2 * edge_tiles.size * feat, bytes_accessed=30_000_000, transcendentals=0),
        name="aggregate",
    )(block_cols, me, edge_tiles, *parts, order)


def finish_kernel(last, *refs):
    parts, (out_ref, *groups) = refs[: 2 * GROUPS], refs[2 * GROUPS :]
    count = parts[0].shape[0]
    for g in range(GROUPS):
        for b in range(count):
            total = parts[2 * g][b].astype(F32) + parts[2 * g + 1][b].astype(F32)
            total = (total.T if last else total).astype(BF16)
            out_ref[g * count + b] = total
            if not last:
                groups[g][b] = total


def finish(parts, last):
    count, feat, size = parts[0].shape
    shape = (size, feat) if last else (feat, size)
    outs = [jax.ShapeDtypeStruct((count * GROUPS,) + shape, BF16)]
    if not last:
        outs += [jax.ShapeDtypeStruct((count,) + shape, BF16)] * GROUPS
    return pl.pallas_call(
        functools.partial(finish_kernel, last),
        out_shape=outs,
        in_specs=[VMEM] * len(parts),
        out_specs=[VMEM] * len(outs),
        compiler_params=PARAMS,
        cost_estimate=pl.CostEstimate(flops=0, bytes_accessed=1_000_000_000 if last else 1, transcendentals=0),
        name="finish",
    )(*parts)


def dense_kernel(cols, start, masked, col_ref, weight_ref, *rest):
    shards, rest = rest[:cols], rest[cols:]
    side_ref, rest = rest[0], rest[1:]
    if masked:
        mask_ref, rest = rest[0], rest[1:]
    out_ref, grad_ref, whole_ref = rest
    blocks, feat, size = out_ref.shape
    at = lambda ref, b: ref[b + start] if ref.shape[0] > blocks else ref[b]
    for m in range(cols):
        place = jnp.bitwise_xor(col_ref[0], m)
        for b in range(blocks):
            whole_ref[place, :, b * size : (b + 1) * size] = at(shards[m], b)
    whole = jnp.concatenate([whole_ref[q] for q in range(cols)], axis=0)
    res = jnp.dot(weight_ref[...], whole, preferred_element_type=F32)
    for b in range(blocks):
        block = res[:, b * size : (b + 1) * size]
        out_ref[b] = (block * at(mask_ref, b).astype(F32) if masked else block).astype(BF16)
    side = jnp.concatenate([at(side_ref, b) for b in range(blocks)], axis=0)
    grad_ref[...] = jnp.dot(whole, side, preferred_element_type=F32)


def dense(weight, shards, side, mask, col, g):
    _, feat, size = shards[0].shape
    cols, blocks = len(shards), side.shape[0] // GROUPS
    args = [weight, *shards, side] + ([] if mask is None else [mask])
    return pl.pallas_call(
        functools.partial(dense_kernel, cols, g * blocks, mask is not None),
        out_shape=[
            jax.ShapeDtypeStruct((blocks, feat, size), BF16),
            jax.ShapeDtypeStruct((cols * feat, side.shape[2]), F32),
        ],
        in_specs=[SMEM] + [VMEM] * len(args),
        out_specs=[VMEM, VMEM],
        scratch_shapes=[pltpu.VMEM((cols, feat, blocks * size), BF16)],
        compiler_params=PARAMS,
        name="dense",
    )(col, *args)


def weight_terms_kernel(me_ref, *refs):
    firsts, seconds, (keep_ref, send_ref) = refs[:GROUPS], refs[GROUPS : 2 * GROUPS], refs[2 * GROUPS :]
    first, second = sum(r[...] for r in firsts).T, sum(r[...] for r in seconds).T
    even = jnp.bitwise_and(me_ref[0], 1) == 0
    keep_ref[...] = jnp.where(even, second, first)
    send_ref[...] = jnp.where(even, first, second).astype(BF16)


def weight_terms(firsts, seconds, me):
    shape = firsts[0].shape[::-1]
    return pl.pallas_call(
        weight_terms_kernel,
        out_shape=[jax.ShapeDtypeStruct(shape, F32), jax.ShapeDtypeStruct(shape, BF16)],
        in_specs=[SMEM] + [VMEM] * (2 * GROUPS),
        out_specs=[VMEM] * 2,
        compiler_params=PARAMS,
        name="weight_terms",
    )(me, *firsts, *seconds)


def swap(value, mask, axis):
    return lax.ppermute(value, axis, [(i, i ^ mask) for i in range(lax.axis_size(axis))])


def add(a, b):
    return (a.astype(F32) + b.astype(F32)).astype(BF16)


def scatter_group(keep, got, masks, beside):
    left = sorted(masks, reverse=True)
    for mask in masks:
        axis = left.index(mask)
        part = lambda v, i: lax.index_in_dim(v, i, axis, keepdims=False)
        sent = swap(add(part(keep, 1), part(got, 1)), mask, "row")
        keep = add(part(keep, 0), part(got, 0))
        got = sent
        left.remove(mask)
        if beside is not None and mask == masks[0]:
            got, beside = lax.optimization_barrier((got, beside))
    return [keep, got], beside


def scatter(pieces, rows, beside=None):
    masks = [1 << b for b in range(1, rows.bit_length() - 1)]
    lead = (2,) * len(masks)
    done = []
    for g in range(GROUPS):
        keep, got = pieces[2 * g], swap(pieces[2 * g + 1], 1, "row")
        order = masks if g % 2 == 0 else masks[::-1]
        terms, beside = scatter_group(keep.reshape(lead + keep.shape[1:]), got.reshape(lead + got.shape[1:]), order, beside)
        done.append(terms)
    return done, beside


def hop(shard, m):
    return swap(shard, m, "col")


def over_chips(value, masks):
    for mask in masks:
        value = value.astype(BF16)
        value = value.astype(F32) + swap(value, mask, "row").astype(F32)
    return value


def per_device(
    node_feats, hidden_act, grad_out, relu_mask, edge_tiles, block_cols, weight_one, weight_two
):
    rows, cols = lax.axis_size("row"), lax.axis_size("col")
    me, col = lax.axis_index("row").astype(jnp.int32), lax.axis_index("col").astype(jnp.int32)
    me_at, col_at = me.reshape(1), col.reshape(1)
    size = edge_tiles.shape[2]
    per = edge_tiles.shape[0] // GROUPS
    chips = [1 << b for b in range(1, rows.bit_length() - 1)]
    cut = lambda v, g: v[g * per : (g + 1) * per]
    blocked = lambda v: v.reshape(v.shape[0] // size, size, v.shape[1])
    after = lax.optimization_barrier

    *pieces, mask = spread(edge_tiles, block_cols, [blocked(grad_out)], me_at, rows, blocked(relu_mask))
    terms, node_feats = scatter(pieces, rows, blocked(node_feats))
    hidden = blocked(hidden_act)
    parts = {0: node_feats, 1: swap(node_feats, 1, "row")}
    own, *groups = finish([t for pair in terms for t in pair], False)
    own, parts = after((own, parts))
    for rel in chips:
        parts[rel] = swap(parts[0], rel, "row")
    if cols == 4:
        near, far = hop(own, 1), [hop(group, 3) for group in groups]
        shards = [[groups[0], near, hop(far[0], 1), far[0]]]
        near, far[1], shards, parts = after((near, far[1], shards, parts))
        shards.append([groups[1], near, hop(far[1], 1), far[1]])
    else:
        shards = [[group] + [hop(group, m) for m in range(1, cols)] for group in groups]
    for rel in chips:
        parts[rel + 1] = swap(parts[rel], 1, "row")
    shards[0], parts = after((shards[0], parts))
    for rel in range(2, rows, 2):
        top = 1 << (rel.bit_length() - 1)
        if rel not in parts:
            parts[rel] = swap(parts[rel - top], top, "row")
    delta, second = dense(weight_two, shards[0], hidden, mask, col_at, 0)
    deltas, seconds, inputs, firsts = [delta], [second], [], []
    if cols == 4:
        near, far = [hop(delta, 1)], [hop(delta, 3)]
    delta, second = dense(weight_two, shards[1], hidden, mask, col_at, 1)
    deltas.append(delta)
    seconds.append(second)
    order = delta
    if cols == 4:
        near[0], far[0], parts, order = after((near[0], far[0], parts, order))
        shards = [[deltas[0], near[0], hop(far[0], 1), far[0]]]
        near.append(hop(delta, 1))
        far.append(hop(delta, 3))
    else:
        shards = [[delta] + [hop(delta, m) for m in range(1, cols)] for delta in deltas]
    for rel in range(1, rows, 2):
        if rel not in parts:
            parts[rel] = swap(parts[rel - 1], 1, "row")
    agg_feats = aggregate(edge_tiles, block_cols, [parts[rel] for rel in range(rows)], me_at, order)
    if cols == 4:
        near[1], far[1], agg_feats = after((near[1], far[1], agg_feats))
        shards.append([deltas[1], near[1], hop(far[1], 1), far[1]])
    for g in range(GROUPS):
        out, grad = dense(weight_one, shards[g], agg_feats, None, col_at, g)
        inputs.append(out)
        firsts.append(grad)
    pieces = spread(edge_tiles, block_cols, inputs, me_at, rows)
    keep, send = weight_terms(firsts, seconds, me_at)
    value = over_chips(keep + swap(send, 1, "row").astype(F32), chips[-1:])
    terms, value = scatter(pieces, rows, value)
    terms, value = after((terms, over_chips(value, chips[:-1])))
    (out,) = finish([t for pair in terms for t in pair], True)
    other = swap(value, 1, "row")
    even = me % 2 == 0
    first_grad, second_grad = jnp.where(even, other, value), jnp.where(even, value, other)
    return out.reshape(-1, out.shape[2]), first_grad, second_grad


def solution(mesh):
    in_specs = (
        P("row", "col"),
        P("row", "col"),
        P("row", "col"),
        P("row", "col"),
        P("row", None, None, None),
        P("row", None),
        P("col", None),
        P("col", None),
    )
    out_specs = (P("row", "col"), P("col", None), P("col", None))
    return jax.shard_map(
        per_device, mesh=mesh, in_specs=in_specs, out_specs=out_specs, check_vma=False
    )
```

```python
import functools

import jax
import jax.numpy as jnp
from jax import lax
from jax.experimental import pallas as pl
from jax.experimental.pallas import tpu as pltpu
from jax.sharding import PartitionSpec as P

GROUPS = 2
COPIES = 4
F32 = jnp.float32
BF16 = jnp.bfloat16
VMEM = pl.BlockSpec(memory_space=pltpu.VMEM)
SMEM = pl.BlockSpec(memory_space=pltpu.SMEM)


def params(mib):
    return pltpu.CompilerParams(vmem_limit_bytes=mib * 1024 * 1024)


def tile_copy(tiles_ref, held, sems, i):
    per = held.shape[0] // COPIES
    part = pl.ds(i * per, per)
    return pltpu.make_async_copy(tiles_ref.at[part], held.at[part], sems.at[i])


def over_rows(tiles_ref, held, sems, one_row):
    per = held.shape[0] // COPIES

    def piece(i, carry):
        tile_copy(tiles_ref, held, sems, i).wait()
        for j in range(per):
            one_row(i * per + j)
        return carry

    lax.fori_loop(0, COPIES, piece, 0)


def spread_kernel(first, pieces, cols_ref, me_ref, tiles_ref, *rest):
    vals, rest = rest[:pieces], rest[pieces:]
    if first:
        mask_ref, *rest = rest
        outs, (mask_out, acc, held, sems, left_ref, mask_held) = rest[: 2 * GROUPS], rest[2 * GROUPS :]
        loads = [
            pltpu.make_async_copy(vals[0], left_ref, sems.at[COPIES]),
            pltpu.make_async_copy(mask_ref, mask_held, sems.at[COPIES + 1]),
        ]
        loads[0].start()
    else:
        outs, (acc, held, sems, left_ref) = rest[: 2 * GROUPS], rest[2 * GROUPS :]
    for i in range(COPIES):
        tile_copy(tiles_ref, held, sems, i).start()
    if first:
        loads[1].start()
    acc[...] = jnp.zeros_like(acc)
    per_row, size = held.shape[1], held.shape[3]
    me = me_ref[0]
    if first:
        loads[0].wait()
    else:
        for g in range(pieces):
            count = vals[g].shape[0]
            left_ref[g * count : (g + 1) * count] = vals[g][...]

    def one_row(r):
        left = left_ref[r].astype(F32).T.astype(BF16) if first else left_ref[r]
        for k in range(0, per_row, 2):
            pair = jnp.concatenate([held[r, k], held[r, k + 1]], axis=1)
            both = jnp.dot(left, pair, preferred_element_type=F32)
            for side in range(2):
                acc[cols_ref[r, k + side]] += both[:, side * size : (side + 1) * size]

    over_rows(tiles_ref, held, sems, one_row)
    halves, count = outs[0].shape[:2]
    for g in range(GROUPS):
        for side in range(2):
            for rel in range(halves):
                owner = jnp.bitwise_xor(me, 2 * rel + side)
                start = (owner * GROUPS + g) * count
                outs[2 * g + side][rel] = acc[pl.ds(start, count)].astype(BF16)
    if first:
        loads[1].wait()
        for b in range(mask_held.shape[0]):
            mask_out[b] = mask_held[b].astype(F32).T.astype(BF16)


def spread(edge_tiles, block_cols, vals, me, rows, mask=None):
    blocks, _, size, _ = edge_tiles.shape
    first = mask is not None
    feat = vals[0].shape[2] if first else vals[0].shape[1]
    out = jax.ShapeDtypeStruct((rows // 2, blocks // GROUPS, feat, size), BF16)
    outs = [out] * (2 * GROUPS)
    scratch = [
        pltpu.VMEM((rows * blocks, feat, size), F32),
        pltpu.VMEM(edge_tiles.shape, BF16),
        pltpu.SemaphoreType.DMA((COPIES + 2,)),
    ]
    anywhere = pl.BlockSpec(memory_space=pl.ANY)
    if first:
        outs.append(jax.ShapeDtypeStruct((blocks, feat, size), BF16))
        scratch += [pltpu.VMEM(v.shape, v.dtype) for v in (vals[0], mask)]
        args, place = [vals[0], mask], anywhere
    else:
        scratch.append(pltpu.VMEM((blocks, feat, size), BF16))
        args, place = vals, VMEM
    return pl.pallas_call(
        functools.partial(spread_kernel, first, len(vals)),
        out_shape=outs,
        in_specs=[SMEM, SMEM, anywhere] + [place] * len(args),
        out_specs=[VMEM] * len(outs),
        scratch_shapes=scratch,
        compiler_params=params(48),
        cost_estimate=pl.CostEstimate(flops=2 * edge_tiles.size * feat, bytes_accessed=30_000_000, transcendentals=0),
        name="spread",
    )(block_cols, me, edge_tiles, *args)


def aggregate_kernel(cols_ref, me_ref, tiles_ref, *rest):
    parts, (out_ref, held, table, sems) = rest[:-4], rest[-4:]
    blocks, per_row = held.shape[:2]
    loads = []
    for rel, part in enumerate(parts):
        place = table.at[pl.ds(jnp.bitwise_xor(me_ref[0], rel) * blocks, blocks)]
        loads.append(pltpu.make_async_copy(part, place, sems.at[COPIES + rel]))
    for load in loads:
        load.start()
    for i in range(COPIES):
        tile_copy(tiles_ref, held, sems, i).start()
    for load in loads:
        load.wait()

    def one_row(r):
        total = None
        for k in range(0, per_row, 2):
            pair = jnp.concatenate([held[r, k], held[r, k + 1]], axis=1)
            picked = jnp.concatenate([table[cols_ref[r, k]], table[cols_ref[r, k + 1]]], axis=0)
            term = jnp.dot(pair, picked, preferred_element_type=F32)
            total = term if total is None else total + term
        out_ref[r] = total.astype(BF16)

    over_rows(tiles_ref, held, sems, one_row)


def aggregate(edge_tiles, block_cols, parts, me):
    blocks, _, size, _ = edge_tiles.shape
    feat = parts[0].shape[2]
    anywhere = pl.BlockSpec(memory_space=pl.ANY)
    return pl.pallas_call(
        aggregate_kernel,
        out_shape=jax.ShapeDtypeStruct((blocks, size, feat), BF16),
        in_specs=[SMEM, SMEM, anywhere] + [anywhere] * len(parts),
        out_specs=VMEM,
        scratch_shapes=[
            pltpu.VMEM(edge_tiles.shape, BF16),
            pltpu.VMEM((len(parts) * blocks, size, feat), BF16),
            pltpu.SemaphoreType.DMA((COPIES + len(parts),)),
        ],
        compiler_params=params(48),
        cost_estimate=pl.CostEstimate(flops=2 * edge_tiles.size * feat, bytes_accessed=30_000_000, transcendentals=0),
        name="aggregate",
    )(block_cols, me, edge_tiles, *parts)


def finish_kernel(last, *refs):
    parts, rest = refs[: 2 * GROUPS], refs[2 * GROUPS :]
    out_ref = rest[3] if last else rest[0]
    count = parts[0].shape[0]
    for g in range(GROUPS):
        for b in range(count):
            total = parts[2 * g][b].astype(F32) + parts[2 * g + 1][b].astype(F32)
            out_ref[g * count + b] = (total.T if last else total).astype(BF16)
    if last:
        me_ref, value_ref, other_ref, _, first_ref, second_ref = rest
        even = jnp.bitwise_and(me_ref[0], 1) == 0
        first_ref[...] = jnp.where(even, other_ref[...], value_ref[...])
        second_ref[...] = jnp.where(even, value_ref[...], other_ref[...])


def finish(parts, grads=()):
    count, feat, size = parts[0].shape
    last = len(grads) > 0
    outs = [jax.ShapeDtypeStruct((count * GROUPS,) + ((size, feat) if last else (feat, size)), BF16)]
    outs += [jax.ShapeDtypeStruct(grad.shape, F32) for grad in grads[1:]]
    return pl.pallas_call(
        functools.partial(finish_kernel, last),
        out_shape=outs,
        in_specs=[VMEM] * len(parts) + [SMEM, VMEM, VMEM][: len(grads)],
        out_specs=[VMEM] * len(outs),
        compiler_params=params(12),
        cost_estimate=pl.CostEstimate(flops=0, bytes_accessed=1_000_000_000 if last else 1, transcendentals=0),
        name="finish",
    )(*parts, *grads)


def dense_kernel(cols, masked, pieces, col_ref, weight_ref, *rest):
    shards, rest = rest[:cols], rest[cols:]
    side_ref, rest = rest[0], rest[1:]
    if masked:
        mask_ref, rest = rest[0], rest[1:]
    outs, (grad_ref,) = rest[:pieces], rest[pieces:]
    blocks, feat, size = shards[0].shape
    per = blocks // pieces
    total = None
    for i, out in enumerate(outs):
        mine = range(i * per, (i + 1) * per)
        whole = jnp.concatenate([jnp.concatenate([shards[m][b] for b in mine], axis=1) for m in range(cols)], axis=0)
        res = jnp.dot(weight_ref[...], whole, preferred_element_type=F32)
        for k, b in enumerate(mine):
            block = res[:, k * size : (k + 1) * size]
            out[k] = (block * mask_ref[b].astype(F32) if masked else block).astype(BF16)
        side = jnp.concatenate([side_ref[b] for b in mine], axis=0)
        term = jnp.dot(whole, side, preferred_element_type=F32)
        total = term if total is None else total + term
    for m in range(cols):
        grad_ref[jnp.bitwise_xor(col_ref[0], m)] = total[m * feat : (m + 1) * feat]


def dense(weight, shards, side, mask, col, pieces):
    blocks, feat, size = shards[0].shape
    cols = len(shards)
    args = [weight, *shards, side] + ([] if mask is None else [mask])
    return pl.pallas_call(
        functools.partial(dense_kernel, cols, mask is not None, pieces),
        out_shape=[jax.ShapeDtypeStruct((blocks // pieces, feat, size), BF16)] * pieces
        + [jax.ShapeDtypeStruct((cols, feat, side.shape[2]), F32)],
        in_specs=[SMEM] + [VMEM] * len(args),
        out_specs=[VMEM] * (pieces + 1),
        compiler_params=params(16),
        name="dense",
    )(col, *args)


def weight_terms_kernel(me_ref, second_ref, *refs):
    firsts, (keep_ref, send_ref) = refs[:-2], refs[-2:]
    cols, feat, width = second_ref.shape
    even = jnp.bitwise_and(me_ref[0], 1) == 0
    first = jnp.concatenate([sum(r[q] for r in firsts) for q in range(cols)], axis=0).T
    second = jnp.concatenate([second_ref[q] for q in range(cols)], axis=0).T
    keep_ref[...] = jnp.where(even, second, first)
    send_ref[...] = jnp.where(even, first, second).astype(BF16)


def weight_terms(firsts, second, me):
    cols, feat, width = second.shape
    shape = (width, cols * feat)
    return pl.pallas_call(
        weight_terms_kernel,
        out_shape=[jax.ShapeDtypeStruct(shape, F32), jax.ShapeDtypeStruct(shape, BF16)],
        in_specs=[SMEM] + [VMEM] * (1 + len(firsts)),
        out_specs=[VMEM] * 2,
        compiler_params=params(8),
        name="weight_terms",
    )(me, second, *firsts)


def swap(value, mask, axis):
    return lax.ppermute(value, axis, [(i, i ^ mask) for i in range(lax.axis_size(axis))])


def add(a, b):
    return (a.astype(F32) + b.astype(F32)).astype(BF16)


def scatter_group(keep, got, masks, beside):
    left = sorted(masks, reverse=True)
    for mask in masks:
        axis = left.index(mask)
        part = lambda v, i: lax.index_in_dim(v, i, axis, keepdims=False)
        sent = swap(add(part(keep, 1), part(got, 1)), mask, "row")
        keep = add(part(keep, 0), part(got, 0))
        got = sent
        left.remove(mask)
        if beside is not None and mask == masks[0]:
            got, beside = lax.optimization_barrier((got, beside))
    return [keep, got], beside


def scatter(pieces, rows, beside=None):
    masks = [1 << b for b in range(1, rows.bit_length() - 1)]
    lead = (2,) * len(masks)
    done = []
    for g in range(GROUPS):
        keep, got = pieces[2 * g], swap(pieces[2 * g + 1], 1, "row")
        order = masks if g % 2 == 0 else masks[::-1]
        terms, beside = scatter_group(keep.reshape(lead + keep.shape[1:]), got.reshape(lead + got.shape[1:]), order, beside)
        done.append(terms)
    return done, beside


def gather_columns(own, cols, beside=()):
    if cols == 4:
        near, far, beside = lax.optimization_barrier((swap(own, 1, "col"), swap(own, 3, "col"), beside))
        return [own, near, swap(far, 1, "col"), far], beside
    return [own] + [swap(own, m, "col") for m in range(1, cols)], beside


def over_chips(value, masks):
    for mask in masks:
        value = value.astype(BF16)
        value = value.astype(F32) + swap(value, mask, "row").astype(F32)
    return value


def per_device(
    node_feats, hidden_act, grad_out, relu_mask, edge_tiles, block_cols, weight_one, weight_two
):
    rows, cols = lax.axis_size("row"), lax.axis_size("col")
    me, col = lax.axis_index("row").astype(jnp.int32), lax.axis_index("col").astype(jnp.int32)
    me_at, col_at = me.reshape(1), col.reshape(1)
    size = edge_tiles.shape[2]
    per = edge_tiles.shape[0] // GROUPS
    chips = [1 << b for b in range(1, rows.bit_length() - 1)]
    cut = lambda v, g: v[g * per : (g + 1) * per]
    blocked = lambda v: v.reshape(v.shape[0] // size, size, v.shape[1])
    after = lax.optimization_barrier

    def by_distance(weight):
        split = weight.reshape(weight.shape[0], cols, weight.shape[1] // cols)
        order = [lax.dynamic_index_in_dim(split, col ^ m, 1, keepdims=False) for m in range(cols)]
        return jnp.concatenate(order, axis=1)

    *pieces, mask = spread(edge_tiles, block_cols, [blocked(grad_out)], me_at, rows, blocked(relu_mask))
    terms, _ = scatter(pieces, rows)
    own, node_feats = after((finish([t for pair in terms for t in pair])[0], blocked(node_feats)))
    own, weight_one, weight_two = after((own, weight_one, weight_two))
    weight_one, weight_two = by_distance(weight_one), by_distance(weight_two)
    shards, _ = gather_columns(own, cols)
    parts = [node_feats] + [swap(node_feats, rel, "row") for rel in range(2, rows, 2)]
    parts = [v for part in parts for v in (part, swap(part, 1, "row"))]
    shards, parts = after((shards, parts))
    *deltas, second = dense(weight_two, shards, blocked(hidden_act), mask, col_at, GROUPS)
    deltas[0], parts = after((deltas[0], parts))
    agg_feats = aggregate(edge_tiles, block_cols, parts, me_at)
    inputs, firsts = [], []
    for g in range(GROUPS):
        shards, beside = gather_columns(deltas[g], cols, agg_feats if g == 0 else ())
        agg_feats = beside if g == 0 else agg_feats
        out, grad = dense(weight_one, shards, cut(agg_feats, g), None, col_at, 1)
        inputs.append(out)
        firsts.append(grad)
    pieces = spread(edge_tiles, block_cols, inputs, me_at, rows)
    keep, send = weight_terms(firsts, second, me_at)
    value = over_chips(keep + swap(send, 1, "row").astype(F32), chips[-1:])
    terms, value = scatter(pieces, rows, value)
    value = over_chips(value, chips[:-1])
    grads = [me_at, value, swap(value, 1, "row")]
    out, first_grad, second_grad = finish([t for pair in terms for t in pair], grads)
    return out.reshape(-1, out.shape[2]), first_grad, second_grad


def solution(mesh):
    in_specs = (
        P("row", "col"),
        P("row", "col"),
        P("row", "col"),
        P("row", "col"),
        P("row", None, None, None),
        P("row", None),
        P("col", None),
        P("col", None),
    )
    out_specs = (P("row", "col"), P("col", None), P("col", None))
    return jax.shard_map(
        per_device, mesh=mesh, in_specs=in_specs, out_specs=out_specs, check_vma=False
    )
```

```python
import functools

import jax
import jax.numpy as jnp
from jax import lax
from jax.experimental import pallas as pl
from jax.experimental.pallas import tpu as pltpu
from jax.sharding import PartitionSpec as P

GROUPS = 2
COPIES = 4
F32 = jnp.float32
BF16 = jnp.bfloat16
VMEM = pl.BlockSpec(memory_space=pltpu.VMEM)
SMEM = pl.BlockSpec(memory_space=pltpu.SMEM)


def params(mib):
    return pltpu.CompilerParams(vmem_limit_bytes=mib * 1024 * 1024)


def tile_copy(tiles_ref, held, sems, i):
    per = held.shape[0] // COPIES
    part = pl.ds(i * per, per)
    return pltpu.make_async_copy(tiles_ref.at[part], held.at[part], sems.at[i])


def over_rows(tiles_ref, held, sems, one_row):
    per = held.shape[0] // COPIES

    def piece(i, carry):
        tile_copy(tiles_ref, held, sems, i).wait()
        for j in range(per):
            one_row(i * per + j)
        return carry

    lax.fori_loop(0, COPIES, piece, 0)


def spread_kernel(first, start, earlier, cols_ref, me_ref, tiles_ref, vals_ref, *rest):
    tiles_ref = tiles_ref.at[pl.ds(start, vals_ref.shape[0])]
    sums, rest = rest[:earlier], rest[earlier:]
    if first:
        mask_ref, *rest = rest
        outs, (mask_out, acc, held, sems, left_ref, mask_held) = rest[: 2 * GROUPS], rest[2 * GROUPS :]
        loads = [
            pltpu.make_async_copy(vals_ref, left_ref, sems.at[COPIES]),
            pltpu.make_async_copy(mask_ref, mask_held, sems.at[COPIES + 1]),
        ]
        loads[0].start()
    else:
        outs, (acc, held, sems) = rest[: 2 * GROUPS], rest[2 * GROUPS :]
    for i in range(COPIES):
        tile_copy(tiles_ref, held, sems, i).start()
    if first:
        loads[1].start()
    acc[...] = jnp.zeros_like(acc)
    per_row, size = held.shape[1], held.shape[3]
    me = me_ref[0]
    if first:
        loads[0].wait()

    def one_row(r):
        left = left_ref[r].astype(F32).T.astype(BF16) if first else vals_ref[r]
        for k in range(0, per_row, 2):
            pair = jnp.concatenate([held[r, k], held[r, k + 1]], axis=1)
            both = jnp.dot(left, pair, preferred_element_type=F32)
            for side in range(2):
                acc[cols_ref[start + r, k + side]] += both[:, side * size : (side + 1) * size]

    over_rows(tiles_ref, held, sems, one_row)
    halves, count = outs[0].shape[:2]
    for g in range(GROUPS):
        for side in range(2):
            for rel in range(halves):
                owner = jnp.bitwise_xor(me, 2 * rel + side)
                total = acc[pl.ds((owner * GROUPS + g) * count, count)]
                if earlier:
                    total = total + sums[2 * g + side][rel].astype(F32)
                outs[2 * g + side][rel] = total.astype(BF16)
    if first:
        loads[1].wait()
        for b in range(mask_held.shape[0]):
            mask_out[b] = mask_held[b].astype(F32).T.astype(BF16)


def spread(edge_tiles, block_cols, vals, me, rows, mask=None, start=0, earlier=()):
    blocks, _, size, _ = edge_tiles.shape
    first = mask is not None
    feat = vals.shape[2] if first else vals.shape[1]
    out = jax.ShapeDtypeStruct((rows // 2, blocks // GROUPS, feat, size), BF16)
    outs = [out] * (2 * GROUPS)
    scratch = [
        pltpu.VMEM((rows * blocks, feat, size), F32),
        pltpu.VMEM((vals.shape[0],) + edge_tiles.shape[1:], BF16),
        pltpu.SemaphoreType.DMA((COPIES + 2,)),
    ]
    anywhere = pl.BlockSpec(memory_space=pl.ANY)
    if first:
        outs.append(jax.ShapeDtypeStruct((blocks, feat, size), BF16))
        scratch += [pltpu.VMEM(v.shape, v.dtype) for v in (vals, mask)]
        args, place = [vals, mask], anywhere
    else:
        args, place = [vals, *earlier], VMEM
    return pl.pallas_call(
        functools.partial(spread_kernel, first, start, len(earlier)),
        out_shape=outs,
        in_specs=[SMEM, SMEM, anywhere] + [place] * len(args),
        out_specs=[VMEM] * len(outs),
        scratch_shapes=scratch,
        compiler_params=params(48 if first else 28),
        cost_estimate=pl.CostEstimate(flops=2 * edge_tiles.size * feat, bytes_accessed=30_000_000, transcendentals=0),
        name="spread",
    )(block_cols, me, edge_tiles, *args)


def aggregate_kernel(cols_ref, me_ref, tiles_ref, *rest):
    parts, (out_ref, held, table, sems) = rest[:-4], rest[-4:]
    blocks, per_row = held.shape[:2]
    loads = []
    for rel, part in enumerate(parts):
        place = table.at[pl.ds(jnp.bitwise_xor(me_ref[0], rel) * blocks, blocks)]
        loads.append(pltpu.make_async_copy(part, place, sems.at[COPIES + rel]))
    for load in loads:
        load.start()
    for i in range(COPIES):
        tile_copy(tiles_ref, held, sems, i).start()
    for load in loads:
        load.wait()

    def one_row(r):
        total = None
        for k in range(0, per_row, 2):
            pair = jnp.concatenate([held[r, k], held[r, k + 1]], axis=1)
            picked = jnp.concatenate([table[cols_ref[r, k]], table[cols_ref[r, k + 1]]], axis=0)
            term = jnp.dot(pair, picked, preferred_element_type=F32)
            total = term if total is None else total + term
        out_ref[r] = total.astype(BF16)

    over_rows(tiles_ref, held, sems, one_row)


def aggregate(edge_tiles, block_cols, parts, me):
    blocks, _, size, _ = edge_tiles.shape
    feat = parts[0].shape[2]
    anywhere = pl.BlockSpec(memory_space=pl.ANY)
    return pl.pallas_call(
        aggregate_kernel,
        out_shape=jax.ShapeDtypeStruct((blocks, size, feat), BF16),
        in_specs=[SMEM, SMEM, anywhere] + [anywhere] * len(parts),
        out_specs=VMEM,
        scratch_shapes=[
            pltpu.VMEM(edge_tiles.shape, BF16),
            pltpu.VMEM((len(parts) * blocks, size, feat), BF16),
            pltpu.SemaphoreType.DMA((COPIES + len(parts),)),
        ],
        compiler_params=params(48),
        cost_estimate=pl.CostEstimate(flops=2 * edge_tiles.size * feat, bytes_accessed=30_000_000, transcendentals=0),
        name="aggregate",
    )(block_cols, me, edge_tiles, *parts)


def finish_kernel(last, *refs):
    parts, rest = refs[: 2 * GROUPS], refs[2 * GROUPS :]
    out_ref = rest[3] if last else rest[0]
    count = parts[0].shape[0]
    for g in range(GROUPS):
        for b in range(count):
            total = parts[2 * g][b].astype(F32) + parts[2 * g + 1][b].astype(F32)
            out_ref[g * count + b] = (total.T if last else total).astype(BF16)
    if last:
        me_ref, value_ref, other_ref, _, first_ref, second_ref = rest
        even = jnp.bitwise_and(me_ref[0], 1) == 0
        first_ref[...] = jnp.where(even, other_ref[...], value_ref[...])
        second_ref[...] = jnp.where(even, value_ref[...], other_ref[...])


def finish(parts, grads=()):
    count, feat, size = parts[0].shape
    last = len(grads) > 0
    outs = [jax.ShapeDtypeStruct((count * GROUPS,) + ((size, feat) if last else (feat, size)), BF16)]
    outs += [jax.ShapeDtypeStruct(grad.shape, F32) for grad in grads[1:]]
    return pl.pallas_call(
        functools.partial(finish_kernel, last),
        out_shape=outs,
        in_specs=[VMEM] * len(parts) + [SMEM, VMEM, VMEM][: len(grads)],
        out_specs=[VMEM] * len(outs),
        compiler_params=params(12),
        cost_estimate=pl.CostEstimate(flops=0, bytes_accessed=1_000_000_000 if last else 1, transcendentals=0),
        name="finish",
    )(*parts, *grads)


def dense_kernel(cols, masked, pieces, col_ref, weight_ref, *rest):
    shards, rest = rest[:cols], rest[cols:]
    side_ref, rest = rest[0], rest[1:]
    if masked:
        mask_ref, rest = rest[0], rest[1:]
    outs, (grad_ref,) = rest[:pieces], rest[pieces:]
    blocks, feat, size = shards[0].shape
    per = blocks // pieces
    total = None
    for i, out in enumerate(outs):
        mine = range(i * per, (i + 1) * per)
        whole = jnp.concatenate([jnp.concatenate([shards[m][b] for b in mine], axis=1) for m in range(cols)], axis=0)
        res = jnp.dot(weight_ref[...], whole, preferred_element_type=F32)
        for k, b in enumerate(mine):
            block = res[:, k * size : (k + 1) * size]
            out[k] = (block * mask_ref[b].astype(F32) if masked else block).astype(BF16)
        side = jnp.concatenate([side_ref[b] for b in mine], axis=0)
        term = jnp.dot(whole, side, preferred_element_type=F32)
        total = term if total is None else total + term
    for m in range(cols):
        grad_ref[jnp.bitwise_xor(col_ref[0], m)] = total[m * feat : (m + 1) * feat]


def dense(weight, shards, side, mask, col, pieces):
    blocks, feat, size = shards[0].shape
    cols = len(shards)
    args = [weight, *shards, side] + ([] if mask is None else [mask])
    return pl.pallas_call(
        functools.partial(dense_kernel, cols, mask is not None, pieces),
        out_shape=[jax.ShapeDtypeStruct((blocks // pieces, feat, size), BF16)] * pieces
        + [jax.ShapeDtypeStruct((cols, feat, side.shape[2]), F32)],
        in_specs=[SMEM] + [VMEM] * len(args),
        out_specs=[VMEM] * (pieces + 1),
        compiler_params=params(16),
        name="dense",
    )(col, *args)


def dense_early_kernel(cols, late, col_ref, weight_ref, *rest):
    shards, (side_ref, out_ref, grad_ref) = rest[: cols - 1], rest[cols - 1 :]
    blocks, feat, size = shards[0].shape
    here = [m for m in range(cols) if m != late]
    per = blocks // GROUPS
    weight = jnp.concatenate([weight_ref[:, m * feat : (m + 1) * feat] for m in here], axis=1)
    total = None
    for i in range(GROUPS):
        mine = range(i * per, (i + 1) * per)
        whole = jnp.concatenate([jnp.concatenate([shard[b] for b in mine], axis=1) for shard in shards], axis=0)
        out_ref[i] = jnp.dot(weight, whole, preferred_element_type=F32)
        term = jnp.dot(whole, jnp.concatenate([side_ref[b] for b in mine], axis=0), preferred_element_type=F32)
        total = term if total is None else total + term
    for i, m in enumerate(here):
        grad_ref[jnp.bitwise_xor(col_ref[0], m)] = total[i * feat : (i + 1) * feat]


def dense_early(weight, shards, side, col, late):
    blocks, feat, size = shards[0].shape
    cols = len(shards)
    args = [weight, *(v for m, v in enumerate(shards) if m != late), side]
    return pl.pallas_call(
        functools.partial(dense_early_kernel, cols, late),
        out_shape=[
            jax.ShapeDtypeStruct((GROUPS, feat, blocks // GROUPS * size), F32),
            jax.ShapeDtypeStruct((cols, feat, side.shape[2]), F32),
        ],
        in_specs=[SMEM] + [VMEM] * len(args),
        out_specs=[VMEM] * 2,
        compiler_params=params(16),
        name="dense_early",
    )(col, *args)


def dense_late_kernel(late, weight_ref, shard_ref, part_ref, side_ref, mask_ref, *rest):
    outs, grad_ref = rest[:GROUPS], rest[GROUPS]
    blocks, feat, size = shard_ref.shape
    per = blocks // GROUPS
    weight = weight_ref[:, late * feat : (late + 1) * feat]
    total = None
    for i, out in enumerate(outs):
        mine = range(i * per, (i + 1) * per)
        whole = jnp.concatenate([shard_ref[b] for b in mine], axis=1)
        res = part_ref[i] + jnp.dot(weight, whole, preferred_element_type=F32)
        for k, b in enumerate(mine):
            out[k] = (res[:, k * size : (k + 1) * size] * mask_ref[b].astype(F32)).astype(BF16)
        term = jnp.dot(whole, jnp.concatenate([side_ref[b] for b in mine], axis=0), preferred_element_type=F32)
        total = term if total is None else total + term
    grad_ref[...] = total


def dense_late(weight, shard, part, side, mask, late):
    blocks, feat, size = shard.shape
    return pl.pallas_call(
        functools.partial(dense_late_kernel, late),
        out_shape=[jax.ShapeDtypeStruct((blocks // GROUPS, feat, size), BF16)] * GROUPS
        + [jax.ShapeDtypeStruct((feat, side.shape[2]), F32)],
        in_specs=[VMEM] * 5,
        out_specs=[VMEM] * (GROUPS + 1),
        compiler_params=params(16),
        name="dense_late",
    )(weight, shard, part, side, mask)


def weight_terms_kernel(late, me_ref, col_ref, second_ref, late_ref, *refs):
    firsts, (keep_ref, send_ref, held) = refs[:-3], refs[-3:]
    cols = second_ref.shape[0]
    even = jnp.bitwise_and(me_ref[0], 1) == 0
    held[...] = second_ref[...]
    held[jnp.bitwise_xor(col_ref[0], late)] = late_ref[...]
    first = jnp.concatenate([sum(r[q] for r in firsts) for q in range(cols)], axis=0).T
    second = jnp.concatenate([held[q] for q in range(cols)], axis=0).T
    keep_ref[...] = jnp.where(even, second, first)
    send_ref[...] = jnp.where(even, first, second).astype(BF16)


def weight_terms(firsts, second, last, me, col, late):
    cols, feat, width = second.shape
    shape = (width, cols * feat)
    return pl.pallas_call(
        functools.partial(weight_terms_kernel, late),
        out_shape=[jax.ShapeDtypeStruct(shape, F32), jax.ShapeDtypeStruct(shape, BF16)],
        in_specs=[SMEM, SMEM] + [VMEM] * (2 + len(firsts)),
        out_specs=[VMEM] * 2,
        scratch_shapes=[pltpu.VMEM(second.shape, F32)],
        compiler_params=params(8),
        name="weight_terms",
    )(me, col, second, last, *firsts)


def swap(value, mask, axis):
    return lax.ppermute(value, axis, [(i, i ^ mask) for i in range(lax.axis_size(axis))])


def add(a, b):
    return (a.astype(F32) + b.astype(F32)).astype(BF16)


def scatter(pieces, rows, value=None):
    chips = [1 << b for b in range(1, rows.bit_length() - 1)]
    shape = (2,) * len(chips) + pieces[0].shape[1:]
    keeps = [pieces[2 * g].reshape(shape) for g in range(GROUPS)]
    gots = [swap(pieces[2 * g + 1], 1, "row").reshape(shape) for g in range(GROUPS)]
    orders = [chips if g % 2 == 0 else chips[::-1] for g in range(GROUPS)]
    lefts = [chips[::-1] for _ in range(GROUPS)]
    for level in range(len(chips)):
        masks = [order[level] for order in orders]
        sent = []
        for g in range(GROUPS):
            axis = lefts[g].index(masks[g])
            lefts[g] = [m for m in lefts[g] if m != masks[g]]
            half = lambda v, i: lax.index_in_dim(v, i, axis, keepdims=False)
            sent.append(add(half(keeps[g], 1), half(gots[g], 1)))
            keeps[g] = add(half(keeps[g], 0), half(gots[g], 0))
        if value is not None:
            keeps, value = lax.optimization_barrier((keeps, value))
        gots = [swap(sent[g], masks[g], "row") for g in range(GROUPS)]
        if value is not None:
            value = value.astype(BF16)
            value = value.astype(F32) + swap(value, chips[-1 - level], "row").astype(F32)
            if level < len(chips) - 1:
                gots, value = lax.optimization_barrier((gots, value))
    return [t for pair in zip(keeps, gots) for t in pair], value


def gather_columns(own, cols, beside=()):
    if cols == 4:
        near, far, beside = lax.optimization_barrier((swap(own, 1, "col"), swap(own, 3, "col"), beside))
        return [own, near, swap(far, 1, "col"), far], beside
    return [own] + [swap(own, m, "col") for m in range(1, cols)], beside


def per_device(
    node_feats, hidden_act, grad_out, relu_mask, edge_tiles, block_cols, weight_one, weight_two
):
    rows, cols = lax.axis_size("row"), lax.axis_size("col")
    me, col = lax.axis_index("row").astype(jnp.int32), lax.axis_index("col").astype(jnp.int32)
    me_at, col_at = me.reshape(1), col.reshape(1)
    size = edge_tiles.shape[2]
    per = edge_tiles.shape[0] // GROUPS
    cut = lambda v, g: v[g * per : (g + 1) * per]
    blocked = lambda v: v.reshape(v.shape[0] // size, size, v.shape[1])
    after = lax.optimization_barrier

    def by_distance(weight):
        split = weight.reshape(weight.shape[0], cols, weight.shape[1] // cols)
        order = [lax.dynamic_index_in_dim(split, col ^ m, 1, keepdims=False) for m in range(cols)]
        return jnp.concatenate(order, axis=1)

    *pieces, mask = spread(edge_tiles, block_cols, blocked(grad_out), me_at, rows, blocked(relu_mask))
    terms, _ = scatter(pieces, rows)
    own, node_feats = after((finish(terms)[0], blocked(node_feats)))
    own, weight_one, weight_two = after((own, weight_one, weight_two))
    weight_one, weight_two = by_distance(weight_one), by_distance(weight_two)
    shards, _ = gather_columns(own, cols)
    parts = [node_feats] + [swap(node_feats, rel, "row") for rel in range(2, rows, 2)]
    parts = [v for part in parts for v in (part, swap(part, 1, "row"))]
    late = 2
    hidden = blocked(hidden_act)
    part, second = dense_early(weight_two, shards, hidden, col_at, late)
    arrived, parts = after((shards[late], parts))
    *deltas, last = dense_late(weight_two, arrived, part, hidden, mask, late)
    deltas[0], parts = after((deltas[0], parts))
    agg_feats = aggregate(edge_tiles, block_cols, parts, me_at)
    pieces, firsts = (), []
    for g in range(GROUPS):
        shards, beside = gather_columns(deltas[g], cols, agg_feats if g == 0 else ())
        agg_feats = beside if g == 0 else agg_feats
        out, grad = dense(weight_one, shards, cut(agg_feats, g), None, col_at, 1)
        pieces = spread(edge_tiles, block_cols, out, me_at, rows, None, g * per, pieces)
        firsts.append(grad)
    keep, send = weight_terms(firsts, second, last, me_at, col_at, late)
    terms, value = scatter(pieces, rows, keep + swap(send, 1, "row").astype(F32))
    grads = [me_at, value, swap(value, 1, "row")]
    out, first_grad, second_grad = finish(terms, grads)
    return out.reshape(-1, out.shape[2]), first_grad, second_grad


def solution(mesh):
    in_specs = (
        P("row", "col"),
        P("row", "col"),
        P("row", "col"),
        P("row", "col"),
        P("row", None, None, None),
        P("row", None),
        P("col", None),
        P("col", None),
    )
    out_specs = (P("row", "col"), P("col", None), P("col", None))
    return jax.shard_map(
        per_device, mesh=mesh, in_specs=in_specs, out_specs=out_specs, check_vma=False
    )
```

```python
import functools

import jax
import jax.numpy as jnp
from jax import lax
from jax.experimental import pallas as pl
from jax.experimental.pallas import tpu as pltpu
from jax.sharding import PartitionSpec as P

GROUPS = 2
COPIES = 4
F32 = jnp.float32
BF16 = jnp.bfloat16
VMEM = pl.BlockSpec(memory_space=pltpu.VMEM)
SMEM = pl.BlockSpec(memory_space=pltpu.SMEM)


def params(mib):
    return pltpu.CompilerParams(vmem_limit_bytes=mib * 1024 * 1024)


def tile_copy(tiles_ref, held, sems, i):
    per = held.shape[0] // COPIES
    part = pl.ds(i * per, per)
    return pltpu.make_async_copy(tiles_ref.at[part], held.at[part], sems.at[i])


def over_rows(tiles_ref, held, sems, one_row):
    per = held.shape[0] // COPIES

    def piece(i, carry):
        tile_copy(tiles_ref, held, sems, i).wait()
        for j in range(per):
            one_row(i * per + j)
        return carry

    lax.fori_loop(0, COPIES, piece, 0)


def spread_kernel(first, pieces, cols_ref, me_ref, tiles_ref, *rest):
    vals, rest = rest[:pieces], rest[pieces:]
    if first:
        mask_ref, *rest = rest
        outs, (mask_out, acc, held, sems, left_ref, mask_held) = rest[: 2 * GROUPS], rest[2 * GROUPS :]
        loads = [
            pltpu.make_async_copy(vals[0], left_ref, sems.at[COPIES]),
            pltpu.make_async_copy(mask_ref, mask_held, sems.at[COPIES + 1]),
        ]
        loads[0].start()
    else:
        outs, (acc, held, sems, left_ref) = rest[: 2 * GROUPS], rest[2 * GROUPS :]
    for i in range(COPIES):
        tile_copy(tiles_ref, held, sems, i).start()
    if first:
        loads[1].start()
    acc[...] = jnp.zeros_like(acc)
    per_row, size = held.shape[1], held.shape[3]
    me = me_ref[0]
    if first:
        loads[0].wait()
    else:
        for g in range(pieces):
            count = vals[g].shape[0]
            left_ref[g * count : (g + 1) * count] = vals[g][...]

    def one_row(r):
        left = left_ref[r].astype(F32).T.astype(BF16) if first else left_ref[r]
        for k in range(0, per_row, 2):
            pair = jnp.concatenate([held[r, k], held[r, k + 1]], axis=1)
            both = jnp.dot(left, pair, preferred_element_type=F32)
            for side in range(2):
                acc[cols_ref[r, k + side]] += both[:, side * size : (side + 1) * size]

    over_rows(tiles_ref, held, sems, one_row)
    halves, count = outs[0].shape[:2]
    for g in range(GROUPS):
        for side in range(2):
            for rel in range(halves):
                owner = jnp.bitwise_xor(me, 2 * rel + side)
                start = (owner * GROUPS + g) * count
                outs[2 * g + side][rel] = acc[pl.ds(start, count)].astype(BF16)
    if first:
        loads[1].wait()
        for b in range(mask_held.shape[0]):
            mask_out[b] = mask_held[b].astype(F32).T.astype(BF16)


def spread(edge_tiles, block_cols, vals, me, rows, mask=None):
    blocks, _, size, _ = edge_tiles.shape
    first = mask is not None
    feat = vals[0].shape[2] if first else vals[0].shape[1]
    out = jax.ShapeDtypeStruct((rows // 2, blocks // GROUPS, feat, size), BF16)
    outs = [out] * (2 * GROUPS)
    scratch = [
        pltpu.VMEM((rows * blocks, feat, size), F32),
        pltpu.VMEM(edge_tiles.shape, BF16),
        pltpu.SemaphoreType.DMA((COPIES + 2,)),
    ]
    anywhere = pl.BlockSpec(memory_space=pl.ANY)
    if first:
        outs.append(jax.ShapeDtypeStruct((blocks, feat, size), BF16))
        scratch += [pltpu.VMEM(v.shape, v.dtype) for v in (vals[0], mask)]
        args, place = [vals[0], mask], anywhere
    else:
        scratch.append(pltpu.VMEM((blocks, feat, size), BF16))
        args, place = vals, VMEM
    return pl.pallas_call(
        functools.partial(spread_kernel, first, len(vals)),
        out_shape=outs,
        in_specs=[SMEM, SMEM, anywhere] + [place] * len(args),
        out_specs=[VMEM] * len(outs),
        scratch_shapes=scratch,
        compiler_params=params(48),
        cost_estimate=pl.CostEstimate(flops=2 * edge_tiles.size * feat, bytes_accessed=30_000_000, transcendentals=0),
        name="spread",
    )(block_cols, me, edge_tiles, *args)


def aggregate_kernel(cols_ref, me_ref, tiles_ref, *rest):
    parts, (out_ref, held, table, sems) = rest[:-4], rest[-4:]
    blocks, per_row = held.shape[:2]
    loads = []
    for rel, part in enumerate(parts):
        place = table.at[pl.ds(jnp.bitwise_xor(me_ref[0], rel) * blocks, blocks)]
        loads.append(pltpu.make_async_copy(part, place, sems.at[COPIES + rel]))
    for load in loads:
        load.start()
    for i in range(COPIES):
        tile_copy(tiles_ref, held, sems, i).start()
    for load in loads:
        load.wait()

    def one_row(r):
        total = None
        for k in range(0, per_row, 2):
            pair = jnp.concatenate([held[r, k], held[r, k + 1]], axis=1)
            picked = jnp.concatenate([table[cols_ref[r, k]], table[cols_ref[r, k + 1]]], axis=0)
            term = jnp.dot(pair, picked, preferred_element_type=F32)
            total = term if total is None else total + term
        out_ref[r] = total.astype(BF16)

    over_rows(tiles_ref, held, sems, one_row)


def aggregate(edge_tiles, block_cols, parts, me):
    blocks, _, size, _ = edge_tiles.shape
    feat = parts[0].shape[2]
    anywhere = pl.BlockSpec(memory_space=pl.ANY)
    return pl.pallas_call(
        aggregate_kernel,
        out_shape=jax.ShapeDtypeStruct((blocks, size, feat), BF16),
        in_specs=[SMEM, SMEM, anywhere] + [anywhere] * len(parts),
        out_specs=VMEM,
        scratch_shapes=[
            pltpu.VMEM(edge_tiles.shape, BF16),
            pltpu.VMEM((len(parts) * blocks, size, feat), BF16),
            pltpu.SemaphoreType.DMA((COPIES + len(parts),)),
        ],
        compiler_params=params(48),
        cost_estimate=pl.CostEstimate(flops=2 * edge_tiles.size * feat, bytes_accessed=30_000_000, transcendentals=0),
        name="aggregate",
    )(block_cols, me, edge_tiles, *parts)


def finish_kernel(last, *refs):
    parts, rest = refs[: 2 * GROUPS], refs[2 * GROUPS :]
    out_ref = rest[3] if last else rest[0]
    count = parts[0].shape[0]
    for g in range(GROUPS):
        for b in range(count):
            total = parts[2 * g][b].astype(F32) + parts[2 * g + 1][b].astype(F32)
            out_ref[g * count + b] = (total.T if last else total).astype(BF16)
    if last:
        me_ref, value_ref, other_ref, _, first_ref, second_ref = rest
        even = jnp.bitwise_and(me_ref[0], 1) == 0
        first_ref[...] = jnp.where(even, other_ref[...], value_ref[...])
        second_ref[...] = jnp.where(even, value_ref[...], other_ref[...])


def finish(parts, grads=()):
    count, feat, size = parts[0].shape
    last = len(grads) > 0
    outs = [jax.ShapeDtypeStruct((count * GROUPS,) + ((size, feat) if last else (feat, size)), BF16)]
    outs += [jax.ShapeDtypeStruct(grad.shape, F32) for grad in grads[1:]]
    return pl.pallas_call(
        functools.partial(finish_kernel, last),
        out_shape=outs,
        in_specs=[VMEM] * len(parts) + [SMEM, VMEM, VMEM][: len(grads)],
        out_specs=[VMEM] * len(outs),
        compiler_params=params(12),
        cost_estimate=pl.CostEstimate(flops=0, bytes_accessed=1_000_000_000 if last else 1, transcendentals=0),
        name="finish",
    )(*parts, *grads)


def dense_kernel(cols, masked, pieces, col_ref, weight_ref, *rest):
    shards, rest = rest[:cols], rest[cols:]
    side_ref, rest = rest[0], rest[1:]
    if masked:
        mask_ref, rest = rest[0], rest[1:]
    outs, (grad_ref,) = rest[:pieces], rest[pieces:]
    blocks, feat, size = shards[0].shape
    per = blocks // pieces
    total = None
    for i, out in enumerate(outs):
        mine = range(i * per, (i + 1) * per)
        whole = jnp.concatenate([jnp.concatenate([shards[m][b] for b in mine], axis=1) for m in range(cols)], axis=0)
        res = jnp.dot(weight_ref[...], whole, preferred_element_type=F32)
        for k, b in enumerate(mine):
            block = res[:, k * size : (k + 1) * size]
            out[k] = (block * mask_ref[b].astype(F32) if masked else block).astype(BF16)
        side = jnp.concatenate([side_ref[b] for b in mine], axis=0)
        term = jnp.dot(whole, side, preferred_element_type=F32)
        total = term if total is None else total + term
    for m in range(cols):
        grad_ref[jnp.bitwise_xor(col_ref[0], m)] = total[m * feat : (m + 1) * feat]


def dense(weight, shards, side, mask, col, pieces):
    blocks, feat, size = shards[0].shape
    cols = len(shards)
    args = [weight, *shards, side] + ([] if mask is None else [mask])
    return pl.pallas_call(
        functools.partial(dense_kernel, cols, mask is not None, pieces),
        out_shape=[jax.ShapeDtypeStruct((blocks // pieces, feat, size), BF16)] * pieces
        + [jax.ShapeDtypeStruct((cols, feat, side.shape[2]), F32)],
        in_specs=[SMEM] + [VMEM] * len(args),
        out_specs=[VMEM] * (pieces + 1),
        compiler_params=params(16),
        name="dense",
    )(col, *args)


def dense_early_kernel(cols, late, col_ref, weight_ref, *rest):
    shards, (side_ref, out_ref, grad_ref) = rest[: cols - 1], rest[cols - 1 :]
    blocks, feat, size = shards[0].shape
    here = [m for m in range(cols) if m != late]
    per = blocks // GROUPS
    weight = jnp.concatenate([weight_ref[:, m * feat : (m + 1) * feat] for m in here], axis=1)
    total = None
    for i in range(GROUPS):
        mine = range(i * per, (i + 1) * per)
        whole = jnp.concatenate([jnp.concatenate([shard[b] for b in mine], axis=1) for shard in shards], axis=0)
        out_ref[i] = jnp.dot(weight, whole, preferred_element_type=F32)
        term = jnp.dot(whole, jnp.concatenate([side_ref[b] for b in mine], axis=0), preferred_element_type=F32)
        total = term if total is None else total + term
    for i, m in enumerate(here):
        grad_ref[jnp.bitwise_xor(col_ref[0], m)] = total[i * feat : (i + 1) * feat]


def dense_early(weight, shards, side, col, late):
    blocks, feat, size = shards[0].shape
    cols = len(shards)
    args = [weight, *(v for m, v in enumerate(shards) if m != late), side]
    return pl.pallas_call(
        functools.partial(dense_early_kernel, cols, late),
        out_shape=[
            jax.ShapeDtypeStruct((GROUPS, feat, blocks // GROUPS * size), F32),
            jax.ShapeDtypeStruct((cols, feat, side.shape[2]), F32),
        ],
        in_specs=[SMEM] + [VMEM] * len(args),
        out_specs=[VMEM] * 2,
        compiler_params=params(16),
        name="dense_early",
    )(col, *args)


def dense_late_kernel(late, weight_ref, shard_ref, part_ref, side_ref, mask_ref, *rest):
    outs, grad_ref = rest[:GROUPS], rest[GROUPS]
    blocks, feat, size = shard_ref.shape
    per = blocks // GROUPS
    weight = weight_ref[:, late * feat : (late + 1) * feat]
    total = None
    for i, out in enumerate(outs):
        mine = range(i * per, (i + 1) * per)
        whole = jnp.concatenate([shard_ref[b] for b in mine], axis=1)
        res = part_ref[i] + jnp.dot(weight, whole, preferred_element_type=F32)
        for k, b in enumerate(mine):
            out[k] = (res[:, k * size : (k + 1) * size] * mask_ref[b].astype(F32)).astype(BF16)
        term = jnp.dot(whole, jnp.concatenate([side_ref[b] for b in mine], axis=0), preferred_element_type=F32)
        total = term if total is None else total + term
    grad_ref[...] = total


def dense_late(weight, shard, part, side, mask, late):
    blocks, feat, size = shard.shape
    return pl.pallas_call(
        functools.partial(dense_late_kernel, late),
        out_shape=[jax.ShapeDtypeStruct((blocks // GROUPS, feat, size), BF16)] * GROUPS
        + [jax.ShapeDtypeStruct((feat, side.shape[2]), F32)],
        in_specs=[VMEM] * 5,
        out_specs=[VMEM] * (GROUPS + 1),
        compiler_params=params(16),
        name="dense_late",
    )(weight, shard, part, side, mask)


def weight_terms_kernel(late, me_ref, col_ref, second_ref, late_ref, *refs):
    firsts, (keep_ref, send_ref, held) = refs[:-3], refs[-3:]
    cols = second_ref.shape[0]
    even = jnp.bitwise_and(me_ref[0], 1) == 0
    held[...] = second_ref[...]
    held[jnp.bitwise_xor(col_ref[0], late)] = late_ref[...]
    first = jnp.concatenate([sum(r[q] for r in firsts) for q in range(cols)], axis=0).T
    second = jnp.concatenate([held[q] for q in range(cols)], axis=0).T
    keep_ref[...] = jnp.where(even, second, first)
    send_ref[...] = jnp.where(even, first, second).astype(BF16)


def weight_terms(firsts, second, last, me, col, late):
    cols, feat, width = second.shape
    shape = (width, cols * feat)
    return pl.pallas_call(
        functools.partial(weight_terms_kernel, late),
        out_shape=[jax.ShapeDtypeStruct(shape, F32), jax.ShapeDtypeStruct(shape, BF16)],
        in_specs=[SMEM, SMEM] + [VMEM] * (2 + len(firsts)),
        out_specs=[VMEM] * 2,
        scratch_shapes=[pltpu.VMEM(second.shape, F32)],
        compiler_params=params(8),
        name="weight_terms",
    )(me, col, second, last, *firsts)


def swap(value, mask, axis):
    return lax.ppermute(value, axis, [(i, i ^ mask) for i in range(lax.axis_size(axis))])


def add(a, b):
    return (a.astype(F32) + b.astype(F32)).astype(BF16)


def scatter(pieces, rows, value=None):
    chips = [1 << b for b in range(1, rows.bit_length() - 1)]
    shape = (2,) * len(chips) + pieces[0].shape[1:]
    keeps = [pieces[2 * g].reshape(shape) for g in range(GROUPS)]
    gots = [swap(pieces[2 * g + 1], 1, "row").reshape(shape) for g in range(GROUPS)]
    orders = [chips if g % 2 == 0 else chips[::-1] for g in range(GROUPS)]
    lefts = [chips[::-1] for _ in range(GROUPS)]
    for level in range(len(chips)):
        masks = [order[level] for order in orders]
        sent = []
        for g in range(GROUPS):
            axis = lefts[g].index(masks[g])
            lefts[g] = [m for m in lefts[g] if m != masks[g]]
            half = lambda v, i: lax.index_in_dim(v, i, axis, keepdims=False)
            sent.append(add(half(keeps[g], 1), half(gots[g], 1)))
            keeps[g] = add(half(keeps[g], 0), half(gots[g], 0))
        if value is not None:
            keeps, value = lax.optimization_barrier((keeps, value))
        gots = [swap(sent[g], masks[g], "row") for g in range(GROUPS)]
        if value is not None:
            value = value.astype(BF16)
            value = value.astype(F32) + swap(value, chips[-1 - level], "row").astype(F32)
            if level < len(chips) - 1:
                gots, value = lax.optimization_barrier((gots, value))
    return [t for pair in zip(keeps, gots) for t in pair], value


def gather_columns(own, cols, beside=(), tied=True):
    if cols == 4:
        near, far = swap(own, 1, "col"), swap(own, 3, "col")
        if tied:
            near, far, beside = lax.optimization_barrier((near, far, beside))
        else:
            near, beside = lax.optimization_barrier((near, beside))
        return [own, near, swap(far, 1, "col"), far], beside
    return [own] + [swap(own, m, "col") for m in range(1, cols)], beside


def per_device(
    node_feats, hidden_act, grad_out, relu_mask, edge_tiles, block_cols, weight_one, weight_two
):
    rows, cols = lax.axis_size("row"), lax.axis_size("col")
    me, col = lax.axis_index("row").astype(jnp.int32), lax.axis_index("col").astype(jnp.int32)
    me_at, col_at = me.reshape(1), col.reshape(1)
    size = edge_tiles.shape[2]
    per = edge_tiles.shape[0] // GROUPS
    cut = lambda v, g: v[g * per : (g + 1) * per]
    blocked = lambda v: v.reshape(v.shape[0] // size, size, v.shape[1])
    after = lax.optimization_barrier

    def by_distance(weight):
        split = weight.reshape(weight.shape[0], cols, weight.shape[1] // cols)
        order = [lax.dynamic_index_in_dim(split, col ^ m, 1, keepdims=False) for m in range(cols)]
        return jnp.concatenate(order, axis=1)

    *pieces, mask = spread(edge_tiles, block_cols, [blocked(grad_out)], me_at, rows, blocked(relu_mask))
    terms, _ = scatter(pieces, rows)
    own, node_feats = after((finish(terms)[0], blocked(node_feats)))
    own, weight_one, weight_two = after((own, weight_one, weight_two))
    weight_one, weight_two = by_distance(weight_one), by_distance(weight_two)
    parts = [node_feats] + [swap(node_feats, rel, "row") for rel in range(2, rows, 2)]
    shards, parts[0] = gather_columns(own, cols, node_feats, False)
    parts = [v for part in parts for v in (part, swap(part, 1, "row"))]
    late = 2
    hidden = blocked(hidden_act)
    part, second = dense_early(weight_two, shards, hidden, col_at, late)
    arrived, parts = after((shards[late], parts))
    *deltas, last = dense_late(weight_two, arrived, part, hidden, mask, late)
    deltas[0], parts = after((deltas[0], parts))
    agg_feats = aggregate(edge_tiles, block_cols, parts, me_at)
    inputs, firsts = [], []
    for g in range(GROUPS):
        shards, beside = gather_columns(deltas[g], cols, agg_feats if g == 0 else ())
        agg_feats = beside if g == 0 else agg_feats
        out, grad = dense(weight_one, shards, cut(agg_feats, g), None, col_at, 1)
        inputs.append(out)
        firsts.append(grad)
    pieces = spread(edge_tiles, block_cols, inputs, me_at, rows)
    keep, send = weight_terms(firsts, second, last, me_at, col_at, late)
    terms, value = scatter(pieces, rows, keep + swap(send, 1, "row").astype(F32))
    grads = [me_at, value, swap(value, 1, "row")]
    out, first_grad, second_grad = finish(terms, grads)
    return out.reshape(-1, out.shape[2]), first_grad, second_grad


def solution(mesh):
    in_specs = (
        P("row", "col"),
        P("row", "col"),
        P("row", "col"),
        P("row", "col"),
        P("row", None, None, None),
        P("row", None),
        P("col", None),
        P("col", None),
    )
    out_specs = (P("row", "col"), P("col", None), P("col", None))
    return jax.shard_map(
        per_device, mesh=mesh, in_specs=in_specs, out_specs=out_specs, check_vma=False
    )
```

```python
import functools

import jax
import jax.numpy as jnp
from jax import lax
from jax.experimental import pallas as pl
from jax.experimental.pallas import tpu as pltpu
from jax.sharding import PartitionSpec as P

GROUPS = 2
COPIES = 4
F32 = jnp.float32
BF16 = jnp.bfloat16
VMEM = pl.BlockSpec(memory_space=pltpu.VMEM)
SMEM = pl.BlockSpec(memory_space=pltpu.SMEM)


def params(mib):
    return pltpu.CompilerParams(vmem_limit_bytes=mib * 1024 * 1024)


def tile_copy(tiles_ref, held, sems, i):
    per = held.shape[0] // COPIES
    part = pl.ds(i * per, per)
    return pltpu.make_async_copy(tiles_ref.at[part], held.at[part], sems.at[i])


def over_rows(tiles_ref, held, sems, one_row):
    per = held.shape[0] // COPIES

    def piece(i, carry):
        tile_copy(tiles_ref, held, sems, i).wait()
        for j in range(per):
            one_row(i * per + j)
        return carry

    lax.fori_loop(0, COPIES, piece, 0)


def spread_kernel(first, pieces, cols_ref, me_ref, tiles_ref, *rest):
    vals, rest = rest[:pieces], rest[pieces:]
    if first:
        mask_ref, *rest = rest
        outs, (mask_out, acc, held, sems, left_ref, mask_held) = rest[: 2 * GROUPS], rest[2 * GROUPS :]
        loads = [
            pltpu.make_async_copy(vals[0], left_ref, sems.at[COPIES]),
            pltpu.make_async_copy(mask_ref, mask_held, sems.at[COPIES + 1]),
        ]
        loads[0].start()
    else:
        outs, (acc, held, sems, left_ref) = rest[: 2 * GROUPS], rest[2 * GROUPS :]
    for i in range(COPIES):
        tile_copy(tiles_ref, held, sems, i).start()
    if first:
        loads[1].start()
    acc[...] = jnp.zeros_like(acc)
    per_row, size = held.shape[1], held.shape[3]
    me = me_ref[0]
    if first:
        loads[0].wait()
    else:
        for g in range(pieces):
            count = vals[g].shape[0]
            left_ref[g * count : (g + 1) * count] = vals[g][...]

    def one_row(r):
        left = left_ref[r].astype(F32).T.astype(BF16) if first else left_ref[r]
        for k in range(0, per_row, 2):
            pair = jnp.concatenate([held[r, k], held[r, k + 1]], axis=1)
            both = jnp.dot(left, pair, preferred_element_type=F32)
            for side in range(2):
                acc[cols_ref[r, k + side]] += both[:, side * size : (side + 1) * size]

    over_rows(tiles_ref, held, sems, one_row)
    halves, count = outs[0].shape[:2]
    for g in range(GROUPS):
        for side in range(2):
            for rel in range(halves):
                owner = jnp.bitwise_xor(me, 2 * rel + side)
                start = (owner * GROUPS + g) * count
                outs[2 * g + side][rel] = acc[pl.ds(start, count)].astype(BF16)
    if first:
        loads[1].wait()
        for b in range(mask_held.shape[0]):
            mask_out[b] = mask_held[b].astype(F32).T.astype(BF16)


def spread(edge_tiles, block_cols, vals, me, rows, mask=None):
    blocks, _, size, _ = edge_tiles.shape
    first = mask is not None
    feat = vals[0].shape[2] if first else vals[0].shape[1]
    out = jax.ShapeDtypeStruct((rows // 2, blocks // GROUPS, feat, size), BF16)
    outs = [out] * (2 * GROUPS)
    scratch = [
        pltpu.VMEM((rows * blocks, feat, size), F32),
        pltpu.VMEM(edge_tiles.shape, BF16),
        pltpu.SemaphoreType.DMA((COPIES + 2,)),
    ]
    anywhere = pl.BlockSpec(memory_space=pl.ANY)
    if first:
        outs.append(jax.ShapeDtypeStruct((blocks, feat, size), BF16))
        scratch += [pltpu.VMEM(v.shape, v.dtype) for v in (vals[0], mask)]
        args, place = [vals[0], mask], anywhere
    else:
        scratch.append(pltpu.VMEM((blocks, feat, size), BF16))
        args, place = vals, VMEM
    return pl.pallas_call(
        functools.partial(spread_kernel, first, len(vals)),
        out_shape=outs,
        in_specs=[SMEM, SMEM, anywhere] + [place] * len(args),
        out_specs=[VMEM] * len(outs),
        scratch_shapes=scratch,
        compiler_params=params(48),
        cost_estimate=pl.CostEstimate(flops=2 * edge_tiles.size * feat, bytes_accessed=30_000_000, transcendentals=0),
        name="spread",
    )(block_cols, me, edge_tiles, *args)


def aggregate_kernel(cols_ref, me_ref, tiles_ref, *rest):
    parts, (out_ref, held, table, sems) = rest[:-4], rest[-4:]
    blocks, per_row = held.shape[:2]
    loads = []
    for rel, part in enumerate(parts):
        place = table.at[pl.ds(jnp.bitwise_xor(me_ref[0], rel) * blocks, blocks)]
        loads.append(pltpu.make_async_copy(part, place, sems.at[COPIES + rel]))
    for load in loads:
        load.start()
    for i in range(COPIES):
        tile_copy(tiles_ref, held, sems, i).start()
    for load in loads:
        load.wait()

    def one_row(r):
        total = None
        for k in range(0, per_row, 2):
            pair = jnp.concatenate([held[r, k], held[r, k + 1]], axis=1)
            picked = jnp.concatenate([table[cols_ref[r, k]], table[cols_ref[r, k + 1]]], axis=0)
            term = jnp.dot(pair, picked, preferred_element_type=F32)
            total = term if total is None else total + term
        out_ref[r] = total.astype(BF16)

    over_rows(tiles_ref, held, sems, one_row)


def aggregate(edge_tiles, block_cols, parts, me):
    blocks, _, size, _ = edge_tiles.shape
    feat = parts[0].shape[2]
    anywhere = pl.BlockSpec(memory_space=pl.ANY)
    return pl.pallas_call(
        aggregate_kernel,
        out_shape=jax.ShapeDtypeStruct((blocks, size, feat), BF16),
        in_specs=[SMEM, SMEM, anywhere] + [anywhere] * len(parts),
        out_specs=VMEM,
        scratch_shapes=[
            pltpu.VMEM(edge_tiles.shape, BF16),
            pltpu.VMEM((len(parts) * blocks, size, feat), BF16),
            pltpu.SemaphoreType.DMA((COPIES + len(parts),)),
        ],
        compiler_params=params(48),
        cost_estimate=pl.CostEstimate(flops=2 * edge_tiles.size * feat, bytes_accessed=30_000_000, transcendentals=0),
        name="aggregate",
    )(block_cols, me, edge_tiles, *parts)


def finish_kernel(last, *refs):
    parts, rest = refs[: 2 * GROUPS], refs[2 * GROUPS :]
    out_ref = rest[3] if last else rest[0]
    count = parts[0].shape[0]
    for g in range(GROUPS):
        for b in range(count):
            total = parts[2 * g][b].astype(F32) + parts[2 * g + 1][b].astype(F32)
            out_ref[g * count + b] = (total.T if last else total).astype(BF16)
    if last:
        me_ref, value_ref, other_ref, _, first_ref, second_ref = rest
        even = jnp.bitwise_and(me_ref[0], 1) == 0
        first_ref[...] = jnp.where(even, other_ref[...], value_ref[...])
        second_ref[...] = jnp.where(even, value_ref[...], other_ref[...])


def finish(parts, grads=()):
    count, feat, size = parts[0].shape
    last = len(grads) > 0
    outs = [jax.ShapeDtypeStruct((count * GROUPS,) + ((size, feat) if last else (feat, size)), BF16)]
    outs += [jax.ShapeDtypeStruct(grad.shape, F32) for grad in grads[1:]]
    return pl.pallas_call(
        functools.partial(finish_kernel, last),
        out_shape=outs,
        in_specs=[VMEM] * len(parts) + [SMEM, VMEM, VMEM][: len(grads)],
        out_specs=[VMEM] * len(outs),
        compiler_params=params(12),
        cost_estimate=pl.CostEstimate(flops=0, bytes_accessed=1_000_000_000 if last else 1, transcendentals=0),
        name="finish",
    )(*parts, *grads)


def dense_kernel(cols, masked, pieces, col_ref, weight_ref, *rest):
    shards, rest = rest[:cols], rest[cols:]
    side_ref, rest = rest[0], rest[1:]
    if masked:
        mask_ref, rest = rest[0], rest[1:]
    outs, (grad_ref,) = rest[:pieces], rest[pieces:]
    blocks, feat, size = shards[0].shape
    per = blocks // pieces
    total = None
    for i, out in enumerate(outs):
        mine = range(i * per, (i + 1) * per)
        whole = jnp.concatenate([jnp.concatenate([shards[m][b] for b in mine], axis=1) for m in range(cols)], axis=0)
        res = jnp.dot(weight_ref[...], whole, preferred_element_type=F32)
        for k, b in enumerate(mine):
            block = res[:, k * size : (k + 1) * size]
            out[k] = (block * mask_ref[b].astype(F32) if masked else block).astype(BF16)
        side = jnp.concatenate([side_ref[b] for b in mine], axis=0)
        term = jnp.dot(whole, side, preferred_element_type=F32)
        total = term if total is None else total + term
    for m in range(cols):
        grad_ref[jnp.bitwise_xor(col_ref[0], m)] = total[m * feat : (m + 1) * feat]


def dense(weight, shards, side, mask, col, pieces):
    blocks, feat, size = shards[0].shape
    cols = len(shards)
    args = [weight, *shards, side] + ([] if mask is None else [mask])
    return pl.pallas_call(
        functools.partial(dense_kernel, cols, mask is not None, pieces),
        out_shape=[jax.ShapeDtypeStruct((blocks // pieces, feat, size), BF16)] * pieces
        + [jax.ShapeDtypeStruct((cols, feat, side.shape[2]), F32)],
        in_specs=[SMEM] + [VMEM] * len(args),
        out_specs=[VMEM] * (pieces + 1),
        compiler_params=params(16),
        name="dense",
    )(col, *args)


def dense_early_kernel(cols, late, col_ref, weight_ref, *rest):
    shards, (side_ref, out_ref, grad_ref) = rest[: cols - 1], rest[cols - 1 :]
    blocks, feat, size = shards[0].shape
    here = [m for m in range(cols) if m != late]
    per = blocks // GROUPS
    weight = jnp.concatenate([weight_ref[:, m * feat : (m + 1) * feat] for m in here], axis=1)
    total = None
    for i in range(GROUPS):
        mine = range(i * per, (i + 1) * per)
        whole = jnp.concatenate([jnp.concatenate([shard[b] for b in mine], axis=1) for shard in shards], axis=0)
        out_ref[i] = jnp.dot(weight, whole, preferred_element_type=F32)
        term = jnp.dot(whole, jnp.concatenate([side_ref[b] for b in mine], axis=0), preferred_element_type=F32)
        total = term if total is None else total + term
    for i, m in enumerate(here):
        grad_ref[jnp.bitwise_xor(col_ref[0], m)] = total[i * feat : (i + 1) * feat]


def dense_early(weight, shards, side, col, late):
    blocks, feat, size = shards[0].shape
    cols = len(shards)
    args = [weight, *(v for m, v in enumerate(shards) if m != late), side]
    return pl.pallas_call(
        functools.partial(dense_early_kernel, cols, late),
        out_shape=[
            jax.ShapeDtypeStruct((GROUPS, feat, blocks // GROUPS * size), F32),
            jax.ShapeDtypeStruct((cols, feat, side.shape[2]), F32),
        ],
        in_specs=[SMEM] + [VMEM] * len(args),
        out_specs=[VMEM] * 2,
        compiler_params=params(16),
        name="dense_early",
    )(col, *args)


def dense_late_kernel(late, weight_ref, shard_ref, part_ref, side_ref, mask_ref, *rest):
    outs, grad_ref = rest[:GROUPS], rest[GROUPS]
    blocks, feat, size = shard_ref.shape
    per = blocks // GROUPS
    weight = weight_ref[:, late * feat : (late + 1) * feat]
    total = None
    for i, out in enumerate(outs):
        mine = range(i * per, (i + 1) * per)
        whole = jnp.concatenate([shard_ref[b] for b in mine], axis=1)
        res = part_ref[i] + jnp.dot(weight, whole, preferred_element_type=F32)
        for k, b in enumerate(mine):
            out[k] = (res[:, k * size : (k + 1) * size] * mask_ref[b].astype(F32)).astype(BF16)
        term = jnp.dot(whole, jnp.concatenate([side_ref[b] for b in mine], axis=0), preferred_element_type=F32)
        total = term if total is None else total + term
    grad_ref[...] = total


def dense_late(weight, shard, part, side, mask, late):
    blocks, feat, size = shard.shape
    return pl.pallas_call(
        functools.partial(dense_late_kernel, late),
        out_shape=[jax.ShapeDtypeStruct((blocks // GROUPS, feat, size), BF16)] * GROUPS
        + [jax.ShapeDtypeStruct((feat, side.shape[2]), F32)],
        in_specs=[VMEM] * 5,
        out_specs=[VMEM] * (GROUPS + 1),
        compiler_params=params(16),
        name="dense_late",
    )(weight, shard, part, side, mask)


def weight_terms_kernel(late, me_ref, col_ref, second_ref, late_ref, *refs):
    firsts, (keep_ref, send_ref, held) = refs[:-3], refs[-3:]
    cols = second_ref.shape[0]
    even = jnp.bitwise_and(me_ref[0], 1) == 0
    held[...] = second_ref[...]
    held[jnp.bitwise_xor(col_ref[0], late)] = late_ref[...]
    first = jnp.concatenate([sum(r[q] for r in firsts) for q in range(cols)], axis=0).T
    second = jnp.concatenate([held[q] for q in range(cols)], axis=0).T
    keep_ref[...] = jnp.where(even, second, first)
    send_ref[...] = jnp.where(even, first, second).astype(BF16)


def weight_terms(firsts, second, last, me, col, late):
    cols, feat, width = second.shape
    shape = (width, cols * feat)
    return pl.pallas_call(
        functools.partial(weight_terms_kernel, late),
        out_shape=[jax.ShapeDtypeStruct(shape, F32), jax.ShapeDtypeStruct(shape, BF16)],
        in_specs=[SMEM, SMEM] + [VMEM] * (2 + len(firsts)),
        out_specs=[VMEM] * 2,
        scratch_shapes=[pltpu.VMEM(second.shape, F32)],
        compiler_params=params(8),
        name="weight_terms",
    )(me, col, second, last, *firsts)


def swap(value, mask, axis):
    return lax.ppermute(value, axis, [(i, i ^ mask) for i in range(lax.axis_size(axis))])


def add(a, b):
    return (a.astype(F32) + b.astype(F32)).astype(BF16)


def scatter(pieces, rows, value=None):
    chips = [1 << b for b in range(1, rows.bit_length() - 1)]
    shape = (2,) * len(chips) + pieces[0].shape[1:]
    keeps = [pieces[2 * g].reshape(shape) for g in range(GROUPS)]
    gots = [swap(pieces[2 * g + 1], 1, "row").reshape(shape) for g in range(GROUPS)]
    orders = [chips if g % 2 else chips[::-1] for g in range(GROUPS)]
    lefts = [chips[::-1] for _ in range(GROUPS)]
    for level in range(len(chips)):
        masks = [order[level] for order in orders]
        sent = []
        for g in range(GROUPS):
            axis = lefts[g].index(masks[g])
            lefts[g] = [m for m in lefts[g] if m != masks[g]]
            half = lambda v, i: lax.index_in_dim(v, i, axis, keepdims=False)
            sent.append(add(half(keeps[g], 1), half(gots[g], 1)))
            keeps[g] = add(half(keeps[g], 0), half(gots[g], 0))
        if value is not None:
            keeps, value = lax.optimization_barrier((keeps, value))
        gots = [swap(sent[g], masks[g], "row") for g in range(GROUPS)]
        if value is not None:
            value = value.astype(BF16)
            value = value.astype(F32) + swap(value, chips[-1 - level], "row").astype(F32)
            if level < len(chips) - 1:
                gots, value = lax.optimization_barrier((gots, value))
    return [t for pair in zip(keeps, gots) for t in pair], value


def gather_columns(own, cols, beside=(), tied=True):
    if cols == 4:
        near, far = swap(own, 1, "col"), swap(own, 3, "col")
        if tied:
            near, far, beside = lax.optimization_barrier((near, far, beside))
        else:
            near, beside = lax.optimization_barrier((near, beside))
        return [own, near, swap(far, 1, "col"), far], beside
    return [own] + [swap(own, m, "col") for m in range(1, cols)], beside


def per_device(
    node_feats, hidden_act, grad_out, relu_mask, edge_tiles, block_cols, weight_one, weight_two
):
    rows, cols = lax.axis_size("row"), lax.axis_size("col")
    me, col = lax.axis_index("row").astype(jnp.int32), lax.axis_index("col").astype(jnp.int32)
    me_at, col_at = me.reshape(1), col.reshape(1)
    size = edge_tiles.shape[2]
    per = edge_tiles.shape[0] // GROUPS
    cut = lambda v, g: v[g * per : (g + 1) * per]
    blocked = lambda v: v.reshape(v.shape[0] // size, size, v.shape[1])
    after = lax.optimization_barrier

    def by_distance(weight):
        split = weight.reshape(weight.shape[0], cols, weight.shape[1] // cols)
        order = [lax.dynamic_index_in_dim(split, col ^ m, 1, keepdims=False) for m in range(cols)]
        return jnp.concatenate(order, axis=1)

    *pieces, mask = spread(edge_tiles, block_cols, [blocked(grad_out)], me_at, rows, blocked(relu_mask))
    terms, _ = scatter(pieces, rows)
    own, node_feats = after((finish(terms)[0], blocked(node_feats)))
    own, weight_one, weight_two = after((own, weight_one, weight_two))
    weight_one, weight_two = by_distance(weight_one), by_distance(weight_two)
    parts = [node_feats] + [swap(node_feats, rel, "row") for rel in range(2, rows, 2)]
    shards, parts[0] = gather_columns(own, cols, node_feats, False)
    parts = [v for part in parts for v in (part, swap(part, 1, "row"))]
    late = 2
    hidden = blocked(hidden_act)
    part, second = dense_early(weight_two, shards, hidden, col_at, late)
    arrived, parts = after((shards[late], parts))
    *deltas, last = dense_late(weight_two, arrived, part, hidden, mask, late)
    deltas[0], parts = after((deltas[0], parts))
    agg_feats = aggregate(edge_tiles, block_cols, parts, me_at)
    inputs, firsts = [], []
    shards = []
    for g in range(GROUPS):
        arrived, beside = gather_columns(deltas[g], cols, agg_feats if g == 0 else (), g == 0)
        agg_feats = beside if g == 0 else agg_feats
        shards.append(arrived)
    shards[0][2], shards[1][1] = after((shards[0][2], shards[1][1]))
    for g in range(GROUPS):
        out, grad = dense(weight_one, shards[g], cut(agg_feats, g), None, col_at, 1)
        inputs.append(out)
        firsts.append(grad)
    pieces = spread(edge_tiles, block_cols, inputs, me_at, rows)
    keep, send = weight_terms(firsts, second, last, me_at, col_at, late)
    terms, value = scatter(pieces, rows, keep + swap(send, 1, "row").astype(F32))
    grads = [me_at, value, swap(value, 1, "row")]
    out, first_grad, second_grad = finish(terms, grads)
    return out.reshape(-1, out.shape[2]), first_grad, second_grad


def solution(mesh):
    in_specs = (
        P("row", "col"),
        P("row", "col"),
        P("row", "col"),
        P("row", "col"),
        P("row", None, None, None),
        P("row", None),
        P("col", None),
        P("col", None),
    )
    out_specs = (P("row", "col"), P("col", None), P("col", None))
    return jax.shard_map(
        per_device, mesh=mesh, in_specs=in_specs, out_specs=out_specs, check_vma=False
    )
```

```python
import functools

import jax
import jax.numpy as jnp
from jax import lax
from jax.experimental import pallas as pl
from jax.experimental.pallas import tpu as pltpu
from jax.sharding import PartitionSpec as P

GROUPS = 2
COPIES = 4
F32 = jnp.float32
BF16 = jnp.bfloat16
VMEM = pl.BlockSpec(memory_space=pltpu.VMEM)
SMEM = pl.BlockSpec(memory_space=pltpu.SMEM)


def params(mib):
    return pltpu.CompilerParams(vmem_limit_bytes=mib * 1024 * 1024)


def tile_copy(tiles_ref, held, sems, i):
    per = held.shape[0] // COPIES
    part = pl.ds(i * per, per)
    return pltpu.make_async_copy(tiles_ref.at[part], held.at[part], sems.at[i])


def over_rows(tiles_ref, held, sems, one_row):
    per = held.shape[0] // COPIES

    def piece(i, carry):
        tile_copy(tiles_ref, held, sems, i).wait()
        for j in range(per):
            one_row(i * per + j)
        return carry

    lax.fori_loop(0, COPIES, piece, 0)


def spread_kernel(first, pieces, cols_ref, me_ref, tiles_ref, *rest):
    vals, rest = rest[:pieces], rest[pieces:]
    if first:
        mask_ref, *rest = rest
        outs, (mask_out, acc, held, sems, left_ref, mask_held) = rest[: 2 * GROUPS], rest[2 * GROUPS :]
        loads = [
            pltpu.make_async_copy(vals[0], left_ref, sems.at[COPIES]),
            pltpu.make_async_copy(mask_ref, mask_held, sems.at[COPIES + 1]),
        ]
        loads[0].start()
    else:
        outs, (acc, held, sems, left_ref) = rest[: 2 * GROUPS], rest[2 * GROUPS :]
    for i in range(COPIES):
        tile_copy(tiles_ref, held, sems, i).start()
    if first:
        loads[1].start()
    acc[...] = jnp.zeros_like(acc)
    per_row, size = held.shape[1], held.shape[3]
    me = me_ref[0]
    if first:
        loads[0].wait()
    else:
        for g in range(pieces):
            count = vals[g].shape[0]
            left_ref[g * count : (g + 1) * count] = vals[g][...]

    def one_row(r):
        left = left_ref[r].astype(F32).T.astype(BF16) if first else left_ref[r]
        for k in range(0, per_row, 2):
            pair = jnp.concatenate([held[r, k], held[r, k + 1]], axis=1)
            both = jnp.dot(left, pair, preferred_element_type=F32)
            for side in range(2):
                acc[cols_ref[r * per_row + k + side]] += both[:, side * size : (side + 1) * size]

    over_rows(tiles_ref, held, sems, one_row)
    halves, count = outs[0].shape[:2]
    for g in range(GROUPS):
        for side in range(2):
            for rel in range(halves):
                owner = jnp.bitwise_xor(me, 2 * rel + side)
                start = (owner * GROUPS + g) * count
                outs[2 * g + side][rel] = acc[pl.ds(start, count)].astype(BF16)
    if first:
        loads[1].wait()
        for b in range(mask_held.shape[0]):
            mask_out[b] = mask_held[b].astype(F32).T.astype(BF16)


def spread(edge_tiles, block_cols, vals, me, rows, mask=None):
    blocks, _, size, _ = edge_tiles.shape
    first = mask is not None
    feat = vals[0].shape[2] if first else vals[0].shape[1]
    out = jax.ShapeDtypeStruct((rows // 2, blocks // GROUPS, feat, size), BF16)
    outs = [out] * (2 * GROUPS)
    scratch = [
        pltpu.VMEM((rows * blocks, feat, size), F32),
        pltpu.VMEM(edge_tiles.shape, BF16),
        pltpu.SemaphoreType.DMA((COPIES + 2,)),
    ]
    anywhere = pl.BlockSpec(memory_space=pl.ANY)
    if first:
        outs.append(jax.ShapeDtypeStruct((blocks, feat, size), BF16))
        scratch += [pltpu.VMEM(v.shape, v.dtype) for v in (vals[0], mask)]
        args, place = [vals[0], mask], anywhere
    else:
        scratch.append(pltpu.VMEM((blocks, feat, size), BF16))
        args, place = vals, VMEM
    return pl.pallas_call(
        functools.partial(spread_kernel, first, len(vals)),
        out_shape=outs,
        in_specs=[SMEM, SMEM, anywhere] + [place] * len(args),
        out_specs=[VMEM] * len(outs),
        scratch_shapes=scratch,
        compiler_params=params(48),
        cost_estimate=pl.CostEstimate(flops=2 * edge_tiles.size * feat, bytes_accessed=30_000_000, transcendentals=0),
        name="spread",
    )(block_cols, me, edge_tiles, *args)


def aggregate_kernel(cols_ref, me_ref, tiles_ref, *rest):
    parts, (out_ref, held, table, sems) = rest[:-4], rest[-4:]
    blocks, per_row = held.shape[:2]
    loads = []
    for rel, part in enumerate(parts):
        place = table.at[pl.ds(jnp.bitwise_xor(me_ref[0], rel) * blocks, blocks)]
        loads.append(pltpu.make_async_copy(part, place, sems.at[COPIES + rel]))
    for load in loads:
        load.start()
    for i in range(COPIES):
        tile_copy(tiles_ref, held, sems, i).start()
    for load in loads:
        load.wait()

    def one_row(r):
        total = None
        for k in range(0, per_row, 2):
            pair = jnp.concatenate([held[r, k], held[r, k + 1]], axis=1)
            at = r * per_row + k
            picked = jnp.concatenate([table[cols_ref[at]], table[cols_ref[at + 1]]], axis=0)
            term = jnp.dot(pair, picked, preferred_element_type=F32)
            total = term if total is None else total + term
        out_ref[r] = total.astype(BF16)

    over_rows(tiles_ref, held, sems, one_row)


def aggregate(edge_tiles, block_cols, parts, me):
    blocks, _, size, _ = edge_tiles.shape
    feat = parts[0].shape[2]
    anywhere = pl.BlockSpec(memory_space=pl.ANY)
    return pl.pallas_call(
        aggregate_kernel,
        out_shape=jax.ShapeDtypeStruct((blocks, size, feat), BF16),
        in_specs=[SMEM, SMEM, anywhere] + [anywhere] * len(parts),
        out_specs=VMEM,
        scratch_shapes=[
            pltpu.VMEM(edge_tiles.shape, BF16),
            pltpu.VMEM((len(parts) * blocks, size, feat), BF16),
            pltpu.SemaphoreType.DMA((COPIES + len(parts),)),
        ],
        compiler_params=params(48),
        cost_estimate=pl.CostEstimate(flops=2 * edge_tiles.size * feat, bytes_accessed=30_000_000, transcendentals=0),
        name="aggregate",
    )(block_cols, me, edge_tiles, *parts)


def finish_kernel(last, *refs):
    parts, rest = refs[: 2 * GROUPS], refs[2 * GROUPS :]
    out_ref = rest[3] if last else rest[0]
    count = parts[0].shape[0]
    for g in range(GROUPS):
        for b in range(count):
            total = parts[2 * g][b].astype(F32) + parts[2 * g + 1][b].astype(F32)
            out_ref[g * count + b] = (total.T if last else total).astype(BF16)
    if last:
        me_ref, value_ref, other_ref, _, first_ref, second_ref = rest
        even = jnp.bitwise_and(me_ref[0], 1) == 0
        first_ref[...] = jnp.where(even, other_ref[...], value_ref[...])
        second_ref[...] = jnp.where(even, value_ref[...], other_ref[...])


def finish(parts, grads=()):
    count, feat, size = parts[0].shape
    last = len(grads) > 0
    outs = [jax.ShapeDtypeStruct((count * GROUPS,) + ((size, feat) if last else (feat, size)), BF16)]
    outs += [jax.ShapeDtypeStruct(grad.shape, F32) for grad in grads[1:]]
    return pl.pallas_call(
        functools.partial(finish_kernel, last),
        out_shape=outs,
        in_specs=[VMEM] * len(parts) + [SMEM, VMEM, VMEM][: len(grads)],
        out_specs=[VMEM] * len(outs),
        compiler_params=params(12),
        cost_estimate=pl.CostEstimate(flops=0, bytes_accessed=1_000_000_000 if last else 1, transcendentals=0),
        name="finish",
    )(*parts, *grads)


def dense_kernel(cols, masked, pieces, col_ref, weight_ref, *rest):
    shards, rest = rest[:cols], rest[cols:]
    side_ref, rest = rest[0], rest[1:]
    if masked:
        mask_ref, rest = rest[0], rest[1:]
    outs, (grad_ref,) = rest[:pieces], rest[pieces:]
    blocks, feat, size = shards[0].shape
    per = blocks // pieces
    total = None
    for i, out in enumerate(outs):
        mine = range(i * per, (i + 1) * per)
        whole = jnp.concatenate([jnp.concatenate([shards[m][b] for b in mine], axis=1) for m in range(cols)], axis=0)
        res = jnp.dot(weight_ref[...], whole, preferred_element_type=F32)
        for k, b in enumerate(mine):
            block = res[:, k * size : (k + 1) * size]
            out[k] = (block * mask_ref[b].astype(F32) if masked else block).astype(BF16)
        side = jnp.concatenate([side_ref[b] for b in mine], axis=0)
        term = jnp.dot(whole, side, preferred_element_type=F32)
        total = term if total is None else total + term
    for m in range(cols):
        grad_ref[jnp.bitwise_xor(col_ref[0], m)] = total[m * feat : (m + 1) * feat]


def dense(weight, shards, side, mask, col, pieces):
    blocks, feat, size = shards[0].shape
    cols = len(shards)
    args = [weight, *shards, side] + ([] if mask is None else [mask])
    return pl.pallas_call(
        functools.partial(dense_kernel, cols, mask is not None, pieces),
        out_shape=[jax.ShapeDtypeStruct((blocks // pieces, feat, size), BF16)] * pieces
        + [jax.ShapeDtypeStruct((cols, feat, side.shape[2]), F32)],
        in_specs=[SMEM] + [VMEM] * len(args),
        out_specs=[VMEM] * (pieces + 1),
        compiler_params=params(16),
        name="dense",
    )(col, *args)


def dense_early_kernel(cols, late, col_ref, weight_ref, *rest):
    shards, (side_ref, out_ref, grad_ref) = rest[: cols - 1], rest[cols - 1 :]
    blocks, feat, size = shards[0].shape
    here = [m for m in range(cols) if m != late]
    per = blocks // GROUPS
    weight = jnp.concatenate([weight_ref[:, m * feat : (m + 1) * feat] for m in here], axis=1)
    total = None
    for i in range(GROUPS):
        mine = range(i * per, (i + 1) * per)
        whole = jnp.concatenate([jnp.concatenate([shard[b] for b in mine], axis=1) for shard in shards], axis=0)
        out_ref[i] = jnp.dot(weight, whole, preferred_element_type=F32)
        term = jnp.dot(whole, jnp.concatenate([side_ref[b] for b in mine], axis=0), preferred_element_type=F32)
        total = term if total is None else total + term
    for i, m in enumerate(here):
        grad_ref[jnp.bitwise_xor(col_ref[0], m)] = total[i * feat : (i + 1) * feat]


def dense_early(weight, shards, side, col, late):
    blocks, feat, size = shards[0].shape
    cols = len(shards)
    args = [weight, *(v for m, v in enumerate(shards) if m != late), side]
    return pl.pallas_call(
        functools.partial(dense_early_kernel, cols, late),
        out_shape=[
            jax.ShapeDtypeStruct((GROUPS, feat, blocks // GROUPS * size), F32),
            jax.ShapeDtypeStruct((cols, feat, side.shape[2]), F32),
        ],
        in_specs=[SMEM] + [VMEM] * len(args),
        out_specs=[VMEM] * 2,
        compiler_params=params(16),
        name="dense_early",
    )(col, *args)


def dense_late_kernel(late, weight_ref, shard_ref, part_ref, side_ref, mask_ref, *rest):
    outs, grad_ref = rest[:GROUPS], rest[GROUPS]
    blocks, feat, size = shard_ref.shape
    per = blocks // GROUPS
    weight = weight_ref[:, late * feat : (late + 1) * feat]
    total = None
    for i, out in enumerate(outs):
        mine = range(i * per, (i + 1) * per)
        whole = jnp.concatenate([shard_ref[b] for b in mine], axis=1)
        res = part_ref[i] + jnp.dot(weight, whole, preferred_element_type=F32)
        for k, b in enumerate(mine):
            out[k] = (res[:, k * size : (k + 1) * size] * mask_ref[b].astype(F32)).astype(BF16)
        term = jnp.dot(whole, jnp.concatenate([side_ref[b] for b in mine], axis=0), preferred_element_type=F32)
        total = term if total is None else total + term
    grad_ref[...] = total


def dense_late(weight, shard, part, side, mask, late):
    blocks, feat, size = shard.shape
    return pl.pallas_call(
        functools.partial(dense_late_kernel, late),
        out_shape=[jax.ShapeDtypeStruct((blocks // GROUPS, feat, size), BF16)] * GROUPS
        + [jax.ShapeDtypeStruct((feat, side.shape[2]), F32)],
        in_specs=[VMEM] * 5,
        out_specs=[VMEM] * (GROUPS + 1),
        compiler_params=params(16),
        name="dense_late",
    )(weight, shard, part, side, mask)


def weight_terms_kernel(late, me_ref, col_ref, second_ref, late_ref, *refs):
    firsts, (keep_ref, send_ref, held) = refs[:-3], refs[-3:]
    cols = second_ref.shape[0]
    even = jnp.bitwise_and(me_ref[0], 1) == 0
    held[...] = second_ref[...]
    held[jnp.bitwise_xor(col_ref[0], late)] = late_ref[...]
    first = jnp.concatenate([sum(r[q] for r in firsts) for q in range(cols)], axis=0).T
    second = jnp.concatenate([held[q] for q in range(cols)], axis=0).T
    keep_ref[...] = jnp.where(even, second, first)
    send_ref[...] = jnp.where(even, first, second).astype(BF16)


def weight_terms(firsts, second, last, me, col, late):
    cols, feat, width = second.shape
    shape = (width, cols * feat)
    return pl.pallas_call(
        functools.partial(weight_terms_kernel, late),
        out_shape=[jax.ShapeDtypeStruct(shape, F32), jax.ShapeDtypeStruct(shape, BF16)],
        in_specs=[SMEM, SMEM] + [VMEM] * (2 + len(firsts)),
        out_specs=[VMEM] * 2,
        scratch_shapes=[pltpu.VMEM(second.shape, F32)],
        compiler_params=params(8),
        name="weight_terms",
    )(me, col, second, last, *firsts)


def swap(value, mask, axis):
    return lax.ppermute(value, axis, [(i, i ^ mask) for i in range(lax.axis_size(axis))])


def add(a, b):
    return (a.astype(F32) + b.astype(F32)).astype(BF16)


def scatter(pieces, rows, value=None):
    chips = [1 << b for b in range(1, rows.bit_length() - 1)]
    shape = (2,) * len(chips) + pieces[0].shape[1:]
    keeps = [pieces[2 * g].reshape(shape) for g in range(GROUPS)]
    gots = [swap(pieces[2 * g + 1], 1, "row").reshape(shape) for g in range(GROUPS)]
    orders = [chips if g % 2 else chips[::-1] for g in range(GROUPS)]
    lefts = [chips[::-1] for _ in range(GROUPS)]
    for level in range(len(chips)):
        masks = [order[level] for order in orders]
        sent = []
        for g in range(GROUPS):
            axis = lefts[g].index(masks[g])
            lefts[g] = [m for m in lefts[g] if m != masks[g]]
            half = lambda v, i: lax.index_in_dim(v, i, axis, keepdims=False)
            sent.append(add(half(keeps[g], 1), half(gots[g], 1)))
            keeps[g] = add(half(keeps[g], 0), half(gots[g], 0))
        if value is not None:
            keeps, value = lax.optimization_barrier((keeps, value))
        gots = [swap(sent[g], masks[g], "row") for g in range(GROUPS)]
        if value is not None:
            value = value.astype(BF16)
            value = value.astype(F32) + swap(value, chips[-1 - level], "row").astype(F32)
            if level < len(chips) - 1:
                gots, value = lax.optimization_barrier((gots, value))
    return [t for pair in zip(keeps, gots) for t in pair], value


def gather_columns(own, cols, beside=(), tied=True):
    if cols == 4:
        near, far = swap(own, 1, "col"), swap(own, 3, "col")
        if tied:
            far, near, beside = lax.optimization_barrier((far, near, beside))
        else:
            near, beside = lax.optimization_barrier((near, beside))
        return [own, near, swap(far, 1, "col"), far], beside
    return [own] + [swap(own, m, "col") for m in range(1, cols)], beside


def per_device(
    node_feats, hidden_act, grad_out, relu_mask, edge_tiles, block_cols, weight_one, weight_two
):
    rows, cols = lax.axis_size("row"), lax.axis_size("col")
    me, col = lax.axis_index("row").astype(jnp.int32), lax.axis_index("col").astype(jnp.int32)
    me_at, col_at = me.reshape(1), col.reshape(1)
    size = edge_tiles.shape[2]
    per = edge_tiles.shape[0] // GROUPS
    cut = lambda v, g: v[g * per : (g + 1) * per]
    blocked = lambda v: v.reshape(v.shape[0] // size, size, v.shape[1])
    after = lax.optimization_barrier

    def by_distance(weight):
        split = weight.reshape(weight.shape[0], cols, weight.shape[1] // cols)
        order = [lax.dynamic_index_in_dim(split, col ^ m, 1, keepdims=False) for m in range(cols)]
        return jnp.concatenate(order, axis=1)

    block_cols = block_cols.reshape(-1)
    *pieces, mask = spread(edge_tiles, block_cols, [blocked(grad_out)], me_at, rows, blocked(relu_mask))
    terms, _ = scatter(pieces, rows)
    own, node_feats = after((finish(terms)[0], blocked(node_feats)))
    own, weight_one, weight_two = after((own, weight_one, weight_two))
    weight_one, weight_two = by_distance(weight_one), by_distance(weight_two)
    parts = [node_feats] + [swap(node_feats, rel, "row") for rel in range(2, rows, 2)]
    shards, parts[0] = gather_columns(own, cols, node_feats, False)
    parts = [v for part in parts for v in (part, swap(part, 1, "row"))]
    late = 2
    hidden = blocked(hidden_act)
    part, second = dense_early(weight_two, shards, hidden, col_at, late)
    arrived, parts = after((shards[late], parts))
    *deltas, last = dense_late(weight_two, arrived, part, hidden, mask, late)
    deltas[0], parts = after((deltas[0], parts))
    agg_feats = aggregate(edge_tiles, block_cols, parts, me_at)
    inputs, firsts = [], []
    shards = []
    for g in range(GROUPS):
        arrived, beside = gather_columns(deltas[g], cols, agg_feats if g == 0 else ())
        agg_feats = beside if g == 0 else agg_feats
        shards.append(arrived)
    for g in range(GROUPS):
        out, grad = dense(weight_one, shards[g], cut(agg_feats, g), None, col_at, 1)
        inputs.append(out)
        firsts.append(grad)
    pieces = spread(edge_tiles, block_cols, inputs, me_at, rows)
    keep, send = weight_terms(firsts, second, last, me_at, col_at, late)
    terms, value = scatter(pieces, rows, keep + swap(send, 1, "row").astype(F32))
    grads = [me_at, value, swap(value, 1, "row")]
    out, first_grad, second_grad = finish(terms, grads)
    return out.reshape(-1, out.shape[2]), first_grad, second_grad


def solution(mesh):
    in_specs = (
        P("row", "col"),
        P("row", "col"),
        P("row", "col"),
        P("row", "col"),
        P("row", None, None, None),
        P("row", None),
        P("col", None),
        P("col", None),
    )
    out_specs = (P("row", "col"), P("col", None), P("col", None))
    return jax.shard_map(
        per_device, mesh=mesh, in_specs=in_specs, out_specs=out_specs, check_vma=False
    )
```

```python
import functools

import jax
import jax.numpy as jnp
from jax import lax
from jax.experimental import pallas as pl
from jax.experimental.pallas import tpu as pltpu
from jax.sharding import PartitionSpec as P

GROUPS = 2
COPIES = 4
F32 = jnp.float32
BF16 = jnp.bfloat16
VMEM = pl.BlockSpec(memory_space=pltpu.VMEM)
SMEM = pl.BlockSpec(memory_space=pltpu.SMEM)


def params(mib):
    return pltpu.CompilerParams(vmem_limit_bytes=mib * 1024 * 1024)


def tile_copy(tiles_ref, held, sems, i):
    per = held.shape[0] // COPIES
    part = pl.ds(i * per, per)
    return pltpu.make_async_copy(tiles_ref.at[part], held.at[part], sems.at[i])


def over_rows(tiles_ref, held, sems, one_row):
    per = held.shape[0] // COPIES

    def piece(i, carry):
        tile_copy(tiles_ref, held, sems, i).wait()
        for j in range(per):
            one_row(i * per + j)
        return carry

    lax.fori_loop(0, COPIES, piece, 0)


def spread_kernel(first, pieces, cols_ref, me_ref, tiles_ref, *rest):
    vals, rest = rest[:pieces], rest[pieces:]
    if first:
        mask_ref, *rest = rest
        outs, (mask_out, acc, held, sems, left_ref, mask_held) = rest[: 2 * GROUPS], rest[2 * GROUPS :]
        loads = [
            pltpu.make_async_copy(vals[0], left_ref, sems.at[COPIES]),
            pltpu.make_async_copy(mask_ref, mask_held, sems.at[COPIES + 1]),
        ]
        loads[0].start()
    else:
        outs, (acc, held, sems, left_ref) = rest[: 2 * GROUPS], rest[2 * GROUPS :]
    for i in range(COPIES):
        tile_copy(tiles_ref, held, sems, i).start()
    if first:
        loads[1].start()
    acc[...] = jnp.zeros_like(acc)
    per_row, size = held.shape[1], held.shape[3]
    me = me_ref[0]
    if first:
        loads[0].wait()
    else:
        for g in range(pieces):
            count = vals[g].shape[0]
            left_ref[g * count : (g + 1) * count] = vals[g][...]

    def one_row(r):
        left = left_ref[r].astype(F32).T.astype(BF16) if first else left_ref[r]
        for k in range(0, per_row, 2):
            pair = jnp.concatenate([held[r, k], held[r, k + 1]], axis=1)
            both = jnp.dot(left, pair, preferred_element_type=F32)
            for side in range(2):
                acc[cols_ref[r * per_row + k + side]] += both[:, side * size : (side + 1) * size]

    over_rows(tiles_ref, held, sems, one_row)
    halves, count = outs[0].shape[:2]
    for g in range(GROUPS):
        for side in range(2):
            for rel in range(halves):
                owner = jnp.bitwise_xor(me, 2 * rel + side)
                start = (owner * GROUPS + g) * count
                outs[2 * g + side][rel] = acc[pl.ds(start, count)].astype(BF16)
    if first:
        loads[1].wait()
        for b in range(mask_held.shape[0]):
            mask_out[b] = mask_held[b].astype(F32).T.astype(BF16)


def spread(edge_tiles, block_cols, vals, me, rows, mask=None):
    blocks, _, size, _ = edge_tiles.shape
    first = mask is not None
    feat = vals[0].shape[2] if first else vals[0].shape[1]
    out = jax.ShapeDtypeStruct((rows // 2, blocks // GROUPS, feat, size), BF16)
    outs = [out] * (2 * GROUPS)
    scratch = [
        pltpu.VMEM((rows * blocks, feat, size), F32),
        pltpu.VMEM(edge_tiles.shape, BF16),
        pltpu.SemaphoreType.DMA((COPIES + 2,)),
    ]
    anywhere = pl.BlockSpec(memory_space=pl.ANY)
    if first:
        outs.append(jax.ShapeDtypeStruct((blocks, feat, size), BF16))
        scratch += [pltpu.VMEM(v.shape, v.dtype) for v in (vals[0], mask)]
        args, place = [vals[0], mask], anywhere
    else:
        scratch.append(pltpu.VMEM((blocks, feat, size), BF16))
        args, place = vals, VMEM
    return pl.pallas_call(
        functools.partial(spread_kernel, first, len(vals)),
        out_shape=outs,
        in_specs=[SMEM, SMEM, anywhere] + [place] * len(args),
        out_specs=[VMEM] * len(outs),
        scratch_shapes=scratch,
        compiler_params=params(48),
        cost_estimate=pl.CostEstimate(flops=2 * edge_tiles.size * feat, bytes_accessed=30_000_000, transcendentals=0),
        name="spread",
    )(block_cols, me, edge_tiles, *args)


def aggregate_kernel(cols_ref, me_ref, tiles_ref, *rest):
    parts, (out_ref, held, table, sems) = rest[:-4], rest[-4:]
    blocks, per_row = held.shape[:2]
    loads = []
    for rel, part in enumerate(parts):
        place = table.at[pl.ds(jnp.bitwise_xor(me_ref[0], rel) * blocks, blocks)]
        loads.append(pltpu.make_async_copy(part, place, sems.at[COPIES + rel]))
    for load in loads:
        load.start()
    for i in range(COPIES):
        tile_copy(tiles_ref, held, sems, i).start()
    for load in loads:
        load.wait()

    def one_row(r):
        total = None
        for k in range(0, per_row, 2):
            pair = jnp.concatenate([held[r, k], held[r, k + 1]], axis=1)
            at = r * per_row + k
            picked = jnp.concatenate([table[cols_ref[at]], table[cols_ref[at + 1]]], axis=0)
            term = jnp.dot(pair, picked, preferred_element_type=F32)
            total = term if total is None else total + term
        out_ref[r] = total.astype(BF16)

    over_rows(tiles_ref, held, sems, one_row)


def aggregate(edge_tiles, block_cols, parts, me):
    blocks, _, size, _ = edge_tiles.shape
    feat = parts[0].shape[2]
    anywhere = pl.BlockSpec(memory_space=pl.ANY)
    return pl.pallas_call(
        aggregate_kernel,
        out_shape=jax.ShapeDtypeStruct((blocks, size, feat), BF16),
        in_specs=[SMEM, SMEM, anywhere] + [anywhere] * len(parts),
        out_specs=VMEM,
        scratch_shapes=[
            pltpu.VMEM(edge_tiles.shape, BF16),
            pltpu.VMEM((len(parts) * blocks, size, feat), BF16),
            pltpu.SemaphoreType.DMA((COPIES + len(parts),)),
        ],
        compiler_params=params(48),
        cost_estimate=pl.CostEstimate(flops=2 * edge_tiles.size * feat, bytes_accessed=30_000_000, transcendentals=0),
        name="aggregate",
    )(block_cols, me, edge_tiles, *parts)


def finish_kernel(last, *refs):
    parts, rest = refs[: 2 * GROUPS], refs[2 * GROUPS :]
    out_ref = rest[3] if last else rest[0]
    count = parts[0].shape[0]
    for g in range(GROUPS):
        for b in range(count):
            total = parts[2 * g][b].astype(F32) + parts[2 * g + 1][b].astype(F32)
            out_ref[g * count + b] = (total.T if last else total).astype(BF16)
    if last:
        me_ref, value_ref, other_ref, _, first_ref, second_ref = rest
        even = jnp.bitwise_and(me_ref[0], 1) == 0
        first_ref[...] = jnp.where(even, other_ref[...], value_ref[...])
        second_ref[...] = jnp.where(even, value_ref[...], other_ref[...])


def finish(parts, grads=()):
    count, feat, size = parts[0].shape
    last = len(grads) > 0
    outs = [jax.ShapeDtypeStruct((count * GROUPS,) + ((size, feat) if last else (feat, size)), BF16)]
    outs += [jax.ShapeDtypeStruct(grad.shape, F32) for grad in grads[1:]]
    return pl.pallas_call(
        functools.partial(finish_kernel, last),
        out_shape=outs,
        in_specs=[VMEM] * len(parts) + [SMEM, VMEM, VMEM][: len(grads)],
        out_specs=[VMEM] * len(outs),
        compiler_params=params(12),
        cost_estimate=pl.CostEstimate(flops=0, bytes_accessed=1_000_000_000 if last else 1, transcendentals=0),
        name="finish",
    )(*parts, *grads)


def dense_kernel(cols, masked, pieces, col_ref, weight_ref, *rest):
    shards, rest = rest[:cols], rest[cols:]
    side_ref, rest = rest[0], rest[1:]
    if masked:
        mask_ref, rest = rest[0], rest[1:]
    outs, (grad_ref,) = rest[:pieces], rest[pieces:]
    blocks, feat, size = shards[0].shape
    per = blocks // pieces
    total = None
    for i, out in enumerate(outs):
        mine = range(i * per, (i + 1) * per)
        whole = jnp.concatenate([jnp.concatenate([shards[m][b] for b in mine], axis=1) for m in range(cols)], axis=0)
        res = jnp.dot(weight_ref[...], whole, preferred_element_type=F32)
        for k, b in enumerate(mine):
            block = res[:, k * size : (k + 1) * size]
            out[k] = (block * mask_ref[b].astype(F32) if masked else block).astype(BF16)
        side = jnp.concatenate([side_ref[b] for b in mine], axis=0)
        term = jnp.dot(whole, side, preferred_element_type=F32)
        total = term if total is None else total + term
    for m in range(cols):
        grad_ref[jnp.bitwise_xor(col_ref[0], m)] = total[m * feat : (m + 1) * feat]


def dense(weight, shards, side, mask, col, pieces):
    blocks, feat, size = shards[0].shape
    cols = len(shards)
    args = [weight, *shards, side] + ([] if mask is None else [mask])
    return pl.pallas_call(
        functools.partial(dense_kernel, cols, mask is not None, pieces),
        out_shape=[jax.ShapeDtypeStruct((blocks // pieces, feat, size), BF16)] * pieces
        + [jax.ShapeDtypeStruct((cols, feat, side.shape[2]), F32)],
        in_specs=[SMEM] + [VMEM] * len(args),
        out_specs=[VMEM] * (pieces + 1),
        compiler_params=params(16),
        name="dense",
    )(col, *args)


def dense_early_kernel(cols, late, col_ref, weight_ref, *rest):
    shards, (side_ref, mask_ref, out_ref, grad_ref, mask_out) = rest[: cols - 1], rest[cols - 1 :]
    mask_out[...] = mask_ref[...]
    blocks, feat, size = shards[0].shape
    here = [m for m in range(cols) if m != late]
    per = blocks // GROUPS
    weight = jnp.concatenate([weight_ref[:, m * feat : (m + 1) * feat] for m in here], axis=1)
    total = None
    for i in range(GROUPS):
        mine = range(i * per, (i + 1) * per)
        whole = jnp.concatenate([jnp.concatenate([shard[b] for b in mine], axis=1) for shard in shards], axis=0)
        out_ref[i] = jnp.dot(weight, whole, preferred_element_type=F32)
        term = jnp.dot(whole, jnp.concatenate([side_ref[b] for b in mine], axis=0), preferred_element_type=F32)
        total = term if total is None else total + term
    for i, m in enumerate(here):
        grad_ref[jnp.bitwise_xor(col_ref[0], m)] = total[i * feat : (i + 1) * feat]


def dense_early(weight, shards, side, mask, col, late):
    blocks, feat, size = shards[0].shape
    cols = len(shards)
    args = [weight, *(v for m, v in enumerate(shards) if m != late), side, mask]
    return pl.pallas_call(
        functools.partial(dense_early_kernel, cols, late),
        out_shape=[
            jax.ShapeDtypeStruct((GROUPS, feat, blocks // GROUPS * size), F32),
            jax.ShapeDtypeStruct((cols, feat, side.shape[2]), F32),
            jax.ShapeDtypeStruct(mask.shape, BF16),
        ],
        in_specs=[SMEM] + [VMEM] * len(args),
        out_specs=[VMEM] * 3,
        compiler_params=params(16),
        name="dense_early",
    )(col, *args)


def dense_late_kernel(late, weight_ref, shard_ref, part_ref, side_ref, mask_ref, *rest):
    outs, grad_ref = rest[:GROUPS], rest[GROUPS]
    blocks, feat, size = shard_ref.shape
    per = blocks // GROUPS
    weight = weight_ref[:, late * feat : (late + 1) * feat]
    total = None
    for i, out in enumerate(outs):
        mine = range(i * per, (i + 1) * per)
        whole = jnp.concatenate([shard_ref[b] for b in mine], axis=1)
        res = part_ref[i] + jnp.dot(weight, whole, preferred_element_type=F32)
        for k, b in enumerate(mine):
            out[k] = (res[:, k * size : (k + 1) * size] * mask_ref[b].astype(F32)).astype(BF16)
        term = jnp.dot(whole, jnp.concatenate([side_ref[b] for b in mine], axis=0), preferred_element_type=F32)
        total = term if total is None else total + term
    grad_ref[...] = total


def dense_late(weight, shard, part, side, mask, late):
    blocks, feat, size = shard.shape
    return pl.pallas_call(
        functools.partial(dense_late_kernel, late),
        out_shape=[jax.ShapeDtypeStruct((blocks // GROUPS, feat, size), BF16)] * GROUPS
        + [jax.ShapeDtypeStruct((feat, side.shape[2]), F32)],
        in_specs=[VMEM] * 5,
        out_specs=[VMEM] * (GROUPS + 1),
        compiler_params=params(16),
        name="dense_late",
    )(weight, shard, part, side, mask)


def weight_terms_kernel(late, me_ref, col_ref, second_ref, late_ref, *refs):
    firsts, (keep_ref, send_ref, held) = refs[:-3], refs[-3:]
    cols = second_ref.shape[0]
    even = jnp.bitwise_and(me_ref[0], 1) == 0
    held[...] = second_ref[...]
    held[jnp.bitwise_xor(col_ref[0], late)] = late_ref[...]
    first = jnp.concatenate([sum(r[q] for r in firsts) for q in range(cols)], axis=0).T
    second = jnp.concatenate([held[q] for q in range(cols)], axis=0).T
    keep_ref[...] = jnp.where(even, second, first)
    send_ref[...] = jnp.where(even, first, second).astype(BF16)


def weight_terms(firsts, second, last, me, col, late):
    cols, feat, width = second.shape
    shape = (width, cols * feat)
    return pl.pallas_call(
        functools.partial(weight_terms_kernel, late),
        out_shape=[jax.ShapeDtypeStruct(shape, F32), jax.ShapeDtypeStruct(shape, BF16)],
        in_specs=[SMEM, SMEM] + [VMEM] * (2 + len(firsts)),
        out_specs=[VMEM] * 2,
        scratch_shapes=[pltpu.VMEM(second.shape, F32)],
        compiler_params=params(8),
        name="weight_terms",
    )(me, col, second, last, *firsts)


def swap(value, mask, axis):
    return lax.ppermute(value, axis, [(i, i ^ mask) for i in range(lax.axis_size(axis))])


def add(a, b):
    return (a.astype(F32) + b.astype(F32)).astype(BF16)


def scatter(pieces, rows, value=None):
    chips = [1 << b for b in range(1, rows.bit_length() - 1)]
    shape = (2,) * len(chips) + pieces[0].shape[1:]
    keeps = [pieces[2 * g].reshape(shape) for g in range(GROUPS)]
    gots = [swap(pieces[2 * g + 1], 1, "row").reshape(shape) for g in range(GROUPS)]
    orders = [chips if g % 2 else chips[::-1] for g in range(GROUPS)]
    lefts = [chips[::-1] for _ in range(GROUPS)]
    for level in range(len(chips)):
        masks = [order[level] for order in orders]
        sent = []
        for g in range(GROUPS):
            axis = lefts[g].index(masks[g])
            lefts[g] = [m for m in lefts[g] if m != masks[g]]
            half = lambda v, i: lax.index_in_dim(v, i, axis, keepdims=False)
            sent.append(add(half(keeps[g], 1), half(gots[g], 1)))
            keeps[g] = add(half(keeps[g], 0), half(gots[g], 0))
        if value is not None:
            keeps, value = lax.optimization_barrier((keeps, value))
        gots = [swap(sent[g], masks[g], "row") for g in range(GROUPS)]
        if value is not None:
            value = value.astype(BF16)
            value = value.astype(F32) + swap(value, chips[-1 - level], "row").astype(F32)
            if level < len(chips) - 1:
                gots, value = lax.optimization_barrier((gots, value))
    return [t for pair in zip(keeps, gots) for t in pair], value


def gather_columns(own, cols, beside=(), tied=True):
    if cols == 4:
        near, far = swap(own, 1, "col"), swap(own, 3, "col")
        if tied:
            far, near, beside = lax.optimization_barrier((far, near, beside))
        else:
            near, beside = lax.optimization_barrier((near, beside))
        return [own, near, swap(far, 1, "col"), far], beside
    return [own] + [swap(own, m, "col") for m in range(1, cols)], beside


def per_device(
    node_feats, hidden_act, grad_out, relu_mask, edge_tiles, block_cols, weight_one, weight_two
):
    rows, cols = lax.axis_size("row"), lax.axis_size("col")
    me, col = lax.axis_index("row").astype(jnp.int32), lax.axis_index("col").astype(jnp.int32)
    me_at, col_at = me.reshape(1), col.reshape(1)
    size = edge_tiles.shape[2]
    per = edge_tiles.shape[0] // GROUPS
    cut = lambda v, g: v[g * per : (g + 1) * per]
    blocked = lambda v: v.reshape(v.shape[0] // size, size, v.shape[1])
    after = lax.optimization_barrier

    def by_distance(weight):
        split = weight.reshape(weight.shape[0], cols, weight.shape[1] // cols)
        order = [lax.dynamic_index_in_dim(split, col ^ m, 1, keepdims=False) for m in range(cols)]
        return jnp.concatenate(order, axis=1)

    block_cols = block_cols.reshape(-1)
    *pieces, mask = spread(edge_tiles, block_cols, [blocked(grad_out)], me_at, rows, blocked(relu_mask))
    terms, _ = scatter(pieces, rows)
    own, node_feats = after((finish(terms)[0], blocked(node_feats)))
    own, weight_one, weight_two = after((own, weight_one, weight_two))
    weight_one, weight_two = by_distance(weight_one), by_distance(weight_two)
    parts = [node_feats] + [swap(node_feats, rel, "row") for rel in range(2, rows, 2)]
    shards, parts[0] = gather_columns(own, cols, node_feats, False)
    parts = [v for part in parts for v in (part, swap(part, 1, "row"))]
    late = 2
    hidden = blocked(hidden_act)
    part, second, mask = dense_early(weight_two, shards, hidden, mask, col_at, late)
    arrived, parts = after((shards[late], parts))
    *deltas, last = dense_late(weight_two, arrived, part, hidden, mask, late)
    deltas[0], parts = after((deltas[0], parts))
    agg_feats = aggregate(edge_tiles, block_cols, parts, me_at)
    inputs, firsts = [], []
    shards = []
    for g in range(GROUPS):
        arrived, beside = gather_columns(deltas[g], cols, agg_feats if g == 0 else ())
        agg_feats = beside if g == 0 else agg_feats
        shards.append(arrived)
    for g in range(GROUPS):
        out, grad = dense(weight_one, shards[g], cut(agg_feats, g), None, col_at, 1)
        inputs.append(out)
        firsts.append(grad)
    pieces = spread(edge_tiles, block_cols, inputs, me_at, rows)
    keep, send = weight_terms(firsts, second, last, me_at, col_at, late)
    terms, value = scatter(pieces, rows, keep + swap(send, 1, "row").astype(F32))
    grads = [me_at, value, swap(value, 1, "row")]
    out, first_grad, second_grad = finish(terms, grads)
    return out.reshape(-1, out.shape[2]), first_grad, second_grad


def solution(mesh):
    in_specs = (
        P("row", "col"),
        P("row", "col"),
        P("row", "col"),
        P("row", "col"),
        P("row", None, None, None),
        P("row", None),
        P("col", None),
        P("col", None),
    )
    out_specs = (P("row", "col"), P("col", None), P("col", None))
    return jax.shard_map(
        per_device, mesh=mesh, in_specs=in_specs, out_specs=out_specs, check_vma=False
    )
```

```python
import functools

import jax
import jax.numpy as jnp
from jax import lax
from jax.experimental import pallas as pl
from jax.experimental.pallas import tpu as pltpu
from jax.sharding import PartitionSpec as P

GROUPS = 2
COPIES = 4
F32 = jnp.float32
BF16 = jnp.bfloat16
VMEM = pl.BlockSpec(memory_space=pltpu.VMEM)
SMEM = pl.BlockSpec(memory_space=pltpu.SMEM)


def params(mib):
    return pltpu.CompilerParams(vmem_limit_bytes=mib * 1024 * 1024)


def tile_copy(tiles_ref, held, sems, i):
    per = held.shape[0] // COPIES
    part = pl.ds(i * per, per)
    return pltpu.make_async_copy(tiles_ref.at[part], held.at[part], sems.at[i])


def over_rows(tiles_ref, held, sems, one_row):
    per = held.shape[0] // COPIES

    def piece(i, carry):
        tile_copy(tiles_ref, held, sems, i).wait()
        for j in range(per):
            one_row(i * per + j)
        return carry

    lax.fori_loop(0, COPIES, piece, 0)


def spread_kernel(first, pieces, cols_ref, me_ref, tiles_ref, *rest):
    vals, rest = rest[:pieces], rest[pieces:]
    if first:
        mask_ref, *rest = rest
        outs, (mask_out, acc, held, sems, left_ref, mask_held) = rest[: 2 * GROUPS], rest[2 * GROUPS :]
        loads = [
            pltpu.make_async_copy(vals[0], left_ref, sems.at[COPIES]),
            pltpu.make_async_copy(mask_ref, mask_held, sems.at[COPIES + 1]),
        ]
        loads[0].start()
    else:
        outs, (acc, held, sems, left_ref) = rest[: 2 * GROUPS], rest[2 * GROUPS :]
    for i in range(COPIES):
        tile_copy(tiles_ref, held, sems, i).start()
    if first:
        loads[1].start()
    acc[...] = jnp.zeros_like(acc)
    per_row, size = held.shape[1], held.shape[3]
    me = me_ref[0]
    if first:
        loads[0].wait()
    else:
        for g in range(pieces):
            count = vals[g].shape[0]
            left_ref[g * count : (g + 1) * count] = vals[g][...]

    def one_row(r):
        left = left_ref[r].astype(F32).T.astype(BF16) if first else left_ref[r]
        for k in range(0, per_row, 2):
            pair = jnp.concatenate([held[r, k], held[r, k + 1]], axis=1)
            both = jnp.dot(left, pair, preferred_element_type=F32)
            for side in range(2):
                acc[cols_ref[r * per_row + k + side]] += both[:, side * size : (side + 1) * size]

    over_rows(tiles_ref, held, sems, one_row)
    halves, count = outs[0].shape[:2]
    for g in range(GROUPS):
        for side in range(2):
            for rel in range(halves):
                owner = jnp.bitwise_xor(me, 2 * rel + side)
                start = (owner * GROUPS + g) * count
                outs[2 * g + side][rel] = acc[pl.ds(start, count)].astype(BF16)
    if first:
        loads[1].wait()
        for b in range(mask_held.shape[0]):
            mask_out[b] = mask_held[b].astype(F32).T.astype(BF16)


def spread(edge_tiles, block_cols, vals, me, rows, mask=None):
    blocks, _, size, _ = edge_tiles.shape
    first = mask is not None
    feat = vals[0].shape[2] if first else vals[0].shape[1]
    out = jax.ShapeDtypeStruct((rows // 2, blocks // GROUPS, feat, size), BF16)
    outs = [out] * (2 * GROUPS)
    scratch = [
        pltpu.VMEM((rows * blocks, feat, size), F32),
        pltpu.VMEM(edge_tiles.shape, BF16),
        pltpu.SemaphoreType.DMA((COPIES + 2,)),
    ]
    anywhere = pl.BlockSpec(memory_space=pl.ANY)
    if first:
        outs.append(jax.ShapeDtypeStruct((blocks, feat, size), BF16))
        scratch += [pltpu.VMEM(v.shape, v.dtype) for v in (vals[0], mask)]
        args, place = [vals[0], mask], anywhere
    else:
        scratch.append(pltpu.VMEM((blocks, feat, size), BF16))
        args, place = vals, VMEM
    return pl.pallas_call(
        functools.partial(spread_kernel, first, len(vals)),
        out_shape=outs,
        in_specs=[SMEM, SMEM, anywhere] + [place] * len(args),
        out_specs=[VMEM] * len(outs),
        scratch_shapes=scratch,
        compiler_params=params(48),
        cost_estimate=pl.CostEstimate(flops=2 * edge_tiles.size * feat, bytes_accessed=30_000_000, transcendentals=0),
        name="spread",
    )(block_cols, me, edge_tiles, *args)


def aggregate_kernel(cols_ref, me_ref, tiles_ref, *rest):
    parts, (out_ref, held, table, sems) = rest[:-4], rest[-4:]
    blocks, per_row = held.shape[:2]
    loads = []
    for rel, part in enumerate(parts):
        place = table.at[pl.ds(jnp.bitwise_xor(me_ref[0], rel) * blocks, blocks)]
        loads.append(pltpu.make_async_copy(part, place, sems.at[COPIES + rel]))
    for load in loads:
        load.start()
    for i in range(COPIES):
        tile_copy(tiles_ref, held, sems, i).start()
    for load in loads:
        load.wait()

    def one_row(r):
        total = None
        for k in range(0, per_row, 2):
            pair = jnp.concatenate([held[r, k], held[r, k + 1]], axis=1)
            at = r * per_row + k
            picked = jnp.concatenate([table[cols_ref[at]], table[cols_ref[at + 1]]], axis=0)
            term = jnp.dot(pair, picked, preferred_element_type=F32)
            total = term if total is None else total + term
        out_ref[r] = total.astype(BF16)

    over_rows(tiles_ref, held, sems, one_row)


def aggregate(edge_tiles, block_cols, parts, me):
    blocks, _, size, _ = edge_tiles.shape
    feat = parts[0].shape[2]
    anywhere = pl.BlockSpec(memory_space=pl.ANY)
    return pl.pallas_call(
        aggregate_kernel,
        out_shape=jax.ShapeDtypeStruct((blocks, size, feat), BF16),
        in_specs=[SMEM, SMEM, anywhere] + [anywhere] * len(parts),
        out_specs=VMEM,
        scratch_shapes=[
            pltpu.VMEM(edge_tiles.shape, BF16),
            pltpu.VMEM((len(parts) * blocks, size, feat), BF16),
            pltpu.SemaphoreType.DMA((COPIES + len(parts),)),
        ],
        compiler_params=params(48),
        cost_estimate=pl.CostEstimate(flops=2 * edge_tiles.size * feat, bytes_accessed=30_000_000, transcendentals=0),
        name="aggregate",
    )(block_cols, me, edge_tiles, *parts)


def finish_kernel(last, *refs):
    parts, rest = refs[: 2 * GROUPS], refs[2 * GROUPS :]
    out_ref = rest[3] if last else rest[0]
    count = parts[0].shape[0]
    for g in range(GROUPS):
        for b in range(count):
            total = parts[2 * g][b].astype(F32) + parts[2 * g + 1][b].astype(F32)
            out_ref[g * count + b] = (total.T if last else total).astype(BF16)
    if last:
        me_ref, value_ref, other_ref, _, first_ref, second_ref = rest
        even = jnp.bitwise_and(me_ref[0], 1) == 0
        first_ref[...] = jnp.where(even, other_ref[...], value_ref[...])
        second_ref[...] = jnp.where(even, value_ref[...], other_ref[...])


def finish(parts, grads=()):
    count, feat, size = parts[0].shape
    last = len(grads) > 0
    outs = [jax.ShapeDtypeStruct((count * GROUPS,) + ((size, feat) if last else (feat, size)), BF16)]
    outs += [jax.ShapeDtypeStruct(grad.shape, F32) for grad in grads[1:]]
    return pl.pallas_call(
        functools.partial(finish_kernel, last),
        out_shape=outs,
        in_specs=[VMEM] * len(parts) + [SMEM, VMEM, VMEM][: len(grads)],
        out_specs=[VMEM] * len(outs),
        compiler_params=params(12),
        cost_estimate=pl.CostEstimate(flops=0, bytes_accessed=1_000_000_000 if last else 1, transcendentals=0),
        name="finish",
    )(*parts, *grads)


def dense_kernel(cols, masked, pieces, col_ref, weight_ref, *rest):
    shards, rest = rest[:cols], rest[cols:]
    side_ref, rest = rest[0], rest[1:]
    if masked:
        mask_ref, rest = rest[0], rest[1:]
    outs, (grad_ref,) = rest[:pieces], rest[pieces:]
    blocks, feat, size = shards[0].shape
    per = blocks // pieces
    total = None
    for i, out in enumerate(outs):
        mine = range(i * per, (i + 1) * per)
        whole = jnp.concatenate([jnp.concatenate([shards[m][b] for b in mine], axis=1) for m in range(cols)], axis=0)
        res = jnp.dot(weight_ref[...], whole, preferred_element_type=F32)
        for k, b in enumerate(mine):
            block = res[:, k * size : (k + 1) * size]
            out[k] = (block * mask_ref[b].astype(F32) if masked else block).astype(BF16)
        side = jnp.concatenate([side_ref[b] for b in mine], axis=0)
        term = jnp.dot(whole, side, preferred_element_type=F32)
        total = term if total is None else total + term
    for m in range(cols):
        grad_ref[jnp.bitwise_xor(col_ref[0], m)] = total[m * feat : (m + 1) * feat]


def dense(weight, shards, side, mask, col, pieces):
    blocks, feat, size = shards[0].shape
    cols = len(shards)
    args = [weight, *shards, side] + ([] if mask is None else [mask])
    return pl.pallas_call(
        functools.partial(dense_kernel, cols, mask is not None, pieces),
        out_shape=[jax.ShapeDtypeStruct((blocks // pieces, feat, size), BF16)] * pieces
        + [jax.ShapeDtypeStruct((cols, feat, side.shape[2]), F32)],
        in_specs=[SMEM] + [VMEM] * len(args),
        out_specs=[VMEM] * (pieces + 1),
        compiler_params=params(16),
        name="dense",
    )(col, *args)


def dense_early_kernel(cols, late, col_ref, weight_ref, *rest):
    shards, (side_ref, mask_ref, out_ref, grad_ref, mask_out) = rest[: cols - 1], rest[cols - 1 :]
    mask_out[...] = mask_ref[...]
    blocks, feat, size = shards[0].shape
    here = [m for m in range(cols) if m != late]
    per = blocks // GROUPS
    weight = jnp.concatenate([weight_ref[:, m * feat : (m + 1) * feat] for m in here], axis=1)
    total = None
    for i in range(GROUPS):
        mine = range(i * per, (i + 1) * per)
        whole = jnp.concatenate([jnp.concatenate([shard[b] for b in mine], axis=1) for shard in shards], axis=0)
        out_ref[i] = jnp.dot(weight, whole, preferred_element_type=F32)
        term = jnp.dot(whole, jnp.concatenate([side_ref[b] for b in mine], axis=0), preferred_element_type=F32)
        total = term if total is None else total + term
    for i, m in enumerate(here):
        grad_ref[jnp.bitwise_xor(col_ref[0], m)] = total[i * feat : (i + 1) * feat]


def dense_early(weight, shards, side, mask, col, late):
    blocks, feat, size = shards[0].shape
    cols = len(shards)
    args = [weight, *(v for m, v in enumerate(shards) if m != late), side, mask]
    return pl.pallas_call(
        functools.partial(dense_early_kernel, cols, late),
        out_shape=[
            jax.ShapeDtypeStruct((GROUPS, feat, blocks // GROUPS * size), F32),
            jax.ShapeDtypeStruct((cols, feat, side.shape[2]), F32),
            jax.ShapeDtypeStruct(mask.shape, BF16),
        ],
        in_specs=[SMEM] + [VMEM] * len(args),
        out_specs=[VMEM] * 3,
        compiler_params=params(16),
        name="dense_early",
    )(col, *args)


def dense_late_kernel(late, weight_ref, shard_ref, part_ref, side_ref, mask_ref, *rest):
    outs, grad_ref = rest[:GROUPS], rest[GROUPS]
    blocks, feat, size = shard_ref.shape
    per = blocks // GROUPS
    weight = weight_ref[:, late * feat : (late + 1) * feat]
    total = None
    for i, out in enumerate(outs):
        mine = range(i * per, (i + 1) * per)
        whole = jnp.concatenate([shard_ref[b] for b in mine], axis=1)
        res = part_ref[i] + jnp.dot(weight, whole, preferred_element_type=F32)
        for k, b in enumerate(mine):
            out[k] = (res[:, k * size : (k + 1) * size] * mask_ref[b].astype(F32)).astype(BF16)
        term = jnp.dot(whole, jnp.concatenate([side_ref[b] for b in mine], axis=0), preferred_element_type=F32)
        total = term if total is None else total + term
    grad_ref[...] = total


def dense_late(weight, shard, part, side, mask, late):
    blocks, feat, size = shard.shape
    return pl.pallas_call(
        functools.partial(dense_late_kernel, late),
        out_shape=[jax.ShapeDtypeStruct((blocks // GROUPS, feat, size), BF16)] * GROUPS
        + [jax.ShapeDtypeStruct((feat, side.shape[2]), F32)],
        in_specs=[VMEM] * 5,
        out_specs=[VMEM] * (GROUPS + 1),
        compiler_params=params(16),
        name="dense_late",
    )(weight, shard, part, side, mask)


def weight_terms_kernel(late, me_ref, col_ref, second_ref, late_ref, *refs):
    firsts, (keep_ref, send_ref, held) = refs[:-3], refs[-3:]
    cols = second_ref.shape[0]
    even = jnp.bitwise_and(me_ref[0], 1) == 0
    held[...] = second_ref[...]
    held[jnp.bitwise_xor(col_ref[0], late)] = late_ref[...]
    first = jnp.concatenate([sum(r[q] for r in firsts) for q in range(cols)], axis=0).T
    second = jnp.concatenate([held[q] for q in range(cols)], axis=0).T
    keep_ref[...] = jnp.where(even, second, first)
    send_ref[...] = jnp.where(even, first, second).astype(BF16)


def weight_terms(firsts, second, last, me, col, late):
    cols, feat, width = second.shape
    shape = (width, cols * feat)
    return pl.pallas_call(
        functools.partial(weight_terms_kernel, late),
        out_shape=[jax.ShapeDtypeStruct(shape, F32), jax.ShapeDtypeStruct(shape, BF16)],
        in_specs=[SMEM, SMEM] + [VMEM] * (2 + len(firsts)),
        out_specs=[VMEM] * 2,
        scratch_shapes=[pltpu.VMEM(second.shape, F32)],
        compiler_params=params(8),
        name="weight_terms",
    )(me, col, second, last, *firsts)


def swap(value, mask, axis):
    return lax.ppermute(value, axis, [(i, i ^ mask) for i in range(lax.axis_size(axis))])


def add(a, b):
    return (a.astype(F32) + b.astype(F32)).astype(BF16)


def scatter(pieces, rows, value=None):
    chips = [1 << b for b in range(1, rows.bit_length() - 1)]
    shape = (2,) * len(chips) + pieces[0].shape[1:]
    keeps = [pieces[2 * g].reshape(shape) for g in range(GROUPS)]
    gots = [swap(pieces[2 * g + 1], 1, "row").reshape(shape) for g in range(GROUPS)]
    orders = [chips if g % 2 else chips[::-1] for g in range(GROUPS)]
    lefts = [chips[::-1] for _ in range(GROUPS)]
    for level in range(len(chips)):
        masks = [order[level] for order in orders]
        sent = []
        for g in range(GROUPS):
            axis = lefts[g].index(masks[g])
            lefts[g] = [m for m in lefts[g] if m != masks[g]]
            half = lambda v, i: lax.index_in_dim(v, i, axis, keepdims=False)
            sent.append(add(half(keeps[g], 1), half(gots[g], 1)))
            keeps[g] = add(half(keeps[g], 0), half(gots[g], 0))
        if value is not None:
            keeps, value = lax.optimization_barrier((keeps, value))
        gots = [swap(sent[g], masks[g], "row") for g in range(GROUPS)]
        if value is not None:
            value = value.astype(BF16)
            value = value.astype(F32) + swap(value, chips[-1 - level], "row").astype(F32)
            if level < len(chips) - 1:
                gots, value = lax.optimization_barrier((gots, value))
    return [t for pair in zip(keeps, gots) for t in pair], value


def gather_columns(own, cols, beside=(), tied=True):
    if cols == 4:
        near, far = swap(own, 1, "col"), swap(own, 3, "col")
        if tied:
            far, near, beside = lax.optimization_barrier((far, near, beside))
        else:
            near, beside = lax.optimization_barrier((near, beside))
        return [own, near, swap(far, 1, "col"), far], beside
    return [own] + [swap(own, m, "col") for m in range(1, cols)], beside


def per_device(
    node_feats, hidden_act, grad_out, relu_mask, edge_tiles, block_cols, weight_one, weight_two
):
    rows, cols = lax.axis_size("row"), lax.axis_size("col")
    me, col = lax.axis_index("row").astype(jnp.int32), lax.axis_index("col").astype(jnp.int32)
    me_at, col_at = me.reshape(1), col.reshape(1)
    size = edge_tiles.shape[2]
    per = edge_tiles.shape[0] // GROUPS
    cut = lambda v, g: v[g * per : (g + 1) * per]
    blocked = lambda v: v.reshape(v.shape[0] // size, size, v.shape[1])
    after = lax.optimization_barrier

    def by_distance(weight):
        split = weight.reshape(weight.shape[0], cols, weight.shape[1] // cols)
        order = [lax.dynamic_index_in_dim(split, col ^ m, 1, keepdims=False) for m in range(cols)]
        return jnp.concatenate(order, axis=1)

    block_cols = block_cols.reshape(-1)
    *pieces, mask = spread(edge_tiles, block_cols, [blocked(grad_out)], me_at, rows, blocked(relu_mask))
    terms, _ = scatter(pieces, rows)
    own, node_feats = after((finish(terms)[0], blocked(node_feats)))
    own, weight_one, weight_two = after((own, weight_one, weight_two))
    weight_one, weight_two = by_distance(weight_one), by_distance(weight_two)
    parts = [node_feats] + [swap(node_feats, rel, "row") for rel in range(2, rows, 2)]
    shards, parts[0] = gather_columns(own, cols, node_feats, False)
    parts = [v for part in parts for v in (part, swap(part, 1, "row"))]
    late = 2
    hidden = blocked(hidden_act)
    part, second, mask = dense_early(weight_two, shards, hidden, mask, col_at, late)
    arrived, parts = after((shards[late], parts))
    *deltas, last = dense_late(weight_two, arrived, part, hidden, mask, late)
    deltas[0], parts = after((deltas[0], parts))
    agg_feats = aggregate(edge_tiles, block_cols, parts, me_at)
    inputs, firsts = [], []
    shards = []
    for g in range(GROUPS):
        arrived, beside = gather_columns(deltas[g], cols, agg_feats if g == 0 else (), g == 0)
        agg_feats = beside if g == 0 else agg_feats
        shards.append(arrived)
    shards[0][2], shards[1][1] = after((shards[0][2], shards[1][1]))
    for g in range(GROUPS):
        out, grad = dense(weight_one, shards[g], cut(agg_feats, g), None, col_at, 1)
        inputs.append(out)
        firsts.append(grad)
    pieces = spread(edge_tiles, block_cols, inputs, me_at, rows)
    keep, send = weight_terms(firsts, second, last, me_at, col_at, late)
    terms, value = scatter(pieces, rows, keep + swap(send, 1, "row").astype(F32))
    grads = [me_at, value, swap(value, 1, "row")]
    out, first_grad, second_grad = finish(terms, grads)
    return out.reshape(-1, out.shape[2]), first_grad, second_grad


def solution(mesh):
    in_specs = (
        P("row", "col"),
        P("row", "col"),
        P("row", "col"),
        P("row", "col"),
        P("row", None, None, None),
        P("row", None),
        P("col", None),
        P("col", None),
    )
    out_specs = (P("row", "col"), P("col", None), P("col", None))
    return jax.shard_map(
        per_device, mesh=mesh, in_specs=in_specs, out_specs=out_specs, check_vma=False
    )
```

```python
import functools

import jax
import jax.numpy as jnp
from jax import lax
from jax.experimental import pallas as pl
from jax.experimental.pallas import tpu as pltpu
from jax.sharding import PartitionSpec as P

GROUPS = 2
COPIES = 2
F32 = jnp.float32
BF16 = jnp.bfloat16
VMEM = pl.BlockSpec(memory_space=pltpu.VMEM)
SMEM = pl.BlockSpec(memory_space=pltpu.SMEM)


def params(mib):
    return pltpu.CompilerParams(vmem_limit_bytes=mib * 1024 * 1024)


def tile_copy(tiles_ref, held, sems, i):
    per = held.shape[0] // COPIES
    part = pl.ds(i * per, per)
    return pltpu.make_async_copy(tiles_ref.at[part], held.at[part], sems.at[i])


def over_rows(tiles_ref, held, sems, one_row):
    per = held.shape[0] // COPIES

    def piece(i, carry):
        tile_copy(tiles_ref, held, sems, i).wait()
        for j in range(per):
            one_row(i * per + j)
        return carry

    lax.fori_loop(0, COPIES, piece, 0)


def spread_kernel(first, pieces, cols_ref, me_ref, tiles_ref, *rest):
    vals, rest = rest[:pieces], rest[pieces:]
    if first:
        mask_ref, *rest = rest
        outs, (mask_out, acc, held, sems, left_ref, mask_held) = rest[: 2 * GROUPS], rest[2 * GROUPS :]
        loads = [
            pltpu.make_async_copy(vals[0], left_ref, sems.at[COPIES]),
            pltpu.make_async_copy(mask_ref, mask_held, sems.at[COPIES + 1]),
        ]
        loads[0].start()
    else:
        outs, (acc, held, sems, left_ref) = rest[: 2 * GROUPS], rest[2 * GROUPS :]
    for i in range(COPIES):
        tile_copy(tiles_ref, held, sems, i).start()
    if first:
        loads[1].start()
    acc[...] = jnp.zeros_like(acc)
    per_row, size = held.shape[1], held.shape[3]
    me = me_ref[0]
    if first:
        loads[0].wait()
    else:
        for g in range(pieces):
            count = vals[g].shape[0]
            left_ref[g * count : (g + 1) * count] = vals[g][...]

    def one_row(r):
        left = left_ref[r].astype(F32).T.astype(BF16) if first else left_ref[r]
        for k in range(0, per_row, 2):
            pair = jnp.concatenate([held[r, k], held[r, k + 1]], axis=1)
            both = jnp.dot(left, pair, preferred_element_type=F32)
            for side in range(2):
                acc[cols_ref[r * per_row + k + side]] += both[:, side * size : (side + 1) * size]

    over_rows(tiles_ref, held, sems, one_row)
    halves, count = outs[0].shape[:2]
    for g in range(GROUPS):
        for side in range(2):
            for rel in range(halves):
                owner = jnp.bitwise_xor(me, 2 * rel + side)
                start = (owner * GROUPS + g) * count
                outs[2 * g + side][rel] = acc[pl.ds(start, count)].astype(BF16)
    if first:
        loads[1].wait()
        for b in range(mask_held.shape[0]):
            mask_out[b] = mask_held[b].astype(F32).T.astype(BF16)


def spread(edge_tiles, block_cols, vals, me, rows, mask=None):
    blocks, _, size, _ = edge_tiles.shape
    first = mask is not None
    feat = vals[0].shape[2] if first else vals[0].shape[1]
    out = jax.ShapeDtypeStruct((rows // 2, blocks // GROUPS, feat, size), BF16)
    outs = [out] * (2 * GROUPS)
    scratch = [
        pltpu.VMEM((rows * blocks, feat, size), F32),
        pltpu.VMEM(edge_tiles.shape, BF16),
        pltpu.SemaphoreType.DMA((COPIES + 2,)),
    ]
    anywhere = pl.BlockSpec(memory_space=pl.ANY)
    if first:
        outs.append(jax.ShapeDtypeStruct((blocks, feat, size), BF16))
        scratch += [pltpu.VMEM(v.shape, v.dtype) for v in (vals[0], mask)]
        args, place = [vals[0], mask], anywhere
    else:
        scratch.append(pltpu.VMEM((blocks, feat, size), BF16))
        args, place = vals, VMEM
    return pl.pallas_call(
        functools.partial(spread_kernel, first, len(vals)),
        out_shape=outs,
        in_specs=[SMEM, SMEM, anywhere] + [place] * len(args),
        out_specs=[VMEM] * len(outs),
        scratch_shapes=scratch,
        compiler_params=params(48),
        cost_estimate=pl.CostEstimate(flops=2 * edge_tiles.size * feat, bytes_accessed=30_000_000, transcendentals=0),
        name="spread",
    )(block_cols, me, edge_tiles, *args)


def aggregate_kernel(cols_ref, me_ref, tiles_ref, *rest):
    parts, (out_ref, held, table, sems) = rest[:-4], rest[-4:]
    blocks, per_row = held.shape[:2]
    loads = []
    for rel, part in enumerate(parts):
        place = table.at[pl.ds(jnp.bitwise_xor(me_ref[0], rel) * blocks, blocks)]
        loads.append(pltpu.make_async_copy(part, place, sems.at[COPIES + rel]))
    for load in loads:
        load.start()
    for i in range(COPIES):
        tile_copy(tiles_ref, held, sems, i).start()
    for load in loads:
        load.wait()

    def one_row(r):
        total = None
        for k in range(0, per_row, 2):
            pair = jnp.concatenate([held[r, k], held[r, k + 1]], axis=1)
            at = r * per_row + k
            picked = jnp.concatenate([table[cols_ref[at]], table[cols_ref[at + 1]]], axis=0)
            term = jnp.dot(pair, picked, preferred_element_type=F32)
            total = term if total is None else total + term
        out_ref[r] = total.astype(BF16)

    over_rows(tiles_ref, held, sems, one_row)


def aggregate(edge_tiles, block_cols, parts, me):
    blocks, _, size, _ = edge_tiles.shape
    feat = parts[0].shape[2]
    anywhere = pl.BlockSpec(memory_space=pl.ANY)
    return pl.pallas_call(
        aggregate_kernel,
        out_shape=jax.ShapeDtypeStruct((blocks, size, feat), BF16),
        in_specs=[SMEM, SMEM, anywhere] + [anywhere] * len(parts),
        out_specs=VMEM,
        scratch_shapes=[
            pltpu.VMEM(edge_tiles.shape, BF16),
            pltpu.VMEM((len(parts) * blocks, size, feat), BF16),
            pltpu.SemaphoreType.DMA((COPIES + len(parts),)),
        ],
        compiler_params=params(48),
        cost_estimate=pl.CostEstimate(flops=2 * edge_tiles.size * feat, bytes_accessed=30_000_000, transcendentals=0),
        name="aggregate",
    )(block_cols, me, edge_tiles, *parts)


def finish_kernel(last, *refs):
    parts, rest = refs[: 2 * GROUPS], refs[2 * GROUPS :]
    out_ref = rest[3] if last else rest[0]
    count = parts[0].shape[0]
    for g in range(GROUPS):
        for b in range(count):
            total = parts[2 * g][b].astype(F32) + parts[2 * g + 1][b].astype(F32)
            out_ref[g * count + b] = (total.T if last else total).astype(BF16)
    if last:
        me_ref, value_ref, other_ref, _, first_ref, second_ref = rest
        even = jnp.bitwise_and(me_ref[0], 1) == 0
        first_ref[...] = jnp.where(even, other_ref[...], value_ref[...])
        second_ref[...] = jnp.where(even, value_ref[...], other_ref[...])


def finish(parts, grads=()):
    count, feat, size = parts[0].shape
    last = len(grads) > 0
    outs = [jax.ShapeDtypeStruct((count * GROUPS,) + ((size, feat) if last else (feat, size)), BF16)]
    outs += [jax.ShapeDtypeStruct(grad.shape, F32) for grad in grads[1:]]
    return pl.pallas_call(
        functools.partial(finish_kernel, last),
        out_shape=outs,
        in_specs=[VMEM] * len(parts) + [SMEM, VMEM, VMEM][: len(grads)],
        out_specs=[VMEM] * len(outs),
        compiler_params=params(12),
        cost_estimate=pl.CostEstimate(flops=0, bytes_accessed=1_000_000_000 if last else 1, transcendentals=0),
        name="finish",
    )(*parts, *grads)


def dense_kernel(cols, masked, pieces, col_ref, weight_ref, *rest):
    shards, rest = rest[:cols], rest[cols:]
    side_ref, rest = rest[0], rest[1:]
    if masked:
        mask_ref, rest = rest[0], rest[1:]
    outs, (grad_ref,) = rest[:pieces], rest[pieces:]
    blocks, feat, size = shards[0].shape
    per = blocks // pieces
    total = None
    for i, out in enumerate(outs):
        mine = range(i * per, (i + 1) * per)
        whole = jnp.concatenate([jnp.concatenate([shards[m][b] for b in mine], axis=1) for m in range(cols)], axis=0)
        res = jnp.dot(weight_ref[...], whole, preferred_element_type=F32)
        for k, b in enumerate(mine):
            block = res[:, k * size : (k + 1) * size]
            out[k] = (block * mask_ref[b].astype(F32) if masked else block).astype(BF16)
        side = jnp.concatenate([side_ref[b] for b in mine], axis=0)
        term = jnp.dot(whole, side, preferred_element_type=F32)
        total = term if total is None else total + term
    for m in range(cols):
        grad_ref[jnp.bitwise_xor(col_ref[0], m)] = total[m * feat : (m + 1) * feat]


def dense(weight, shards, side, mask, col, pieces):
    blocks, feat, size = shards[0].shape
    cols = len(shards)
    args = [weight, *shards, side] + ([] if mask is None else [mask])
    return pl.pallas_call(
        functools.partial(dense_kernel, cols, mask is not None, pieces),
        out_shape=[jax.ShapeDtypeStruct((blocks // pieces, feat, size), BF16)] * pieces
        + [jax.ShapeDtypeStruct((cols, feat, side.shape[2]), F32)],
        in_specs=[SMEM] + [VMEM] * len(args),
        out_specs=[VMEM] * (pieces + 1),
        compiler_params=params(16),
        name="dense",
    )(col, *args)


def dense_early_kernel(cols, late, col_ref, weight_ref, *rest):
    shards, (side_ref, mask_ref, out_ref, grad_ref, mask_out) = rest[: cols - 1], rest[cols - 1 :]
    mask_out[...] = mask_ref[...]
    blocks, feat, size = shards[0].shape
    here = [m for m in range(cols) if m != late]
    per = blocks // GROUPS
    weight = jnp.concatenate([weight_ref[:, m * feat : (m + 1) * feat] for m in here], axis=1)
    total = None
    for i in range(GROUPS):
        mine = range(i * per, (i + 1) * per)
        whole = jnp.concatenate([jnp.concatenate([shard[b] for b in mine], axis=1) for shard in shards], axis=0)
        out_ref[i] = jnp.dot(weight, whole, preferred_element_type=F32)
        term = jnp.dot(whole, jnp.concatenate([side_ref[b] for b in mine], axis=0), preferred_element_type=F32)
        total = term if total is None else total + term
    for i, m in enumerate(here):
        grad_ref[jnp.bitwise_xor(col_ref[0], m)] = total[i * feat : (i + 1) * feat]


def dense_early(weight, shards, side, mask, col, late):
    blocks, feat, size = shards[0].shape
    cols = len(shards)
    args = [weight, *(v for m, v in enumerate(shards) if m != late), side, mask]
    return pl.pallas_call(
        functools.partial(dense_early_kernel, cols, late),
        out_shape=[
            jax.ShapeDtypeStruct((GROUPS, feat, blocks // GROUPS * size), F32),
            jax.ShapeDtypeStruct((cols, feat, side.shape[2]), F32),
            jax.ShapeDtypeStruct(mask.shape, BF16),
        ],
        in_specs=[SMEM] + [VMEM] * len(args),
        out_specs=[VMEM] * 3,
        compiler_params=params(16),
        name="dense_early",
    )(col, *args)


def dense_late_kernel(late, weight_ref, shard_ref, part_ref, side_ref, mask_ref, *rest):
    outs, grad_ref = rest[:GROUPS], rest[GROUPS]
    blocks, feat, size = shard_ref.shape
    per = blocks // GROUPS
    weight = weight_ref[:, late * feat : (late + 1) * feat]
    total = None
    for i, out in enumerate(outs):
        mine = range(i * per, (i + 1) * per)
        whole = jnp.concatenate([shard_ref[b] for b in mine], axis=1)
        res = part_ref[i] + jnp.dot(weight, whole, preferred_element_type=F32)
        for k, b in enumerate(mine):
            out[k] = (res[:, k * size : (k + 1) * size] * mask_ref[b].astype(F32)).astype(BF16)
        term = jnp.dot(whole, jnp.concatenate([side_ref[b] for b in mine], axis=0), preferred_element_type=F32)
        total = term if total is None else total + term
    grad_ref[...] = total


def dense_late(weight, shard, part, side, mask, late):
    blocks, feat, size = shard.shape
    return pl.pallas_call(
        functools.partial(dense_late_kernel, late),
        out_shape=[jax.ShapeDtypeStruct((blocks // GROUPS, feat, size), BF16)] * GROUPS
        + [jax.ShapeDtypeStruct((feat, side.shape[2]), F32)],
        in_specs=[VMEM] * 5,
        out_specs=[VMEM] * (GROUPS + 1),
        compiler_params=params(16),
        name="dense_late",
    )(weight, shard, part, side, mask)


def weight_terms_kernel(late, me_ref, col_ref, second_ref, late_ref, *refs):
    firsts, (keep_ref, send_ref, held) = refs[:-3], refs[-3:]
    cols = second_ref.shape[0]
    even = jnp.bitwise_and(me_ref[0], 1) == 0
    held[...] = second_ref[...]
    held[jnp.bitwise_xor(col_ref[0], late)] = late_ref[...]
    first = jnp.concatenate([sum(r[q] for r in firsts) for q in range(cols)], axis=0).T
    second = jnp.concatenate([held[q] for q in range(cols)], axis=0).T
    keep_ref[...] = jnp.where(even, second, first)
    send_ref[...] = jnp.where(even, first, second).astype(BF16)


def weight_terms(firsts, second, last, me, col, late):
    cols, feat, width = second.shape
    shape = (width, cols * feat)
    return pl.pallas_call(
        functools.partial(weight_terms_kernel, late),
        out_shape=[jax.ShapeDtypeStruct(shape, F32), jax.ShapeDtypeStruct(shape, BF16)],
        in_specs=[SMEM, SMEM] + [VMEM] * (2 + len(firsts)),
        out_specs=[VMEM] * 2,
        scratch_shapes=[pltpu.VMEM(second.shape, F32)],
        compiler_params=params(8),
        name="weight_terms",
    )(me, col, second, last, *firsts)


def swap(value, mask, axis):
    return lax.ppermute(value, axis, [(i, i ^ mask) for i in range(lax.axis_size(axis))])


def add(a, b):
    return (a.astype(F32) + b.astype(F32)).astype(BF16)


def scatter(pieces, rows, value=None):
    chips = [1 << b for b in range(1, rows.bit_length() - 1)]
    shape = (2,) * len(chips) + pieces[0].shape[1:]
    keeps = [pieces[2 * g].reshape(shape) for g in range(GROUPS)]
    gots = [swap(pieces[2 * g + 1], 1, "row").reshape(shape) for g in range(GROUPS)]
    orders = [chips if g % 2 else chips[::-1] for g in range(GROUPS)]
    lefts = [chips[::-1] for _ in range(GROUPS)]
    for level in range(len(chips)):
        masks = [order[level] for order in orders]
        sent = []
        for g in range(GROUPS):
            axis = lefts[g].index(masks[g])
            lefts[g] = [m for m in lefts[g] if m != masks[g]]
            half = lambda v, i: lax.index_in_dim(v, i, axis, keepdims=False)
            sent.append(add(half(keeps[g], 1), half(gots[g], 1)))
            keeps[g] = add(half(keeps[g], 0), half(gots[g], 0))
        if value is not None:
            keeps, value = lax.optimization_barrier((keeps, value))
        gots = [swap(sent[g], masks[g], "row") for g in range(GROUPS)]
        if value is not None:
            value = value.astype(BF16)
            value = value.astype(F32) + swap(value, chips[-1 - level], "row").astype(F32)
            if level < len(chips) - 1:
                gots, value = lax.optimization_barrier((gots, value))
    return [t for pair in zip(keeps, gots) for t in pair], value


def gather_columns(own, cols, beside=(), tied=True):
    if cols == 4:
        near, far = swap(own, 1, "col"), swap(own, 3, "col")
        if tied:
            far, near, beside = lax.optimization_barrier((far, near, beside))
        else:
            near, beside = lax.optimization_barrier((near, beside))
        return [own, near, swap(far, 1, "col"), far], beside
    return [own] + [swap(own, m, "col") for m in range(1, cols)], beside


def per_device(
    node_feats, hidden_act, grad_out, relu_mask, edge_tiles, block_cols, weight_one, weight_two
):
    rows, cols = lax.axis_size("row"), lax.axis_size("col")
    me, col = lax.axis_index("row").astype(jnp.int32), lax.axis_index("col").astype(jnp.int32)
    me_at, col_at = me.reshape(1), col.reshape(1)
    size = edge_tiles.shape[2]
    per = edge_tiles.shape[0] // GROUPS
    cut = lambda v, g: v[g * per : (g + 1) * per]
    blocked = lambda v: v.reshape(v.shape[0] // size, size, v.shape[1])
    after = lax.optimization_barrier

    def by_distance(weight):
        split = weight.reshape(weight.shape[0], cols, weight.shape[1] // cols)
        order = [lax.dynamic_index_in_dim(split, col ^ m, 1, keepdims=False) for m in range(cols)]
        return jnp.concatenate(order, axis=1)

    block_cols = block_cols.reshape(-1)
    *pieces, mask = spread(edge_tiles, block_cols, [blocked(grad_out)], me_at, rows, blocked(relu_mask))
    terms, _ = scatter(pieces, rows)
    own, node_feats = after((finish(terms)[0], blocked(node_feats)))
    own, weight_one, weight_two = after((own, weight_one, weight_two))
    weight_one, weight_two = by_distance(weight_one), by_distance(weight_two)
    parts = [node_feats] + [swap(node_feats, rel, "row") for rel in range(2, rows, 2)]
    shards, parts[0] = gather_columns(own, cols, node_feats, False)
    parts = [v for part in parts for v in (part, swap(part, 1, "row"))]
    late = 2
    hidden = blocked(hidden_act)
    part, second, mask = dense_early(weight_two, shards, hidden, mask, col_at, late)
    arrived, parts = after((shards[late], parts))
    *deltas, last = dense_late(weight_two, arrived, part, hidden, mask, late)
    deltas[0], parts = after((deltas[0], parts))
    agg_feats = aggregate(edge_tiles, block_cols, parts, me_at)
    inputs, firsts = [], []
    shards = []
    for g in range(GROUPS):
        arrived, beside = gather_columns(deltas[g], cols, agg_feats if g == 0 else (), g == 0)
        agg_feats = beside if g == 0 else agg_feats
        shards.append(arrived)
    shards[0][2], shards[1][1] = after((shards[0][2], shards[1][1]))
    for g in range(GROUPS):
        out, grad = dense(weight_one, shards[g], cut(agg_feats, g), None, col_at, 1)
        inputs.append(out)
        firsts.append(grad)
    pieces = spread(edge_tiles, block_cols, inputs, me_at, rows)
    keep, send = weight_terms(firsts, second, last, me_at, col_at, late)
    terms, value = scatter(pieces, rows, keep + swap(send, 1, "row").astype(F32))
    grads = [me_at, value, swap(value, 1, "row")]
    out, first_grad, second_grad = finish(terms, grads)
    return out.reshape(-1, out.shape[2]), first_grad, second_grad


def solution(mesh):
    in_specs = (
        P("row", "col"),
        P("row", "col"),
        P("row", "col"),
        P("row", "col"),
        P("row", None, None, None),
        P("row", None),
        P("col", None),
        P("col", None),
    )
    out_specs = (P("row", "col"), P("col", None), P("col", None))
    return jax.shard_map(
        per_device, mesh=mesh, in_specs=in_specs, out_specs=out_specs, check_vma=False
    )
```
